32 devices in a mesh: dp: 8 (over z, x), chan: 4 (over y, core).
Axes of the slice: x: 2, y: 2, z: 4, core: 2. Of those that a mesh axis runs over, the one named last changes fastest.
Arguments:
- inputs: bfloat16 [4, 8, 512, 1024], P(None, 'dp', 'chan'), may hold values from -6 to 6
- cotangent: bfloat16 [4, 8, 512, 1024], P(None, 'dp', 'chan'), may hold values from -6 to 6
- lengths: int32 [4, 8], P(None, 'dp'), may hold values from 1 to 512, as said below
- tile_slot: int32 [23], replicated, may hold values from 0 to 23, as said below
- master: float32 [24, 1024, 1024], P('dp', 'chan')
- tile_first: float32 [24, 1024, 1024], P('dp', 'chan')
- tile_second: float32 [24, 1024, 1024], P('dp', 'chan'), as said below
- norm_params: float32 [10, 1024], replicated
- norm_first: float32 [10, 1024], replicated
- norm_second: float32 [10, 1024], replicated, as said below
- conv_params: float32 [7, 1024], P(None, 'chan')
- conv_first: float32 [7, 1024], P(None, 'chan')
- conv_second: float32 [7, 1024], P(None, 'chan'), as said below
Outputs:
- outputs: bfloat16 [4, 8, 512, 1024], P(None, 'dp', 'chan')
- input_grad: float32 [4, 8, 512, 1024], P(None, 'dp', 'chan')
- tile_first_new: float32 [24, 1024, 1024], P('dp', 'chan')
- tile_second_new: float32 [24, 1024, 1024], P('dp', 'chan')
- tile_master_new: float32 [24, 1024, 1024], P('dp', 'chan')
- tile_bf16_new: bfloat16 [24, 1024, 1024], P('dp', 'chan')
- norm_first_new: float32 [10, 1024], replicated
- norm_second_new: float32 [10, 1024], replicated
- norm_params_new: float32 [10, 1024], replicated
- conv_first_new: float32 [7, 1024], P(None, 'chan')
- conv_second_new: float32 [7, 1024], P(None, 'chan')
- conv_params_new: float32 [7, 1024], P(None, 'chan')
The draws below stay inside these ranges and needn't reach their ends.
Inputs may be any that keep to these rules, and one draw needn't show every extreme that they name: `lengths`: in every micro-batch one clip has exactly 512 frames. The entries are distinct: tile k lives at position tile_slot[k] % 3 of dp index tile_slot[k] // 3; some dp index holds exactly 3 tiles. `tile_second`: Positive. `norm_second`: Positive. `conv_second`: Positive.
All inputs are finite; a program needn't handle non-finite values.
Results may differ from the reference program's by a relative error of at most 0.03.
Values may be sent and summed in bfloat16 or wider, within the bound.
No kernel may reach another device: no remote copies, remote signals or barrier semaphores. Data moves between devices by JAX's collectives and lax.ppermute only.
A program may use at most 384 MiB of HBM per device.

```python
import jax
import jax.numpy as jnp
from jax import lax

D = 1024
FF = 4096
HEADS = 8
HEAD_DIM = 128
KERNEL = 5
LEN = 512
MICRO = 4
STEP = 10
RW = 256
FQ = 4
NB = 23
SLOTS = 3
N_DP = 8
N_CHAN = 4


def slot_table(key):
    key = jax.random.fold_in(key, 11)
    first_key, second_key, third_key = jax.random.split(key, 3)
    slot_total = N_DP * SLOTS
    full_owner = jax.random.randint(first_key, (), 0, N_DP)
    slot_index = jnp.arange(slot_total, dtype=jnp.int32)
    ranking = jax.random.permutation(second_key, slot_total).astype(jnp.int32) + SLOTS
    ranking = jnp.where(slot_index // SLOTS == full_owner, slot_index % SLOTS, ranking)
    ordered = jnp.argsort(ranking).astype(jnp.int32)
    chosen = ordered[:NB]
    tile_order = jax.random.permutation(third_key, NB)
    return jnp.zeros((NB,), jnp.int32).at[tile_order].set(chosen).astype(jnp.int32)


def tiles_by_slot(key):
    table = slot_table(key)
    return jnp.full((N_DP * SLOTS,), -1, jnp.int32).at[table].set(jnp.arange(NB, dtype=jnp.int32))


def grad_size_tiles(key):
    tile_of_slot = tiles_by_slot(key)
    frames = float(N_DP * MICRO * LEN)
    factor = jnp.full((N_DP * SLOTS,), 0.2, jnp.float32)
    factor = jnp.where(tile_of_slot == 4 * FQ, 0.6, factor)
    factor = jnp.where(tile_of_slot == 4 * FQ + 1, 0.45, factor)
    factor = jnp.where(tile_of_slot == 4 * FQ + 2, 0.6, factor)
    factor = jnp.where(tile_of_slot == 4 * FQ + 3, 1.64 * LEN ** (-0.5), factor)
    factor = jnp.where(tile_of_slot == 4 * FQ + 4, 0.3, factor)
    factor = jnp.where(tile_of_slot == 4 * FQ + 5, 0.15, factor)
    factor = jnp.where(tile_of_slot == 4 * FQ + 6, 0.4, factor)
    return factor * frames ** 0.5


def grad_size_norms():
    frames = float(N_DP * MICRO * LEN)
    row_factor = jnp.array([0.4, 0.8, 0.3, 0.4, 1.0, 0.4, 0.8, 0.3, 0.4, 1.0], jnp.float32)
    return row_factor * frames ** 0.5


def grad_size_convs():
    frames = float(N_DP * MICRO * LEN)
    row_index = jnp.arange(KERNEL + 2)
    row_factor = jnp.where(row_index == KERNEL + 1, 0.4, 0.3).astype(jnp.float32)
    return row_factor * frames ** 0.5


def signed_noise(key, shape):
    return jax.random.normal(key, shape, jnp.float32)


def spread_factor(key, shape):
    return jnp.exp(jax.random.uniform(key, shape, jnp.float32, -0.693, 0.693))


def draw_tile_slot(key, part):
    return slot_table(key)


def draw_lengths(key, part):
    key = jax.random.fold_in(key, 5)
    first_key, second_key = jax.random.split(key, 2)
    groups = jnp.arange(N_DP, dtype=jnp.int32)
    ramp = LEN * (N_DP + 2 * groups) // (3 * N_DP)
    factor = jax.random.randint(first_key, (MICRO, N_DP), 60, 101)
    base_len = jnp.maximum(ramp[None, :] * factor // 100, LEN // 8)
    longest = jax.random.randint(second_key, (MICRO,), 3 * N_DP // 4, N_DP)
    return jnp.where(groups[None, :] == longest[:, None], LEN, base_len).astype(jnp.int32)


def draw_master(key, part):
    tile_of_slot = tiles_by_slot(key)
    key = jax.random.fold_in(key, 3)
    slot_total = N_DP * SLOTS
    scale = jnp.full((slot_total,), D ** (-0.5), jnp.float32)
    out_scale = 2.0 * FF ** (-0.5)
    scale = jnp.where((tile_of_slot >= FQ) & (tile_of_slot < 2 * FQ), out_scale, scale)
    scale = jnp.where((tile_of_slot >= 3 * FQ) & (tile_of_slot < 4 * FQ), out_scale, scale)
    scale = jnp.where((tile_of_slot == 4 * FQ) | (tile_of_slot == 4 * FQ + 1), (1.5 / D) ** 0.5, scale)
    scale = jnp.where(tile_of_slot == 4 * FQ + 3, (LEN / (16.0 * D)) ** 0.5, scale)
    noise = signed_noise(key, (slot_total, D, D))
    return (noise * scale[:, None, None]).astype(jnp.float32)


def draw_tile_first(key, part):
    size = grad_size_tiles(key)
    key = jax.random.fold_in(key, 13)
    noise = signed_noise(key, (N_DP * SLOTS, D, D))
    return (noise * 0.11 * size[:, None, None]).astype(jnp.float32)


def draw_tile_second(key, part):
    size = grad_size_tiles(key)
    key = jax.random.fold_in(key, 17)
    factor = spread_factor(key, (N_DP * SLOTS, D, D))
    return (factor * 0.041 * (size * size)[:, None, None]).astype(jnp.float32)


def draw_norm_params(key, part):
    key = jax.random.fold_in(key, 7)
    noise = signed_noise(key, (10, D))
    row_index = jnp.arange(10)[:, None]
    return jnp.where(row_index < 5, 1.0 + 0.15 * noise, 0.3 * noise).astype(jnp.float32)


def draw_norm_first(key, part):
    key = jax.random.fold_in(key, 19)
    noise = signed_noise(key, (10, D))
    return (noise * 0.11 * grad_size_norms()[:, None]).astype(jnp.float32)


def draw_norm_second(key, part):
    key = jax.random.fold_in(key, 23)
    size = grad_size_norms()
    factor = spread_factor(key, (10, D))
    return (factor * 0.041 * (size * size)[:, None]).astype(jnp.float32)


def draw_conv_params(key, part):
    key = jax.random.fold_in(key, 9)
    noise = signed_noise(key, (KERNEL + 2, D))
    row_index = jnp.arange(KERNEL + 2)[:, None]
    values_out = jnp.where(row_index < KERNEL, 0.45 * noise, 0.3 * noise)
    values_out = jnp.where(row_index == KERNEL, 1.0 + 0.15 * noise, values_out)
    return values_out.astype(jnp.float32)


def draw_conv_first(key, part):
    key = jax.random.fold_in(key, 29)
    noise = signed_noise(key, (KERNEL + 2, D))
    return (noise * 0.11 * grad_size_convs()[:, None]).astype(jnp.float32)


def draw_conv_second(key, part):
    key = jax.random.fold_in(key, 31)
    size = grad_size_convs()
    factor = spread_factor(key, (KERNEL + 2, D))
    return (factor * 0.041 * (size * size)[:, None]).astype(jnp.float32)


def levels(own_key, shape, pieces, least, high):
    factor_of, own = 1.0, jax.random.fold_in(own_key, 6)
    for axis_at, shards_of in pieces:
        draws = jnp.exp(jax.random.uniform(jax.random.fold_in(own, axis_at), (shards_of,), jnp.float32, least / len(pieces), high / len(pieces)))
        factor_of = factor_of * jnp.repeat(draws, shape[axis_at] // shards_of).reshape([-1 if axis == axis_at else 1 for axis in range(len(shape))])
    return factor_of


def normal_values(stream_key, extent, scale, most, cuts=(), kind=jnp.bfloat16):
    values = jax.random.normal(stream_key, extent, jnp.float32) * scale
    if len(cuts) > 0:
        values = levels(stream_key, extent, cuts, -0.22, 0.18) * values
    return jnp.clip(values, min=-most, max=most).astype(kind)


def setup_inputs(seed: int = 0) -> dict:
    arg_keys = jax.random.split(jax.random.key(seed), 14)
    inputs = normal_values(arg_keys[0], (MICRO, N_DP, LEN, D), 1.0, 6.0, ((1, 8), (2, 4)))
    cotangent = normal_values(arg_keys[1], (MICRO, N_DP, LEN, D), 1.0, 6.0, ((1, 8), (2, 4)))
    lengths = draw_lengths(jax.random.fold_in(arg_keys[13], 71), 0)
    tile_slot = draw_tile_slot(jax.random.fold_in(arg_keys[13], 71), 0)
    master = draw_master(jax.random.fold_in(arg_keys[13], 71), 0)
    tile_first = draw_tile_first(jax.random.fold_in(arg_keys[13], 71), 0)
    tile_second = draw_tile_second(jax.random.fold_in(arg_keys[13], 71), 0)
    norm_params = draw_norm_params(jax.random.fold_in(arg_keys[13], 71), 0)
    norm_first = draw_norm_first(jax.random.fold_in(arg_keys[13], 71), 0)
    norm_second = draw_norm_second(jax.random.fold_in(arg_keys[13], 71), 0)
    conv_params = draw_conv_params(jax.random.fold_in(arg_keys[13], 71), 0)
    conv_first = draw_conv_first(jax.random.fold_in(arg_keys[13], 71), 0)
    conv_second = draw_conv_second(jax.random.fold_in(arg_keys[13], 71), 0)
    return {"inputs": inputs, "cotangent": cotangent, "lengths": lengths, "tile_slot": tile_slot, "master": master, "tile_first": tile_first, "tile_second": tile_second, "norm_params": norm_params, "norm_first": norm_first, "norm_second": norm_second, "conv_params": conv_params, "conv_first": conv_first, "conv_second": conv_second}


@jax.custom_vjp
def low(v):
    return lax.optimization_barrier(v.astype(jnp.bfloat16)).astype(jnp.float32)

@jax.custom_vjp
def low_back(v):
    return v

def low_keep(v):
    return (low(v), None)

def low_pass(kept, grad):
    return (grad,)

def back_keep(v):
    return (v, None)

def back_low(kept, grad):
    return (low(grad),)
low.defvjp(low_keep, low_pass)
low_back.defvjp(back_keep, back_low)
norm_eps = 1e-05
masked_score = -1e+30
beta_one = 0.9
beta_two = 0.98
adam_eps = 1e-08
tile_rate = 0.06
small_rate = 0.6
weight_decay = 0.01

def matmul_hi(left, right):
    return jnp.dot(left, right, precision=lax.Precision.HIGHEST, preferred_element_type=jnp.float32)

def layer_norm(stream, norm_gain, norm_bias):
    center = stream - lax.optimization_barrier(jnp.mean(stream, axis=-1, keepdims=True))
    spread = lax.optimization_barrier(jnp.mean(center * center, axis=-1, keepdims=True))
    return center * lax.rsqrt(spread + norm_eps) * norm_gain + norm_bias

def silu_act(value_in):
    return value_in * jax.nn.sigmoid(value_in)

def hidden_rows(block):
    return block.reshape(FQ, N_CHAN, RW, D).transpose(1, 0, 2, 3).reshape(FF, D)

def feed_forward(stream, norm_gain, norm_bias, w_in, w_out):
    normed = low(layer_norm(stream, norm_gain, norm_bias))
    hidden = low_back(matmul_hi(normed, w_in.T))
    active = low(silu_act(hidden))
    return stream + 0.5 * low_back(matmul_hi(active, w_out))

def attend_clip(operands):
    queries, keys_all, values_all, key_mask = operands
    scores = jnp.einsum('qhd,khd->hqk', queries, keys_all, precision=lax.Precision.HIGHEST)
    scores = low_back(scores * HEAD_DIM ** (-0.5))
    scores = jnp.where(key_mask[None, None, :] > 0, scores, masked_score)
    attn_probs = low(jax.nn.softmax(scores, axis=-1))
    return jnp.einsum('hqk,khd->qhd', attn_probs, values_all, precision=lax.Precision.HIGHEST)

def attention(stream, norm_gain, norm_bias, w_query, w_key, w_value, w_output, key_mask):
    normed = low(layer_norm(stream, norm_gain, norm_bias))
    heads_shape = (stream.shape[0], LEN, HEADS, HEAD_DIM)
    queries = low(low_back(matmul_hi(normed, w_query.T))).reshape(heads_shape)
    keys_all = low(low_back(matmul_hi(normed, w_key.T))).reshape(heads_shape)
    values_all = low(low_back(matmul_hi(normed, w_value.T))).reshape(heads_shape)
    per_head = lax.map(jax.checkpoint(attend_clip), (queries, keys_all, values_all, key_mask))
    merged = low(low_back(per_head.reshape(stream.shape)))
    return stream + low_back(matmul_hi(merged, w_output))

def convolve(stream, norm_gain, norm_bias, p_value, p_gate, p_output, conv_params, key_mask):
    normed = low(layer_norm(stream, norm_gain, norm_bias))
    linear = low_back(matmul_hi(normed, p_value.T))
    gating = low_back(matmul_hi(normed, p_gate.T))
    frame_mask = key_mask[..., None]
    gated_glu = linear * jax.nn.sigmoid(gating) * frame_mask
    margin = (KERNEL - 1) // 2
    padded = jnp.pad(gated_glu, ((0, 0), (margin, margin), (0, 0)))
    mixed_conv = jnp.zeros_like(gated_glu)
    for offset in range(KERNEL):
        mixed_conv = mixed_conv + conv_params[offset] * padded[:, offset:offset + LEN]
    frame_count = jnp.sum(key_mask)
    center = mixed_conv - lax.optimization_barrier(jnp.sum(mixed_conv * frame_mask, axis=(0, 1))) / frame_count
    spread = lax.optimization_barrier(jnp.sum(frame_mask * center * center, axis=(0, 1))) / frame_count
    normal = center * lax.rsqrt(spread + norm_eps) * conv_params[KERNEL] + conv_params[KERNEL + 1]
    active = low(silu_act(normal))
    return stream + low_back(matmul_hi(active, p_output))

def layer(source, key_mask, tile_mats, norms, conv_params):
    in_first = hidden_rows(tile_mats[0:FQ])
    out_first = hidden_rows(tile_mats[FQ:2 * FQ])
    in_second = hidden_rows(tile_mats[2 * FQ:3 * FQ])
    out_second = hidden_rows(tile_mats[3 * FQ:4 * FQ])
    base_tile = 4 * FQ
    stream_one = feed_forward(source, norms[0], norms[5], in_first, out_first)
    stream_two = attention(stream_one, norms[1], norms[6], tile_mats[base_tile], tile_mats[base_tile + 1], tile_mats[base_tile + 2], tile_mats[base_tile + 3], key_mask)
    stream_three = convolve(stream_two, norms[2], norms[7], tile_mats[base_tile + 4], tile_mats[base_tile + 5], tile_mats[base_tile + 6], conv_params, key_mask)
    stream_four = feed_forward(stream_three, norms[3], norms[8], in_second, out_second)
    return layer_norm(stream_four, norms[4], norms[9])

def adamw_step(weight, gradient, first_old, second_old, rate, decay):
    first_new = beta_one * first_old + (1.0 - beta_one) * gradient
    second_new = beta_two * second_old + (1.0 - beta_two) * gradient * gradient
    first_hat = first_new / (1.0 - beta_one ** STEP)
    second_hat = second_new / (1.0 - beta_two ** STEP)
    weight_new = weight - rate * (first_hat / (jnp.sqrt(second_hat) + adam_eps) + decay * weight)
    return (first_new, second_new, weight_new)

def reference(inputs, cotangent, lengths, tile_slot, master, tile_first, tile_second, norm_params, norm_first, norm_second, conv_params, conv_first, conv_second):
    tile_mats = master.astype(jnp.bfloat16).astype(jnp.float32)[tile_slot]
    positions = jnp.arange(LEN, dtype=jnp.int32)
    outputs = []
    in_grads = []
    tile_grad = jnp.zeros(tile_mats.shape, jnp.float32)
    norm_grad = jnp.zeros(norm_params.shape, jnp.float32)
    conv_grad = jnp.zeros(conv_params.shape, jnp.float32)
    for micro_index in range(MICRO):
        key_mask = (positions[None, :] < lengths[micro_index][:, None]).astype(jnp.float32)

        def forward(source, mats, norms, convs):
            return layer(source, key_mask, mats, norms, convs)
        result, pullback = jax.vjp(forward, inputs[micro_index].astype(jnp.float32), tile_mats, norm_params, conv_params)
        source_grad, mats_grad, norms_grad, convs_grad = pullback(cotangent[micro_index].astype(jnp.float32))
        outputs.append(result.astype(jnp.bfloat16))
        in_grads.append(source_grad)
        tile_grad = tile_grad + mats_grad
        norm_grad = norm_grad + norms_grad
        conv_grad = conv_grad + convs_grad
    slot_grad = jnp.zeros(master.shape, jnp.float32).at[tile_slot].set(tile_grad)
    tile_m, tile_v, tile_w = adamw_step(master, slot_grad, tile_first, tile_second, tile_rate, weight_decay)
    norm_m, norm_v, norm_w = adamw_step(norm_params, norm_grad, norm_first, norm_second, small_rate, 0.0)
    conv_m, conv_v, conv_w = adamw_step(conv_params, conv_grad, conv_first, conv_second, small_rate, 0.0)
    return (jnp.stack(outputs), jnp.stack(in_grads), tile_m, tile_v, tile_w, tile_w.astype(jnp.bfloat16), norm_m, norm_v, norm_w, conv_m, conv_v, conv_w)
```

```python
import jax
import jax.numpy as jnp
from jax import lax
from jax.experimental import pallas as pl
from jax.experimental.pallas import tpu as pltpu
from jax.sharding import PartitionSpec as P

HEAD_DIM = 128
STEP = 10

norm_eps = 1e-05
masked_score = -1e30
beta_one = 0.9
beta_two = 0.98
adam_eps = 1e-08
tile_rate = 0.06
small_rate = 0.6
weight_decay = 0.01

BOTH = ("dp", "chan")
bf16 = jnp.bfloat16
f32 = jnp.float32


def dot_rows(left, right):
    return lax.dot_general(left, right, (((1,), (1,)), ((), ())), preferred_element_type=f32)


def dot_plain(left, right):
    return jnp.dot(left, right, preferred_element_type=f32)


def dot_cols(left, right):
    return lax.dot_general(left, right, (((0,), (0,)), ((), ())), preferred_element_type=f32)


def adamw_step(weight, gradient, first_old, second_old, rate, decay):
    first_new = beta_one * first_old + (1.0 - beta_one) * gradient
    second_new = beta_two * second_old + (1.0 - beta_two) * gradient * gradient
    first_hat = first_new / (1.0 - beta_one**STEP)
    second_hat = second_new / (1.0 - beta_two**STEP)
    weight_new = weight - rate * (first_hat / (jnp.sqrt(second_hat) + adam_eps) + decay * weight)
    return (first_new, second_new, weight_new)


def exchange(value, axis, mask):
    size = lax.axis_size(axis)
    return lax.ppermute(value, axis, [(i, i ^ mask) for i in range(size)])


def swap_blocks(value, axis):
    size = lax.axis_size(axis)
    me = lax.axis_index(axis)
    result = value
    for mask in range(1, size):
        sent = lax.dynamic_index_in_dim(value, me ^ mask, 0, keepdims=True)
        result = lax.dynamic_update_slice_in_dim(result, exchange(sent, axis, mask), me ^ mask, 0)
    return result


def gather_small(value, axis):
    size = lax.axis_size(axis)
    me = lax.axis_index(axis)
    result = jnp.zeros((size,) + value.shape, value.dtype)
    result = lax.dynamic_update_slice_in_dim(result, value[None], me, 0)
    for mask in range(1, size):
        result = lax.dynamic_update_slice_in_dim(
            result, exchange(value[None], axis, mask), me ^ mask, 0
        )
    return result


def butterfly_sum(value, axis):
    size = lax.axis_size(axis)
    mask = 1
    while mask < size:
        value = value + exchange(value, axis, mask)
        mask *= 2
    return value


def gather_tiles(own, tile_slot):
    slots, rows, width = own.shape
    chan_count = lax.axis_size("chan")
    everything = lax.all_gather(own, BOTH, axis=0, tiled=True)
    owner, place = tile_slot // slots, tile_slot % slots
    block = (owner[:, None] * chan_count + jnp.arange(chan_count)[None, :]) * slots + place[:, None]
    tiles = everything.at[block.reshape(-1)].get(mode="promise_in_bounds")
    return tiles.reshape(tile_slot.shape[0], chan_count * rows, width)


def reduce_tiles(grads, tile_slot, slots):
    tiles, full, width = grads.shape
    chan_count, dp_count = lax.axis_size("chan"), lax.axis_size("dp")
    rows = full // chan_count
    slot = jnp.arange(dp_count * slots, dtype=jnp.int32)
    hit = slot[:, None] == tile_slot[None, :]
    tile_of = jnp.argmax(hit, axis=1).astype(jnp.int32).reshape(dp_count, 1, slots)
    filled = jnp.any(hit, axis=1)
    block = (tile_of * chan_count + jnp.arange(chan_count)[None, :, None]).reshape(-1)
    placed = grads.reshape(tiles * chan_count, rows, width).at[block].get(mode="promise_in_bounds")
    placed = placed.reshape(dp_count * chan_count * slots, rows, width)
    total = lax.psum_scatter(placed, BOTH, scatter_dimension=0, tiled=True).astype(f32)
    mine = lax.dynamic_slice_in_dim(filled, lax.axis_index("dp") * slots, slots)
    return jnp.where(mine[:, None, None], total, 0.0)


def norm_stats(stream):
    mean = jnp.mean(stream, axis=-1, keepdims=True)
    center = stream - mean
    spread = jnp.mean(center * center, axis=-1, keepdims=True)
    return (mean, lax.rsqrt(spread + norm_eps))


def norm_apply(stream, stats, gain, bias):
    mean, inv = stats
    return (stream - mean) * inv * gain + bias


def norm_backward(stream, stats, gain, upstream):
    mean, inv = stats
    hat = (stream - mean) * inv
    scaled = upstream * gain
    back = (
        scaled
        - jnp.mean(scaled, axis=-1, keepdims=True)
        - hat * jnp.mean(scaled * hat, axis=-1, keepdims=True)
    ) * inv
    return (back, jnp.sum(upstream * hat, axis=0), jnp.sum(upstream, axis=0))


def masked_probs(query, key, valid):
    scores = dot_rows(query, key) * HEAD_DIM ** (-0.5)
    column = lax.broadcasted_iota(jnp.int32, scores.shape, 1)
    scores = jnp.where(column < valid, scores, masked_score)
    exponent = jnp.exp(scores - jnp.max(scores, axis=-1, keepdims=True))
    return exponent / jnp.sum(exponent, axis=-1, keepdims=True)


def attend_kernel(valid_ref, q_ref, k_ref, v_ref, out_ref):
    probs = masked_probs(q_ref[...], k_ref[...], valid_ref[0]).astype(bf16)
    out_ref[...] = dot_plain(probs, v_ref[...]).astype(bf16)


def attend_back_kernel(valid_ref, q_ref, k_ref, v_ref, g_ref, dq_ref, dk_ref, dv_ref):
    query, key, grad = q_ref[...], k_ref[...], g_ref[...]
    probs = masked_probs(query, key, valid_ref[0])
    grad_probs = dot_rows(grad, v_ref[...])
    row_dot = jnp.sum(probs * grad_probs, axis=-1, keepdims=True)
    grad_scores = (probs * (grad_probs - row_dot)).astype(bf16)
    scale = HEAD_DIM ** (-0.5)
    dq_ref[...] = (dot_plain(grad_scores, key) * scale).astype(bf16)
    dk_ref[...] = (dot_cols(grad_scores, query) * scale).astype(bf16)
    dv_ref[...] = dot_cols(probs.astype(bf16), grad).astype(bf16)


def head_call(kernel, valid, operands, out_count, flops):
    rows, width = operands[0].shape
    spec = pl.BlockSpec((rows, HEAD_DIM), lambda h: (0, h))
    shape = jax.ShapeDtypeStruct((rows, width), bf16)
    return pl.pallas_call(
        kernel,
        grid=(width // HEAD_DIM,),
        in_specs=[pl.BlockSpec(memory_space=pltpu.SMEM)] + [spec] * len(operands),
        out_specs=[spec] * out_count,
        out_shape=[shape] * out_count,
        cost_estimate=pl.CostEstimate(
            flops=flops * rows * rows * width,
            bytes_accessed=2 * rows * width * (len(operands) + out_count),
            transcendentals=rows * rows * width // HEAD_DIM,
        ),
        compiler_params=pltpu.CompilerParams(vmem_limit_bytes=48 * 1024 * 1024),
    )(valid, *operands)


def ffn_forward(stream, gain, bias, w_in, w_out):
    stats = norm_stats(stream)
    normed = norm_apply(stream, stats, gain, bias).astype(bf16)
    hidden = dot_rows(normed, w_in)
    sig = jax.nn.sigmoid(hidden)
    active = (hidden * sig).astype(bf16)
    slope = (sig * (1.0 + hidden * (1.0 - sig))).astype(bf16)
    return (stream + 0.5 * dot_plain(active, w_out), (stats, normed, active, slope))


def ffn_backward(upstream, stream, gain, kept, w_in, w_out):
    stats, normed, active, slope = kept
    incoming = (0.5 * upstream).astype(bf16)
    grad_out = dot_cols(active, incoming).astype(bf16)
    grad_hidden = (dot_rows(incoming, w_out) * slope.astype(f32)).astype(bf16)
    grad_in = dot_cols(grad_hidden, normed).astype(bf16)
    back, grad_gain, grad_bias = norm_backward(stream, stats, gain, dot_plain(grad_hidden, w_in))
    return (upstream + back, grad_in, grad_out, grad_gain, grad_bias)


def shift_rows(value, offset):
    rows = value.shape[0]
    if offset == 0:
        return value
    if offset > 0:
        return jnp.pad(value[offset:], ((0, offset), (0, 0)))
    return jnp.pad(value[: rows + offset], ((-offset, 0), (0, 0)))


def merge_stats(one, two):
    count_a, mean_a, dev_a = one
    count_b, mean_b, dev_b = two
    count = count_a + count_b
    mean = (count_a * mean_a + count_b * mean_b) / count
    gap = mean_a - mean_b
    return (count, mean, dev_a + dev_b + gap * gap * (count_a * count_b / count))


def shards(
    inputs,
    cotangent,
    lengths,
    tile_slot,
    master,
    tile_first,
    tile_second,
    norm_params,
    norm_first,
    norm_second,
    conv_params,
    conv_first,
    conv_second,
):
    micro, _, seg_rows, width = inputs.shape
    slots, rows_tile, _ = master.shape
    chan_count, dp_count = lax.axis_size("chan"), lax.axis_size("dp")
    chan_index = lax.axis_index("chan")
    assert micro == chan_count
    rows = seg_rows * chan_count
    tile_count = tile_slot.shape[0]
    quarter = (tile_count - 7) // 4
    base = 4 * quarter

    tiles = gather_tiles(master.astype(bf16), tile_slot)
    source = swap_blocks(inputs[:, 0], "chan").reshape(rows, width).astype(f32)
    upstream = swap_blocks(cotangent[:, 0], "chan").reshape(rows, width).astype(f32)
    convs = jnp.moveaxis(gather_small(conv_params, "chan"), 0, 1).reshape(-1, width)
    valid = lax.dynamic_slice_in_dim(lengths[:, 0], chan_index, 1)

    def stack_rows(first):
        return tiles[first : first + quarter].reshape(quarter * width, width)

    in_first, out_first = stack_rows(0), stack_rows(quarter)
    in_second, out_second = stack_rows(2 * quarter), stack_rows(3 * quarter)
    w_query, w_key, w_value, w_output, p_value, p_gate, p_output = [
        tiles[base + i] for i in range(7)
    ]
    gains, biases = norm_params[:5], norm_params[5:]
    taps = convs.shape[0] - 2
    margin = (taps - 1) // 2
    bn_gain, bn_bias = convs[taps], convs[taps + 1]
    frame_mask = (jnp.arange(rows, dtype=jnp.int32) < valid[0]).astype(f32)[:, None]

    stream_one, kept_one = ffn_forward(source, gains[0], biases[0], in_first, out_first)

    stats_att = norm_stats(stream_one)
    att_in = norm_apply(stream_one, stats_att, gains[1], biases[1]).astype(bf16)
    queries = dot_rows(att_in, w_query).astype(bf16)
    keys = dot_rows(att_in, w_key).astype(bf16)
    values = dot_rows(att_in, w_value).astype(bf16)
    (merged,) = head_call(attend_kernel, valid, (queries, keys, values), 1, 4)
    stream_two = stream_one + dot_plain(merged, w_output)

    stats_conv = norm_stats(stream_two)
    conv_in = norm_apply(stream_two, stats_conv, gains[2], biases[2]).astype(bf16)
    linear = dot_rows(conv_in, p_value)
    gate_sig = jax.nn.sigmoid(dot_rows(conv_in, p_gate))
    glu = linear * gate_sig * frame_mask
    depth = jnp.zeros_like(glu)
    for t in range(taps):
        depth = depth + convs[t] * shift_rows(glu, t - margin)
    count = valid[0].astype(f32)
    local_mean = jnp.sum(depth * frame_mask, axis=0) / count
    local_gap = (depth - local_mean) * frame_mask
    local_dev = jnp.sum(local_gap * local_gap, axis=0)
    stats = (jnp.full((width,), count), local_mean, local_dev)
    mask = 1
    while mask < dp_count:
        other = exchange(jnp.stack(stats), "dp", mask)
        stats = merge_stats(stats, (other[0], other[1], other[2]))
        mask *= 2
    total_count, bn_mean, bn_dev = stats
    inv_std = lax.rsqrt(bn_dev / total_count + norm_eps)
    center = depth - bn_mean
    normal = center * inv_std * bn_gain + bn_bias
    conv_sig = jax.nn.sigmoid(normal)
    conv_act = (normal * conv_sig).astype(bf16)
    stream_three = stream_two + dot_plain(conv_act, p_output)

    stream_four, kept_four = ffn_forward(stream_three, gains[3], biases[3], in_second, out_second)
    stats_last = norm_stats(stream_four)
    result = norm_apply(stream_four, stats_last, gains[4], biases[4]).astype(bf16)

    grad_four, gain_four, bias_four = norm_backward(stream_four, stats_last, gains[4], upstream)
    grad_three, gin_second, gout_second, gain_three, bias_three = ffn_backward(
        grad_four, stream_three, gains[3], kept_four, in_second, out_second
    )

    incoming = grad_three.astype(bf16)
    grad_po = dot_cols(conv_act, incoming).astype(bf16)
    conv_slope = conv_sig * (1.0 + normal * (1.0 - conv_sig))
    grad_normal = dot_rows(incoming, p_output) * conv_slope
    own_sums = jnp.stack([jnp.sum(grad_normal, axis=0), jnp.sum(grad_normal * center, axis=0)])
    sum_plain, sum_center = butterfly_sum(own_sums, "dp")
    bn_scale = bn_gain * inv_std
    grad_depth = bn_scale * grad_normal - frame_mask * bn_scale * (
        sum_plain + inv_std * inv_std * sum_center * center
    ) / total_count
    grad_glu = jnp.zeros_like(glu)
    tap_grads = []
    for t in range(taps):
        grad_glu = grad_glu + convs[t] * shift_rows(grad_depth, margin - t)
        tap_grads.append(jnp.sum(grad_depth * shift_rows(glu, t - margin), axis=0))
    grad_glu = grad_glu * frame_mask
    grad_linear = (grad_glu * gate_sig).astype(bf16)
    grad_gating = (grad_glu * linear * gate_sig * (1.0 - gate_sig)).astype(bf16)
    grad_pv = dot_cols(grad_linear, conv_in).astype(bf16)
    grad_pg = dot_cols(grad_gating, conv_in).astype(bf16)
    back, gain_two, bias_two = norm_backward(
        stream_two,
        stats_conv,
        gains[2],
        dot_plain(grad_linear, p_value) + dot_plain(grad_gating, p_gate),
    )
    grad_two = grad_three + back

    incoming = grad_two.astype(bf16)
    grad_wo = dot_cols(merged, incoming).astype(bf16)
    grad_merged = dot_rows(incoming, w_output).astype(bf16)
    grad_q, grad_k, grad_v = head_call(
        attend_back_kernel, valid, (queries, keys, values, grad_merged), 3, 10
    )
    grad_wq = dot_cols(grad_q, att_in).astype(bf16)
    grad_wk = dot_cols(grad_k, att_in).astype(bf16)
    grad_wv = dot_cols(grad_v, att_in).astype(bf16)
    back, gain_one, bias_one = norm_backward(
        stream_one,
        stats_att,
        gains[1],
        dot_plain(grad_q, w_query) + dot_plain(grad_k, w_key) + dot_plain(grad_v, w_value),
    )
    grad_one = grad_two + back

    grad_zero, gin_first, gout_first, gain_zero, bias_zero = ffn_backward(
        grad_one, source, gains[0], kept_one, in_first, out_first
    )

    grads = jnp.concatenate(
        [gin_first, gout_first, gin_second, gout_second]
        + [grad_wq, grad_wk, grad_wv, grad_wo, grad_pv, grad_pg, grad_po]
    ).reshape(tile_count, width, width)
    owned = reduce_tiles(grads, tile_slot, slots)

    small = jnp.stack(
        [gain_zero, gain_one, gain_two, gain_three, gain_four]
        + [bias_zero, bias_one, bias_two, bias_three, bias_four]
        + tap_grads
        + [own_sums[1] * inv_std, own_sums[0]]
    )
    small = butterfly_sum(butterfly_sum(small, "dp"), "chan")
    norm_total = small[: norm_params.shape[0]]
    conv_grad = lax.dynamic_slice_in_dim(
        small[norm_params.shape[0] :], chan_index * rows_tile, rows_tile, 1
    )

    tile_m, tile_v, tile_w = adamw_step(
        master, owned, tile_first, tile_second, tile_rate, weight_decay
    )
    norm_m, norm_v, norm_w = adamw_step(
        norm_params, norm_total, norm_first, norm_second, small_rate, 0.0
    )
    conv_m, conv_v, conv_w = adamw_step(
        conv_params, conv_grad, conv_first, conv_second, small_rate, 0.0
    )
    block_out = swap_blocks(result.reshape(chan_count, seg_rows, width), "chan")
    block_grad = swap_blocks(
        grad_zero.astype(bf16).reshape(chan_count, seg_rows, width), "chan"
    ).astype(f32)
    return (
        block_out[:, None],
        block_grad[:, None],
        tile_m,
        tile_v,
        tile_w,
        tile_w.astype(bf16),
        norm_m,
        norm_v,
        norm_w,
        conv_m,
        conv_v,
        conv_w,
    )


def solution(mesh):
    in_specs = (
        P(None, "dp", "chan", None),
        P(None, "dp", "chan", None),
        P(None, "dp"),
        P(),
        P("dp", "chan", None),
        P("dp", "chan", None),
        P("dp", "chan", None),
        P(),
        P(),
        P(),
        P(None, "chan"),
        P(None, "chan"),
        P(None, "chan"),
    )
    out_specs = (
        P(None, "dp", "chan", None),
        P(None, "dp", "chan", None),
        P("dp", "chan", None),
        P("dp", "chan", None),
        P("dp", "chan", None),
        P("dp", "chan", None),
        P(),
        P(),
        P(),
        P(None, "chan"),
        P(None, "chan"),
        P(None, "chan"),
    )
    return jax.shard_map(shards, mesh=mesh, in_specs=in_specs, out_specs=out_specs, check_vma=False)
```

```python
import jax
import jax.numpy as jnp
from jax import lax
from jax.experimental import pallas as pl
from jax.experimental.pallas import tpu as pltpu
from jax.sharding import PartitionSpec as P

HEAD_DIM = 128
STEP = 10

norm_eps = 1e-05
masked_score = -1e30
beta_one = 0.9
beta_two = 0.98
adam_eps = 1e-08
tile_rate = 0.06
small_rate = 0.6
weight_decay = 0.01

BOTH = ("dp", "chan")
bf16 = jnp.bfloat16
f32 = jnp.float32


def dot_rows(left, right):
    return lax.dot_general(left, right, (((1,), (1,)), ((), ())), preferred_element_type=f32)


def dot_plain(left, right):
    return jnp.dot(left, right, preferred_element_type=f32)


def dot_cols(left, right):
    return lax.dot_general(left, right, (((0,), (0,)), ((), ())), preferred_element_type=f32)


def adamw_step(weight, gradient, first_old, second_old, rate, decay):
    first_new = beta_one * first_old + (1.0 - beta_one) * gradient
    second_new = beta_two * second_old + (1.0 - beta_two) * gradient * gradient
    first_hat = first_new / (1.0 - beta_one**STEP)
    second_hat = second_new / (1.0 - beta_two**STEP)
    weight_new = weight - rate * (first_hat / (jnp.sqrt(second_hat) + adam_eps) + decay * weight)
    return (first_new, second_new, weight_new)


def exchange(value, axis, mask):
    size = lax.axis_size(axis)
    return lax.ppermute(value, axis, [(i, i ^ mask) for i in range(size)])


def swap_blocks(value, axis):
    size = lax.axis_size(axis)
    me = lax.axis_index(axis)
    result = value
    for mask in range(1, size):
        sent = lax.dynamic_index_in_dim(value, me ^ mask, 0, keepdims=True)
        result = lax.dynamic_update_slice_in_dim(result, exchange(sent, axis, mask), me ^ mask, 0)
    return result


def gather_small(value, axis):
    size = lax.axis_size(axis)
    me = lax.axis_index(axis)
    result = jnp.zeros((size,) + value.shape, value.dtype)
    result = lax.dynamic_update_slice_in_dim(result, value[None], me, 0)
    for mask in range(1, size):
        result = lax.dynamic_update_slice_in_dim(
            result, exchange(value[None], axis, mask), me ^ mask, 0
        )
    return result


def butterfly_sum(value, axis):
    size = lax.axis_size(axis)
    mask = 1
    while mask < size:
        value = value + exchange(value, axis, mask)
        mask *= 2
    return value


BITS = {"core": 1, "y": 2, "x": 4, "z1": 8, "z2": 16}
ORDERS = (
    ("z2", "y", "z1", "x"),
    ("z1", "z2", "y", "x"),
    ("z2", "y", "x", "z1"),
    ("z1", "x", "y", "z2"),
    ("z2", "z1", "x", "y"),
    ("z1", "x", "z2", "y"),
)
LAST = (("x", (0, 1)), ("z1", (2,)), ("z2", (3,)), ("y", (4, 5)))
HALVES = 2


def is_slice(dp_count, chan_count, slots):
    return (dp_count, chan_count, slots) == (8, 4, 3)


def swap(value, name):
    size = lax.axis_size("dp") * lax.axis_size("chan")
    return lax.ppermute(value, BOTH, [(i, i ^ BITS[name]) for i in range(size)])


def step_groups(step, orders):
    groups = {}
    for part, order in enumerate(orders):
        groups.setdefault(order[step], []).append(part)
    return groups


def block_rows(own):
    half = own.shape[1] // HALVES
    return [own[p // HALVES, (p % HALVES) * half : (p % HALVES + 1) * half][None] for p in range(6)]


def gather_parts(own, extra, small):
    own = lax.optimization_barrier(own)
    state = block_rows(own)
    moved = []
    for step in range(4):
        groups = step_groups(step, ORDERS)
        sent = {
            name: (jnp.concatenate([state[p] for p in parts]) if len(parts) > 1 else state[parts[0]])
            for name, parts in groups.items()
        }
        if step == 0:
            half = own.shape[1] // HALVES
            sent = {ORDERS[h][0]: own[:, h * half : (h + 1) * half] for h in range(HALVES)}
            sent, extra = lax.optimization_barrier((sent, extra))
            moved = [exchange(value, "chan", mask + 1) for mask, value in enumerate(extra)]
        elif step == 1:
            sent, small = lax.optimization_barrier((sent, small))
            small = jnp.stack([small, exchange(small, "chan", 2)])
        elif step == 2:
            sent, small = lax.optimization_barrier((sent, small))
            small = jnp.concatenate([small, exchange(small, "chan", 1)])
        else:
            sent = lax.optimization_barrier(sent)
        got = {name: swap(value, name) for name, value in sent.items()}
        if step == 3:
            return ([sent[n] for n, _ in LAST], [got[n] for n, _ in LAST], moved, small)
        got, moved, small = lax.optimization_barrier((got, moved, small))
        size = 1 << step
        for name, parts in groups.items():
            for i, p in enumerate(parts):
                state[p] = jnp.concatenate([state[p], got[name][i * size : (i + 1) * size]])


def place_of(part, bits):
    order = ORDERS[part]
    index = bits[order[2]] * 4 + bits[order[1]] * 2 + bits[order[0]]
    for _, parts in LAST:
        if part in parts:
            return (bits[order[3]], index + 8 * parts.index(part))


def slot_places(slot, slots):
    owner = slot // slots
    gap = owner ^ lax.axis_index("dp")
    bits = {"x": gap & 1, "z1": (gap >> 1) & 1, "z2": (gap >> 2) & 1}
    rows = []
    for dy in range(2):
        for h in range(HALVES):
            at = [place_of(s * HALVES + h, dict(bits, y=jnp.full_like(gap, dy))) for s in range(slots)]
            position = slot % slots
            far = jnp.select([position == s for s in range(slots)], [a[0] for a in at])
            index = jnp.select([position == s for s in range(slots)], [a[1] for a in at])
            rows.append((far * 16 + index).astype(jnp.int32))
    return (slot % slots).astype(jnp.int32), jnp.stack(rows)


def array_of(position, h):
    part = position * HALVES + h
    return [i for i, (_, parts) in enumerate(LAST) if part in parts][0]


def staged(count, depth, load, drain_in, store, drain_out):
    ahead = depth // 2
    for i in range(count + ahead):
        if i < count:
            if i >= depth:
                drain_out(i - depth)
            load(i)
        if i >= ahead:
            drain_in(i - ahead)
            store(i - ahead)
    for i in range(max(count - depth, 0), count):
        drain_out(i)


DEPTH = 8


def when_placed(position_ref, place_ref, tile, b, act):
    place = place_ref[b, tile]
    index = lax.rem(place, 16)
    for s in range(3):
        for far in range(2):

            @pl.when((position_ref[tile] == s) & (place // 16 == far))
            def _():
                act(array_of(s, b % HALVES), far, index)


def assemble_kernel(sizes, position_ref, place_ref, *refs):
    sources, outs = refs[:16], refs[16 : 16 + len(sizes)]
    buffer, in_sem, out_sem = refs[16 + len(sizes) :]
    items, first = [], 0
    for g, count in enumerate(sizes):
        items += [(core, g, j, first + j) for core in range(2) for j in range(count)]
        first += count

    def load(i):
        core, _, _, tile = items[i]
        for b in range(4):
            when_placed(
                position_ref,
                place_ref,
                tile,
                b,
                lambda array, far, index: pltpu.make_async_copy(
                    sources[core * 8 + far * 4 + array].at[index],
                    buffer.at[i % DEPTH, b],
                    in_sem.at[i % DEPTH],
                ).start(),
            )

    def drain_in(i):
        slot = buffer.at[i % DEPTH]
        pltpu.make_async_copy(slot, slot, in_sem.at[i % DEPTH]).wait()

    def out_copy(i):
        core, g, j, _ = items[i]
        return pltpu.make_async_copy(
            buffer.at[i % DEPTH], outs[g].at[core, j], out_sem.at[i % DEPTH]
        )

    staged(
        len(items), DEPTH, load, drain_in, lambda i: out_copy(i).start(), lambda i: out_copy(i).wait()
    )


def gather_tiles_here(own, tile_slot, sizes, extra, small):
    near, far, moved, small = gather_parts(own, extra, small)
    near_other = [swap(v, "core") for v in near]
    far_other = [swap(v, "core") for v in far]
    position, place = slot_places(tile_slot, own.shape[0])
    rows, width = near[0].shape[1:]
    anywhere = pl.BlockSpec(memory_space=pl.ANY)
    smem = pl.BlockSpec(memory_space=pltpu.SMEM)
    mats = pl.pallas_call(
        lambda *refs: assemble_kernel(sizes, *refs),
        in_specs=[smem, smem] + [anywhere] * 16,
        out_specs=[anywhere] * len(sizes),
        out_shape=[jax.ShapeDtypeStruct((2, n, 4, rows, width), own.dtype) for n in sizes],
        scratch_shapes=[
            pltpu.VMEM((DEPTH, 4, rows, width), own.dtype),
            pltpu.SemaphoreType.DMA((DEPTH,)),
            pltpu.SemaphoreType.DMA((DEPTH,)),
        ],
        compiler_params=pltpu.CompilerParams(vmem_limit_bytes=32 * 1024 * 1024),
    )(position, place, *near, *far, *near_other, *far_other)
    return [m.reshape(-1, width) for m in mats], moved, small


def scatter_kernel(sizes, position_ref, place_ref, *refs):
    sources, outs = refs[: len(sizes)], refs[len(sizes) : len(sizes) + 8]
    buffer, in_sem, out_sem = refs[len(sizes) + 8 :]
    items = [(g, j) for g, count in enumerate(sizes) for j in range(count)]

    def in_copy(i):
        g, j = items[i]
        return pltpu.make_async_copy(
            sources[g].at[j], buffer.at[i % DEPTH], in_sem.at[i % DEPTH]
        )

    def store(i):
        for b in range(4):
            when_placed(
                position_ref,
                place_ref,
                i,
                b,
                lambda array, far, index: pltpu.make_async_copy(
                    buffer.at[i % DEPTH, b],
                    outs[far * 4 + array].at[index],
                    out_sem.at[i % DEPTH],
                ).start(),
            )

    def drain_out(i):
        slot = buffer.at[i % DEPTH]
        pltpu.make_async_copy(slot, slot, out_sem.at[i % DEPTH]).wait()

    staged(
        len(items),
        DEPTH,
        lambda i: in_copy(i).start(),
        lambda i: in_copy(i).wait(),
        store,
        drain_out,
    )


def reduce_tiles_here(halves, tile_slot, slots, sizes, small):
    rows, width = halves[0].shape[2:]
    position, place = slot_places(tile_slot, slots)
    anywhere = pl.BlockSpec(memory_space=pl.ANY)
    smem = pl.BlockSpec(memory_space=pltpu.SMEM)
    shapes = [jax.ShapeDtypeStruct((8 * len(parts), rows, width), bf16) for _, parts in LAST]
    arrays = pl.pallas_call(
        lambda *refs: scatter_kernel(sizes, *refs),
        in_specs=[smem, smem] + [anywhere] * len(sizes),
        out_specs=[anywhere] * 8,
        out_shape=shapes + shapes,
        scratch_shapes=[
            pltpu.VMEM((DEPTH, 4, rows, width), bf16),
            pltpu.SemaphoreType.DMA((DEPTH,)),
            pltpu.SemaphoreType.DMA((DEPTH,)),
        ],
        compiler_params=pltpu.CompilerParams(vmem_limit_bytes=32 * 1024 * 1024),
    )(position, place, *halves)
    keep = {n: a for (n, _), a in zip(LAST, arrays[:4])}
    send = {n: a for (n, _), a in zip(LAST, arrays[4:])}
    state = [None] * 6
    for step in range(3, -1, -1):
        groups = step_groups(step, ORDERS)
        if step < 3:
            send, keep = {}, {}
            size = 1 << step
            for name, parts in groups.items():
                send[name] = jnp.concatenate([state[p][size:] for p in parts]).astype(bf16)
                keep[name] = jnp.concatenate([state[p][:size] for p in parts]).astype(bf16)
        send, small = lax.optimization_barrier((send, small))
        got = {name: swap(value, name) for name, value in send.items()}
        small = small + swap(small, ("z2", "z1", "x", "y")[step])
        got, small = lax.optimization_barrier((got, small))
        size = 1 << step
        for name, parts in groups.items():
            for i, p in enumerate(parts):
                cut = slice(i * size, (i + 1) * size)
                state[p] = keep[name][cut].astype(f32) + got[name][cut].astype(f32)
    return jnp.concatenate(state).reshape(slots, HALVES * rows, width), small


def owned_mask(tile_slot, slots):
    slot = lax.axis_index("dp") * slots + jnp.arange(slots, dtype=jnp.int32)
    return jnp.any(slot[:, None] == tile_slot[None, :], axis=1)[:, None, None]


def gather_tiles(own, tile_slot, sizes):
    width = own.shape[2]
    strips = lax.all_gather(own, "dp", axis=0, tiled=True)
    strips = strips.at[tile_slot].get(mode="promise_in_bounds")
    whole = lax.all_gather(strips, "chan", axis=1, tiled=True)
    mats, first = [], 0
    for n in sizes:
        mats.append(whole[first : first + n].reshape(-1, width))
        first += n
    return mats


def reduce_tiles(grads, tile_slot, slots):
    slot = jnp.arange(lax.axis_size("dp") * slots, dtype=jnp.int32)
    tile_of = jnp.argmax(slot[:, None] == tile_slot[None, :], axis=1).astype(jnp.int32)
    strips = lax.psum_scatter(grads, "chan", scatter_dimension=1, tiled=True)
    placed = strips.at[tile_of].get(mode="promise_in_bounds")
    return lax.psum_scatter(placed, "dp", scatter_dimension=0, tiled=True).astype(f32)


def norm_stats(stream):
    mean = jnp.mean(stream, axis=-1, keepdims=True)
    center = stream - mean
    spread = jnp.mean(center * center, axis=-1, keepdims=True)
    return (mean, lax.rsqrt(spread + norm_eps))


def norm_apply(stream, stats, gain, bias):
    mean, inv = stats
    return (stream - mean) * inv * gain + bias


def norm_backward(stream, stats, gain, upstream):
    mean, inv = stats
    hat = (stream - mean) * inv
    scaled = upstream * gain
    back = (
        scaled
        - jnp.mean(scaled, axis=-1, keepdims=True)
        - hat * jnp.mean(scaled * hat, axis=-1, keepdims=True)
    ) * inv
    return (back, jnp.sum(upstream * hat, axis=0), jnp.sum(upstream, axis=0))


def masked_probs(query, key, valid):
    scores = dot_rows(query, key) * HEAD_DIM ** (-0.5)
    column = lax.broadcasted_iota(jnp.int32, scores.shape, 1)
    scores = jnp.where(column < valid, scores, masked_score)
    exponent = jnp.exp(scores - jnp.max(scores, axis=-1, keepdims=True))
    return exponent / jnp.sum(exponent, axis=-1, keepdims=True)


def attend_kernel(valid_ref, q_ref, k_ref, v_ref, out_ref):
    probs = masked_probs(q_ref[...], k_ref[...], valid_ref[0]).astype(bf16)
    out_ref[...] = dot_plain(probs, v_ref[...]).astype(bf16)


def attend_back_kernel(valid_ref, q_ref, k_ref, v_ref, g_ref, dq_ref, dk_ref, dv_ref):
    query, key, grad = q_ref[...], k_ref[...], g_ref[...]
    probs = masked_probs(query, key, valid_ref[0])
    grad_probs = dot_rows(grad, v_ref[...])
    row_dot = jnp.sum(probs * grad_probs, axis=-1, keepdims=True)
    grad_scores = (probs * (grad_probs - row_dot)).astype(bf16)
    scale = HEAD_DIM ** (-0.5)
    dq_ref[...] = (dot_plain(grad_scores, key) * scale).astype(bf16)
    dk_ref[...] = (dot_cols(grad_scores, query) * scale).astype(bf16)
    dv_ref[...] = dot_cols(probs.astype(bf16), grad).astype(bf16)


def head_call(kernel, valid, operands, out_count, flops):
    rows, width = operands[0].shape
    spec = pl.BlockSpec((rows, HEAD_DIM), lambda h: (0, h))
    shape = jax.ShapeDtypeStruct((rows, width), bf16)
    return pl.pallas_call(
        kernel,
        grid=(width // HEAD_DIM,),
        in_specs=[pl.BlockSpec(memory_space=pltpu.SMEM)] + [spec] * len(operands),
        out_specs=[spec] * out_count,
        out_shape=[shape] * out_count,
        cost_estimate=pl.CostEstimate(
            flops=flops * rows * rows * width,
            bytes_accessed=2 * rows * width * (len(operands) + out_count),
            transcendentals=rows * rows * width // HEAD_DIM,
        ),
        compiler_params=pltpu.CompilerParams(vmem_limit_bytes=48 * 1024 * 1024),
    )(valid, *operands)


def ffn_forward(stream, gain, bias, w_in, w_out):
    stats = norm_stats(stream)
    normed = norm_apply(stream, stats, gain, bias).astype(bf16)
    hidden = dot_rows(normed, w_in)
    sig = jax.nn.sigmoid(hidden)
    active = (hidden * sig).astype(bf16)
    slope = (sig * (1.0 + hidden * (1.0 - sig))).astype(bf16)
    return (stream + 0.5 * dot_plain(active, w_out), (stats, normed, active, slope))


def weight_grad(left, right, local):
    if not local:
        return dot_cols(left, right).astype(bf16)
    half = left.shape[1] // 2
    other = swap(dot_cols(left[:, half:], right).astype(bf16), "core")
    return (dot_cols(left[:, :half], right) + other.astype(f32)).astype(bf16)


def ffn_backward(upstream, stream, gain, kept, w_in, w_out, local):
    stats, normed, active, slope = kept
    incoming = (0.5 * upstream).astype(bf16)
    grad_out = weight_grad(active, incoming, local)
    grad_hidden = (dot_rows(incoming, w_out) * slope.astype(f32)).astype(bf16)
    grad_in = weight_grad(grad_hidden, normed, local)
    back, grad_gain, grad_bias = norm_backward(stream, stats, gain, dot_plain(grad_hidden, w_in))
    return (upstream + back, grad_in, grad_out, grad_gain, grad_bias)


def shift_rows(value, offset):
    rows = value.shape[0]
    if offset == 0:
        return value
    if offset > 0:
        return jnp.pad(value[offset:], ((0, offset), (0, 0)))
    return jnp.pad(value[: rows + offset], ((-offset, 0), (0, 0)))


def merge_stats(one, two):
    count_a, mean_a, dev_a = one
    count_b, mean_b, dev_b = two
    count = count_a + count_b
    mean = (count_a * mean_a + count_b * mean_b) / count
    gap = mean_a - mean_b
    return (count, mean, dev_a + dev_b + gap * gap * (count_a * count_b / count))


def shards(
    inputs,
    cotangent,
    lengths,
    tile_slot,
    master,
    tile_first,
    tile_second,
    norm_params,
    norm_first,
    norm_second,
    conv_params,
    conv_first,
    conv_second,
):
    micro, _, seg_rows, width = inputs.shape
    slots, rows_tile, _ = master.shape
    chan_count, dp_count = lax.axis_size("chan"), lax.axis_size("dp")
    chan_index = lax.axis_index("chan")
    assert micro == chan_count
    rows = seg_rows * chan_count
    tile_count = tile_slot.shape[0]
    quarter = (tile_count - 7) // 4
    base = 4 * quarter

    sizes = (quarter,) * 4 + (1,) * 7
    local = is_slice(dp_count, chan_count, slots)
    both = jnp.stack([inputs[:, 0], cotangent[:, 0]], axis=1)
    mine = both
    if local:
        extra = [
            lax.dynamic_index_in_dim(both, chan_index ^ mask, 0, keepdims=True)
            for mask in range(1, chan_count)
        ]
        mats, moved, convs = gather_tiles_here(
            master.astype(bf16), tile_slot, sizes, extra, conv_params
        )
        for mask in range(1, chan_count):
            mine = lax.dynamic_update_slice_in_dim(mine, moved[mask - 1], chan_index ^ mask, 0)
        near = jnp.array([0, 2, 1, 3], jnp.int32)
        position = near[jnp.arange(chan_count, dtype=jnp.int32) ^ chan_index]
    else:
        mats = gather_tiles(master.astype(bf16), tile_slot, sizes)
        mine = swap_blocks(both, "chan")
        convs = gather_small(conv_params, "chan")
        position = jnp.arange(chan_count, dtype=jnp.int32)
    source = mine[:, 0].reshape(rows, width).astype(f32)
    upstream = mine[:, 1].reshape(rows, width).astype(f32)
    convs = jnp.moveaxis(convs, 0, 1).reshape(-1, width)
    valid = lax.dynamic_slice_in_dim(lengths[:, 0], chan_index, 1)
    in_first, out_first, in_second, out_second = mats[:4]
    w_query, w_key, w_value, w_output, p_value, p_gate, p_output = mats[4:]
    gains, biases = norm_params[:5], norm_params[5:]
    taps = convs.shape[0] - 2
    margin = (taps - 1) // 2
    bn_gain, bn_bias = convs[taps], convs[taps + 1]
    frame_mask = (jnp.arange(rows, dtype=jnp.int32) < valid[0]).astype(f32)[:, None]

    stream_one, kept_one = ffn_forward(source, gains[0], biases[0], in_first, out_first)

    stats_att = norm_stats(stream_one)
    att_in = norm_apply(stream_one, stats_att, gains[1], biases[1]).astype(bf16)
    queries = dot_rows(att_in, w_query).astype(bf16)
    keys = dot_rows(att_in, w_key).astype(bf16)
    values = dot_rows(att_in, w_value).astype(bf16)
    (merged,) = head_call(attend_kernel, valid, (queries, keys, values), 1, 4)
    stream_two = stream_one + dot_plain(merged, w_output)

    stats_conv = norm_stats(stream_two)
    conv_in = norm_apply(stream_two, stats_conv, gains[2], biases[2]).astype(bf16)
    linear = dot_rows(conv_in, p_value)
    gate_sig = jax.nn.sigmoid(dot_rows(conv_in, p_gate))
    glu = linear * gate_sig * frame_mask
    depth = jnp.zeros_like(glu)
    for t in range(taps):
        depth = depth + convs[t] * shift_rows(glu, t - margin)
    count = valid[0].astype(f32)
    local_mean = jnp.sum(depth * frame_mask, axis=0) / count
    local_gap = (depth - local_mean) * frame_mask
    local_dev = jnp.sum(local_gap * local_gap, axis=0)
    stats = (jnp.full((width,), count), local_mean, local_dev)
    mask = 1
    while mask < dp_count:
        other = exchange(jnp.stack(stats), "dp", mask)
        stats = merge_stats(stats, (other[0], other[1], other[2]))
        mask *= 2
    total_count, bn_mean, bn_dev = stats
    inv_std = lax.rsqrt(bn_dev / total_count + norm_eps)
    center = depth - bn_mean
    normal = center * inv_std * bn_gain + bn_bias
    conv_sig = jax.nn.sigmoid(normal)
    conv_act = (normal * conv_sig).astype(bf16)
    stream_three = stream_two + dot_plain(conv_act, p_output)

    stream_four, kept_four = ffn_forward(stream_three, gains[3], biases[3], in_second, out_second)
    stats_last = norm_stats(stream_four)
    result = norm_apply(stream_four, stats_last, gains[4], biases[4]).astype(bf16)

    grad_four, gain_four, bias_four = norm_backward(stream_four, stats_last, gains[4], upstream)
    grad_three, gin_second, gout_second, gain_three, bias_three = ffn_backward(
        grad_four, stream_three, gains[3], kept_four, in_second, out_second, local
    )

    incoming = grad_three.astype(bf16)
    grad_po = weight_grad(conv_act, incoming, local)
    conv_slope = conv_sig * (1.0 + normal * (1.0 - conv_sig))
    grad_normal = dot_rows(incoming, p_output) * conv_slope
    own_sums = jnp.stack([jnp.sum(grad_normal, axis=0), jnp.sum(grad_normal * center, axis=0)])
    sum_plain, sum_center = butterfly_sum(own_sums, "dp")
    bn_scale = bn_gain * inv_std
    grad_depth = bn_scale * grad_normal - frame_mask * bn_scale * (
        sum_plain + inv_std * inv_std * sum_center * center
    ) / total_count
    grad_glu = jnp.zeros_like(glu)
    tap_grads = []
    for t in range(taps):
        grad_glu = grad_glu + convs[t] * shift_rows(grad_depth, margin - t)
        tap_grads.append(jnp.sum(grad_depth * shift_rows(glu, t - margin), axis=0))
    grad_glu = grad_glu * frame_mask
    grad_linear = (grad_glu * gate_sig).astype(bf16)
    grad_gating = (grad_glu * linear * gate_sig * (1.0 - gate_sig)).astype(bf16)
    grad_pv = weight_grad(grad_linear, conv_in, local)
    grad_pg = weight_grad(grad_gating, conv_in, local)
    back, gain_two, bias_two = norm_backward(
        stream_two,
        stats_conv,
        gains[2],
        dot_plain(grad_linear, p_value) + dot_plain(grad_gating, p_gate),
    )
    grad_two = grad_three + back

    incoming = grad_two.astype(bf16)
    grad_wo = weight_grad(merged, incoming, local)
    grad_merged = dot_rows(incoming, w_output).astype(bf16)
    grad_q, grad_k, grad_v = head_call(
        attend_back_kernel, valid, (queries, keys, values, grad_merged), 3, 10
    )
    grad_wq = weight_grad(grad_q, att_in, local)
    grad_wk = weight_grad(grad_k, att_in, local)
    grad_wv = weight_grad(grad_v, att_in, local)
    back, gain_one, bias_one = norm_backward(
        stream_one,
        stats_att,
        gains[1],
        dot_plain(grad_q, w_query) + dot_plain(grad_k, w_key) + dot_plain(grad_v, w_value),
    )
    grad_one = grad_two + back

    grad_zero, gin_first, gout_first, gain_zero, bias_zero = ffn_backward(
        grad_one, source, gains[0], kept_one, in_first, out_first, local
    )

    grads = [gin_first, gout_first, gin_second, gout_second]
    grads += [grad_wq, grad_wk, grad_wv, grad_wo, grad_pv, grad_pg, grad_po]
    conv_small = jnp.stack(tap_grads + [own_sums[1] * inv_std, own_sums[0]])
    conv_small = conv_small.reshape(-1, chan_count, rows_tile)[:, position].reshape(-1, width)
    small = jnp.concatenate(
        [
            jnp.stack(
                [gain_zero, gain_one, gain_two, gain_three, gain_four]
                + [bias_zero, bias_one, bias_two, bias_three, bias_four]
            ),
            conv_small,
        ]
    )
    if local:
        halves = [g.reshape(n, 4, -1, width) for g, n in zip(grads, sizes)]
        small = small + swap(small, "core")
        owned, small = reduce_tiles_here(halves, tile_slot, slots, sizes, small)
    else:
        owned = reduce_tiles(
            jnp.concatenate(grads).reshape(tile_count, width, width), tile_slot, slots
        )
        small = butterfly_sum(butterfly_sum(small, "dp"), "chan")
    owned = jnp.where(owned_mask(tile_slot, slots), owned, 0.0)
    norm_total = small[: norm_params.shape[0]]
    conv_grad = lax.dynamic_slice_in_dim(
        small[norm_params.shape[0] :], chan_index * rows_tile, rows_tile, 1
    )

    tile_m, tile_v, tile_w = adamw_step(
        master, owned, tile_first, tile_second, tile_rate, weight_decay
    )
    norm_m, norm_v, norm_w = adamw_step(
        norm_params, norm_total, norm_first, norm_second, small_rate, 0.0
    )
    conv_m, conv_v, conv_w = adamw_step(
        conv_params, conv_grad, conv_first, conv_second, small_rate, 0.0
    )
    block_out = swap_blocks(result.reshape(chan_count, seg_rows, width), "chan")
    block_grad = swap_blocks(
        grad_zero.astype(bf16).reshape(chan_count, seg_rows, width), "chan"
    ).astype(f32)
    return (
        block_out[:, None],
        block_grad[:, None],
        tile_m,
        tile_v,
        tile_w,
        tile_w.astype(bf16),
        norm_m,
        norm_v,
        norm_w,
        conv_m,
        conv_v,
        conv_w,
    )


def solution(mesh):
    in_specs = (
        P(None, "dp", "chan", None),
        P(None, "dp", "chan", None),
        P(None, "dp"),
        P(),
        P("dp", "chan", None),
        P("dp", "chan", None),
        P("dp", "chan", None),
        P(),
        P(),
        P(),
        P(None, "chan"),
        P(None, "chan"),
        P(None, "chan"),
    )
    out_specs = (
        P(None, "dp", "chan", None),
        P(None, "dp", "chan", None),
        P("dp", "chan", None),
        P("dp", "chan", None),
        P("dp", "chan", None),
        P("dp", "chan", None),
        P(),
        P(),
        P(),
        P(None, "chan"),
        P(None, "chan"),
        P(None, "chan"),
    )
    return jax.shard_map(shards, mesh=mesh, in_specs=in_specs, out_specs=out_specs, check_vma=False)
```

```python
import jax
import jax.numpy as jnp
from jax import lax
from jax.experimental import pallas as pl
from jax.experimental.pallas import tpu as pltpu
from jax.sharding import PartitionSpec as P

HEAD_DIM = 128
STEP = 10

norm_eps = 1e-05
masked_score = -1e30
beta_one = 0.9
beta_two = 0.98
adam_eps = 1e-08
tile_rate = 0.06
small_rate = 0.6
weight_decay = 0.01

BOTH = ("dp", "chan")
bf16 = jnp.bfloat16
f32 = jnp.float32


def dot_rows(left, right):
    return lax.dot_general(left, right, (((1,), (1,)), ((), ())), preferred_element_type=f32)


def dot_plain(left, right):
    return jnp.dot(left, right, preferred_element_type=f32)


def dot_cols(left, right):
    return lax.dot_general(left, right, (((0,), (0,)), ((), ())), preferred_element_type=f32)


def adamw_step(weight, gradient, first_old, second_old, rate, decay):
    first_new = beta_one * first_old + (1.0 - beta_one) * gradient
    second_new = beta_two * second_old + (1.0 - beta_two) * gradient * gradient
    first_hat = first_new / (1.0 - beta_one**STEP)
    second_hat = second_new / (1.0 - beta_two**STEP)
    weight_new = weight - rate * (first_hat / (jnp.sqrt(second_hat) + adam_eps) + decay * weight)
    return (first_new, second_new, weight_new)


def exchange(value, axis, mask):
    size = lax.axis_size(axis)
    return lax.ppermute(value, axis, [(i, i ^ mask) for i in range(size)])


def swap_blocks(value, axis):
    size = lax.axis_size(axis)
    me = lax.axis_index(axis)
    result = value
    for mask in range(1, size):
        sent = lax.dynamic_index_in_dim(value, me ^ mask, 0, keepdims=True)
        result = lax.dynamic_update_slice_in_dim(result, exchange(sent, axis, mask), me ^ mask, 0)
    return result


def swap_in_hops(value):
    me = lax.axis_index("chan")
    pairs = value.reshape((2, 2) + value.shape[1:])
    core, y = lax.rem(me, 2), lax.div(me, 2)
    keep = lax.dynamic_index_in_dim(pairs, core, 1, keepdims=False)
    sent = lax.dynamic_index_in_dim(pairs, 1 - core, 1, keepdims=False)
    got = exchange(sent, "chan", 1)
    low = jnp.where(core == 0, keep, got)
    high = jnp.where(core == 0, got, keep)
    mixed = jnp.stack([low, high], axis=1)
    there = lax.dynamic_index_in_dim(mixed, 1 - y, 0, keepdims=False)
    here = lax.dynamic_index_in_dim(mixed, y, 0, keepdims=False)
    return here, there


def finish_hops(here, arrived_there):
    y = lax.div(lax.axis_index("chan"), 2)
    low = jnp.where(y == 0, here, arrived_there)
    high = jnp.where(y == 0, arrived_there, here)
    return jnp.concatenate([low, high])


def gather_small(value, axis):
    size = lax.axis_size(axis)
    me = lax.axis_index(axis)
    result = jnp.zeros((size,) + value.shape, value.dtype)
    result = lax.dynamic_update_slice_in_dim(result, value[None], me, 0)
    for mask in range(1, size):
        result = lax.dynamic_update_slice_in_dim(
            result, exchange(value[None], axis, mask), me ^ mask, 0
        )
    return result


def butterfly_sum(value, axis):
    size = lax.axis_size(axis)
    mask = 1
    while mask < size:
        value = value + exchange(value, axis, mask)
        mask *= 2
    return value


BITS = {"core": 1, "y": 2, "x": 4, "z1": 8, "z2": 16}
ORDERS = (
    ("z2", "y", "z1", "x"),
    ("z1", "z2", "y", "x"),
    ("z2", "y", "x", "z1"),
    ("z1", "x", "y", "z2"),
    ("z2", "z1", "x", "y"),
    ("z1", "x", "z2", "y"),
)
LAST = (("x", (0, 1)), ("z1", (2,)), ("z2", (3,)), ("y", (4, 5)))
HALVES = 2


def is_slice(dp_count, chan_count, slots):
    return (dp_count, chan_count, slots) == (8, 4, 3)


def swap(value, name):
    size = lax.axis_size("dp") * lax.axis_size("chan")
    return lax.ppermute(value, BOTH, [(i, i ^ BITS[name]) for i in range(size)])


def step_groups(step, orders):
    groups = {}
    for part, order in enumerate(orders):
        groups.setdefault(order[step], []).append(part)
    return groups


def gather_parts(master, extra, small):
    half = master.shape[1] // HALVES
    own = [master[:, h * half : (h + 1) * half].astype(bf16) for h in range(HALVES)]
    own = lax.optimization_barrier(own)
    state = [own[p % HALVES][p // HALVES][None] for p in range(6)]
    moved = []
    for step in range(4):
        groups = step_groups(step, ORDERS)
        sent = {
            name: (jnp.concatenate([state[p] for p in parts]) if len(parts) > 1 else state[parts[0]])
            for name, parts in groups.items()
        }
        if step == 0:
            sent = {ORDERS[h][0]: own[h] for h in range(HALVES)}
            sent, extra = lax.optimization_barrier((sent, extra))
            moved = [exchange(value, "chan", mask + 1) for mask, value in enumerate(extra)]
        elif step == 1:
            sent, small = lax.optimization_barrier((sent, small))
            small = jnp.stack([small, exchange(small, "chan", 2)])
        elif step == 2:
            sent, small = lax.optimization_barrier((sent, small))
            small = jnp.concatenate([small, exchange(small, "chan", 1)])
        else:
            sent = lax.optimization_barrier(sent)
        got = {name: swap(value, name) for name, value in sent.items()}
        if step == 3:
            return ([sent[n] for n, _ in LAST], [got[n] for n, _ in LAST], moved, small)
        got, moved, small = lax.optimization_barrier((got, moved, small))
        size = 1 << step
        for name, parts in groups.items():
            for i, p in enumerate(parts):
                state[p] = jnp.concatenate([state[p], got[name][i * size : (i + 1) * size]])


def place_of(part, bits):
    order = ORDERS[part]
    index = bits[order[2]] * 4 + bits[order[1]] * 2 + bits[order[0]]
    for _, parts in LAST:
        if part in parts:
            return (bits[order[3]], index + 8 * parts.index(part))


def array_of(position, h):
    part = position * HALVES + h
    return [i for i, (_, parts) in enumerate(LAST) if part in parts][0]


def slot_places(slot, slots):
    owner, position = slot // slots, slot % slots
    gap = owner ^ lax.axis_index("dp")
    bits = {"x": gap & 1, "z1": (gap >> 1) & 1, "z2": (gap >> 2) & 1}
    rows = []
    for dy in range(2):
        for h in range(HALVES):
            codes = []
            for s in range(slots):
                far, index = place_of(s * HALVES + h, dict(bits, y=jnp.full_like(gap, dy)))
                codes.append((far * 4 + array_of(s, h)) * 16 + index)
            rows.append(jnp.select([position == s for s in range(slots)], codes))
    return jnp.stack(rows).astype(jnp.int32)


def at_place(place, arrays, act):
    which, index = lax.div(place, 16), lax.rem(place, 16)
    for i, array in enumerate(arrays):

        @pl.when(which == i)
        def _():
            act(array, index)


def staged(count, depth, load, drain_in, store, drain_out):
    ahead = depth // 2
    for i in range(count + ahead):
        if i < count:
            if i >= depth:
                drain_out(i - depth)
            load(i)
        if i >= ahead:
            drain_in(i - ahead)
            store(i - ahead)
    for i in range(max(count - depth, 0), count):
        drain_out(i)


DEPTH = 8


SOURCES = 13


def sixteen(refs):
    near, at = [], 0
    for _, parts in LAST:
        near.append(refs[8].at[pl.ds(at, 8 * len(parts))])
        at += 8 * len(parts)
    return list(refs[:8]) + near + list(refs[9:SOURCES])


def assemble_kernel(first, place_ref, *refs):
    sources, outs = sixteen(refs), refs[SOURCES:-3]
    buffer, in_sem, out_sem = refs[-3:]
    items = [(core, g) for core in range(2) for g in range(len(outs))]

    def load(i):
        core, g = items[i]
        for b in range(4):
            at_place(
                place_ref[b, first + g],
                sources[core * 8 : core * 8 + 8],
                lambda array, index: pltpu.make_async_copy(
                    array.at[index], buffer.at[i % DEPTH, b], in_sem.at[i % DEPTH]
                ).start(),
            )

    def drain_in(i):
        slot = buffer.at[i % DEPTH]
        pltpu.make_async_copy(slot, slot, in_sem.at[i % DEPTH]).wait()

    def out_copy(i):
        core, g = items[i]
        return pltpu.make_async_copy(buffer.at[i % DEPTH], outs[g].at[core], out_sem.at[i % DEPTH])

    staged(
        len(items), DEPTH, load, drain_in, lambda i: out_copy(i).start(), lambda i: out_copy(i).wait()
    )


ANYWHERE = pl.BlockSpec(memory_space=pl.ANY)
IN_SMEM = pl.BlockSpec(memory_space=pltpu.SMEM)
IN_VMEM = pl.BlockSpec(memory_space=pltpu.VMEM)


def assemble(place, sources, first, count):
    rows, width = sources[0].shape[1:]
    mats = pl.pallas_call(
        lambda *refs: assemble_kernel(first, *refs),
        in_specs=[IN_SMEM] + [ANYWHERE] * SOURCES,
        out_specs=[ANYWHERE] * count,
        out_shape=[jax.ShapeDtypeStruct((2, 4, rows, width), bf16)] * count,
        scratch_shapes=[
            pltpu.VMEM((DEPTH, 4, rows, width), bf16),
            pltpu.SemaphoreType.DMA((DEPTH,)),
            pltpu.SemaphoreType.DMA((DEPTH,)),
        ],
        compiler_params=pltpu.CompilerParams(vmem_limit_bytes=32 * 1024 * 1024),
        cost_estimate=pl.CostEstimate(
            flops=0, bytes_accessed=count * 32 * rows * width, transcendentals=0
        ),
    )(place, *sources)
    return [m.reshape(-1, width) for m in mats]


def gather_sources(master, extra, small):
    near, far, moved, small = gather_parts(master, extra, small)
    near_other = swap(jnp.concatenate(near), "core")
    far_other = [swap(v, "core") for v in far]
    return near + far + [near_other] + far_other, moved, small


BPS = 2
STEPS = 4 // BPS


def fetch_rows(at, item, firsts, count, place_ref, sources, buffers, sems):
    core, step = item
    rows = sources[0].shape[1]
    for m, first in enumerate(firsts):
        for i in range(BPS):
            for j in range(count):
                at_place(
                    place_ref[step * BPS + i, first + j],
                    sources[core * 8 : core * 8 + 8],
                    lambda array, index: pltpu.make_async_copy(
                        array.at[index],
                        buffers[m].at[at, pl.ds((i * count + j) * rows, rows)],
                        sems.at[m, at],
                    ).start(),
                )


def arrived(m, at, buffers, sems):
    pltpu.make_async_copy(buffers[m].at[at], buffers[m].at[at], sems.at[m, at]).wait()
    return buffers[m][at]


def ffn_kernel(firsts, count, place_ref, normed_ref, base_ref, *refs):
    sources = sixteen(refs)
    out_ref, act_ref, slope_ref, in_buf, out_buf, sems = refs[SOURCES:]
    buffers = (in_buf, out_buf)
    size = in_buf.shape[1]
    items = [(core, q) for core in range(2) for q in range(STEPS)]
    for i in range(2):
        fetch_rows(i, items[i], firsts, count, place_ref, sources, buffers, sems)
    for i, (core, q) in enumerate(items):
        cut = slice(i * size, (i + 1) * size)
        hidden = dot_rows(normed_ref[...], arrived(0, i % 2, buffers, sems))
        sig = jax.nn.sigmoid(hidden)
        active = (hidden * sig).astype(bf16)
        act_ref[:, cut] = active
        slope_ref[:, cut] = (sig * (1.0 + hidden * (1.0 - sig))).astype(bf16)
        before = base_ref[...] if i == 0 else out_ref[...]
        out_ref[...] = before + 0.5 * dot_plain(active, arrived(1, i % 2, buffers, sems))
        if i + 2 < len(items):
            fetch_rows(i % 2, items[i + 2], firsts, count, place_ref, sources, buffers, sems)


def ffn_back_kernel(cores, based, firsts, count, place_ref, e_ref, act_ref, slope_ref, normed_ref, *refs):
    base_ref, refs = (refs[0], refs[1:]) if based else (None, refs)
    sources, refs = sixteen(refs), refs[SOURCES:]
    dx_ref, grads, refs = refs[0], refs[1 : 1 + 2 * len(cores)], refs[1 + 2 * len(cores) :]
    in_grads, out_grads, put_sems, in_buf, out_buf, sems = refs
    buffers = (in_buf, out_buf)
    size = in_buf.shape[1]
    items = [(core, q) for core in cores for q in range(STEPS)]
    for i in range(2):
        fetch_rows(i, items[i], firsts, count, place_ref, sources, buffers, sems)

    def copy(m, i):
        core, q = items[i]
        target = grads[2 * cores.index(core) + m].at[pl.ds(q * size, size)]
        buffer = (in_grads, out_grads)[m]
        return pltpu.make_async_copy(buffer.at[i % 2], target, put_sems.at[m, i % 2])

    for i, (core, q) in enumerate(items):
        cut = slice((core * STEPS + q) * size, (core * STEPS + q + 1) * size)
        incoming = e_ref[...]
        grad = dot_rows(incoming, arrived(1, i % 2, buffers, sems)) * slope_ref[:, cut].astype(f32)
        grad = grad.astype(bf16)
        change = dot_plain(grad, arrived(0, i % 2, buffers, sems))
        if i + 2 < len(items):
            fetch_rows(i % 2, items[i + 2], firsts, count, place_ref, sources, buffers, sems)
        if i > 0:
            dx_ref[...] += change
        elif based:
            dx_ref[...] = base_ref[...] + change
        else:
            dx_ref[...] = change
        if i >= 2:
            copy(1, i - 2).wait()
        out_grads[i % 2] = dot_cols(act_ref[:, cut], incoming).astype(bf16)
        copy(1, i).start()
        if i >= 2:
            copy(0, i - 2).wait()
        in_grads[i % 2] = dot_cols(grad, normed_ref[...]).astype(bf16)
        copy(0, i).start()
    for i in range(len(items) - 2, len(items)):
        for m in range(2):
            copy(m, i).wait()


def grads_kernel(pairs, lefts, rights, *refs):
    left_refs, right_refs = refs[:lefts], refs[lefts : lefts + rights]
    other, own, buffer, sems = refs[lefts + rights :]
    half = own.shape[1]
    for k, (i, j) in enumerate(pairs):
        slot = k % 2
        if k >= 2:
            pltpu.make_async_copy(buffer.at[slot], buffer.at[slot], sems.at[slot]).wait()
        buffer[slot] = dot_cols(left_refs[i][...], right_refs[j][...]).astype(bf16)
        pltpu.make_async_copy(buffer.at[slot, pl.ds(0, half)], own.at[k], sems.at[slot]).start()
        pltpu.make_async_copy(buffer.at[slot, pl.ds(half, half)], other.at[k], sems.at[slot]).start()
    for slot in range(2):
        pltpu.make_async_copy(buffer.at[slot], buffer.at[slot], sems.at[slot]).wait()


def single_grads(pairs, lefts, rights):
    rows, width = lefts[0].shape
    shape = jax.ShapeDtypeStruct((len(pairs), width // 2, width), bf16)
    return pl.pallas_call(
        lambda *refs: grads_kernel(pairs, len(lefts), len(rights), *refs),
        in_specs=[IN_VMEM] * (len(lefts) + len(rights)),
        out_specs=[ANYWHERE] * 2,
        out_shape=[shape] * 2,
        scratch_shapes=[pltpu.VMEM((2, width, width), bf16), pltpu.SemaphoreType.DMA((2,))],
        compiler_params=pltpu.CompilerParams(vmem_limit_bytes=32 * 1024 * 1024),
        cost_estimate=pl.CostEstimate(
            flops=2 * len(pairs) * rows * width * width,
            bytes_accessed=2 * len(pairs) * width * (width + 2 * rows),
            transcendentals=0,
        ),
    )(*lefts, *rights)


def ffn_scratch(count, rows, width):
    return [
        pltpu.VMEM((2, BPS * count * rows, width), bf16),
        pltpu.VMEM((2, BPS * count * rows, width), bf16),
        pltpu.SemaphoreType.DMA((2, 2)),
    ]


def ffn_forward_here(stream, gain, bias, firsts, count, place, sources):
    rows, width = stream.shape
    block = sources[0].shape[1]
    hidden = 8 * count * block
    shape = jax.ShapeDtypeStruct
    stats = norm_stats(stream)
    normed = norm_apply(stream, stats, gain, bias).astype(bf16)
    result, active, slope = pl.pallas_call(
        lambda *refs: ffn_kernel(firsts, count, *refs),
        in_specs=[IN_SMEM] + [IN_VMEM] * 2 + [ANYWHERE] * SOURCES,
        out_specs=[IN_VMEM] * 3,
        out_shape=[
            shape((rows, width), f32),
            shape((rows, hidden), bf16),
            shape((rows, hidden), bf16),
        ],
        scratch_shapes=ffn_scratch(count, block, width),
        compiler_params=pltpu.CompilerParams(vmem_limit_bytes=FORWARD_MB * 1024 * 1024),
        cost_estimate=pl.CostEstimate(
            flops=4 * rows * width * hidden,
            bytes_accessed=4 * hidden * (width + rows),
            transcendentals=rows * hidden,
        ),
    )(place, normed, stream, *sources)
    return (result, (stats, normed, active, slope))


FORWARD_MB = 40
BACKWARD_MB = 48


def ffn_backward_here(upstream, stream, gain, kept, firsts, count, place, sources, calls):
    stats, normed, active, slope = kept
    rows, width = stream.shape
    block = sources[0].shape[1]
    half = 4 * count * block
    size = BPS * count * block
    shape = jax.ShapeDtypeStruct
    incoming = (0.5 * upstream).astype(bf16)
    base, grads = [], []
    for cores in calls:
        dx, *some = pl.pallas_call(
            lambda *refs, cores=cores: ffn_back_kernel(cores, bool(base), firsts, count, *refs),
            in_specs=[IN_SMEM] + [IN_VMEM] * (4 + len(base)) + [ANYWHERE] * SOURCES,
            out_specs=[IN_VMEM] + [ANYWHERE] * (2 * len(cores)),
            out_shape=[shape((rows, width), f32)]
            + [shape((half, width), bf16)] * (2 * len(cores)),
            scratch_shapes=[
                pltpu.VMEM((2, size, width), bf16),
                pltpu.VMEM((2, size, width), bf16),
                pltpu.SemaphoreType.DMA((2, 2)),
            ]
            + ffn_scratch(count, block, width),
            compiler_params=pltpu.CompilerParams(vmem_limit_bytes=BACKWARD_MB * 1024 * 1024),
            cost_estimate=pl.CostEstimate(
                flops=8 * rows * width * half * len(cores),
                bytes_accessed=8 * half * (width + rows) * len(cores),
                transcendentals=0,
            ),
        )(place, incoming, active, slope, normed, *base, *sources)
        base = [dx]
        if not grads:
            some = [swap(v, "core") for v in some[:2]] + some[2:]
        grads += some
    other_in, other_out, own_in, own_out = grads
    back, grad_gain, grad_bias = norm_backward(stream, stats, gain, dx)
    return (upstream + back, (own_in, other_in), (own_out, other_out), grad_gain, grad_bias)


SCATTER = 6


def scatter_kernel(groups, place_ref, *refs):
    owns, others = refs[: len(groups)], refs[len(groups) : 2 * len(groups)]
    outs = refs[2 * len(groups) : 2 * len(groups) + 8]
    own_buf, other_buf, in_sem, out_sem = refs[2 * len(groups) + 8 :]
    items = []
    for g, (first, count, whole) in enumerate(groups):
        if whole:
            items += [(g, k, [(b, first + k) for b in range(4)]) for k in range(count)]
        else:
            items += [(g, b, [(b, first + j) for j in range(count)]) for b in range(4)]

    def in_copies(i):
        g, k, _ = items[i]
        slot = i % SCATTER
        return (
            pltpu.make_async_copy(owns[g].at[k], own_buf.at[slot], in_sem.at[0, slot]),
            pltpu.make_async_copy(others[g].at[k], other_buf.at[slot], in_sem.at[1, slot]),
        )

    def load(i):
        for copy in in_copies(i):
            copy.start()

    def drain_in(i):
        for copy in in_copies(i):
            copy.wait()

    def store(i):
        slot = i % SCATTER
        own_buf[slot] = (own_buf[slot].astype(f32) + other_buf[slot].astype(f32)).astype(bf16)
        for at, (b, tile) in enumerate(items[i][2]):
            at_place(
                place_ref[b, tile],
                outs,
                lambda array, index: pltpu.make_async_copy(
                    own_buf.at[slot, at], array.at[index], out_sem.at[slot]
                ).start(),
            )

    def drain_out(i):
        slot = own_buf.at[i % SCATTER]
        pltpu.make_async_copy(slot, slot, out_sem.at[i % SCATTER]).wait()

    staged(len(items), SCATTER, load, drain_in, store, drain_out)


def reduce_tiles_here(groups, owns, others, place, slots, small, ahead):
    rows, width = owns[0].shape[2:]
    shapes = [jax.ShapeDtypeStruct((8 * len(parts), rows, width), bf16) for _, parts in LAST]
    arrays = pl.pallas_call(
        lambda *refs: scatter_kernel(groups, *refs),
        in_specs=[IN_SMEM] + [ANYWHERE] * (2 * len(groups)),
        out_specs=[ANYWHERE] * 8,
        out_shape=shapes + shapes,
        scratch_shapes=[
            pltpu.VMEM((SCATTER, 4, rows, width), bf16),
            pltpu.VMEM((SCATTER, 4, rows, width), bf16),
            pltpu.SemaphoreType.DMA((2, SCATTER)),
            pltpu.SemaphoreType.DMA((SCATTER,)),
        ],
        compiler_params=pltpu.CompilerParams(vmem_limit_bytes=32 * 1024 * 1024),
        cost_estimate=pl.CostEstimate(
            flops=0, bytes_accessed=6 * 92 * rows * width, transcendentals=0
        ),
    )(place, *owns, *others)
    arrays, ahead = lax.optimization_barrier((arrays, ahead))
    keep = {n: a for (n, _), a in zip(LAST, arrays[:4])}
    send = {n: a for (n, _), a in zip(LAST, arrays[4:])}
    state = [None] * 6
    for step in range(3, -1, -1):
        groups = step_groups(step, ORDERS)
        if step < 3:
            send, keep = {}, {}
            size = 1 << step
            for name, parts in groups.items():
                send[name] = jnp.concatenate([state[p][size:] for p in parts]).astype(bf16)
                keep[name] = jnp.concatenate([state[p][:size] for p in parts]).astype(bf16)
        send, small = lax.optimization_barrier((send, small))
        got = {name: swap(value, name) for name, value in send.items()}
        small = small + swap(small, ("z2", "z1", "x", "y")[step])
        got, small = lax.optimization_barrier((got, small))
        if step == 0:
            return [keep[n] for n in groups], [got[n] for n in groups], small, ahead
        size = 1 << step
        for name, parts in groups.items():
            for i, p in enumerate(parts):
                cut = slice(i * size, (i + 1) * size)
                state[p] = keep[name][cut].astype(f32) + got[name][cut].astype(f32)


def update_kernel(filled_ref, k0, g0, k1, g1, w_ref, m_ref, v_ref, m_new, v_new, w_new, b_new):
    half = pl.program_id(1)
    first = k0[...].astype(f32) + g0[...].astype(f32)
    second = k1[...].astype(f32) + g1[...].astype(f32)
    gradient = jnp.where(half == 0, first, second)
    gradient = jnp.where(filled_ref[pl.program_id(0)] > 0, gradient, 0.0)
    moment, square, weight = adamw_step(
        w_ref[...], gradient, m_ref[...], v_ref[...], tile_rate, weight_decay
    )
    m_new[...], v_new[...], w_new[...] = moment, square, weight
    b_new[...] = weight.astype(bf16)


def update_tiles_here(keep, got, filled, master, tile_first, tile_second):
    slots, full, width = master.shape
    rows = full // HALVES
    part = pl.BlockSpec((1, rows, width), lambda s, h: (s, 0, 0))
    here = pl.BlockSpec((1, rows, width), lambda s, h: (s, h, 0))
    shape = jax.ShapeDtypeStruct(master.shape, f32)
    return pl.pallas_call(
        update_kernel,
        grid=(slots, HALVES),
        in_specs=[IN_SMEM] + [part] * 4 + [here] * 3,
        out_specs=[here] * 4,
        out_shape=[shape] * 3 + [jax.ShapeDtypeStruct(master.shape, bf16)],
        compiler_params=pltpu.CompilerParams(vmem_limit_bytes=32 * 1024 * 1024),
        cost_estimate=pl.CostEstimate(
            flops=20 * slots * full * width,
            bytes_accessed=30 * slots * full * width,
            transcendentals=slots * full * width,
        ),
    )(filled, keep[0], got[0], keep[1], got[1], master, tile_first, tile_second)


def owned_mask(tile_slot, slots):
    slot = lax.axis_index("dp") * slots + jnp.arange(slots, dtype=jnp.int32)
    return jnp.any(slot[:, None] == tile_slot[None, :], axis=1)


def gather_tiles(own, tile_slot, sizes):
    width = own.shape[2]
    strips = lax.all_gather(own, "dp", axis=0, tiled=True)
    strips = strips.at[tile_slot].get(mode="promise_in_bounds")
    whole = lax.all_gather(strips, "chan", axis=1, tiled=True)
    mats, first = [], 0
    for n in sizes:
        mats.append(whole[first : first + n].reshape(-1, width))
        first += n
    return mats


def reduce_tiles(grads, tile_slot, slots):
    slot = jnp.arange(lax.axis_size("dp") * slots, dtype=jnp.int32)
    tile_of = jnp.argmax(slot[:, None] == tile_slot[None, :], axis=1).astype(jnp.int32)
    strips = lax.psum_scatter(grads, "chan", scatter_dimension=1, tiled=True)
    placed = strips.at[tile_of].get(mode="promise_in_bounds")
    return lax.psum_scatter(placed, "dp", scatter_dimension=0, tiled=True).astype(f32)


def norm_stats(stream):
    mean = jnp.mean(stream, axis=-1, keepdims=True)
    center = stream - mean
    spread = jnp.mean(center * center, axis=-1, keepdims=True)
    return (mean, lax.rsqrt(spread + norm_eps))


def norm_apply(stream, stats, gain, bias):
    mean, inv = stats
    return (stream - mean) * inv * gain + bias


def norm_backward(stream, stats, gain, upstream):
    mean, inv = stats
    hat = (stream - mean) * inv
    scaled = upstream * gain
    back = (
        scaled
        - jnp.mean(scaled, axis=-1, keepdims=True)
        - hat * jnp.mean(scaled * hat, axis=-1, keepdims=True)
    ) * inv
    return (back, jnp.sum(upstream * hat, axis=0), jnp.sum(upstream, axis=0))


def masked_probs(query, key, valid):
    scores = dot_rows(query, key)
    column = lax.broadcasted_iota(jnp.int32, scores.shape, 1)
    scores = jnp.where(column < valid, scores * HEAD_DIM ** (-0.5), masked_score)
    exponent = jnp.exp(scores - jnp.max(scores, axis=-1, keepdims=True))
    return exponent * (1.0 / jnp.sum(exponent, axis=-1, keepdims=True))


def attend_kernel(valid_ref, q_ref, k_ref, v_ref, out_ref):
    probs = masked_probs(q_ref[...], k_ref[...], valid_ref[0]).astype(bf16)
    out_ref[...] = dot_plain(probs, v_ref[...]).astype(bf16)


def attend_back_kernel(valid_ref, q_ref, k_ref, v_ref, g_ref, dq_ref, dk_ref, dv_ref):
    query, key, grad = q_ref[...], k_ref[...], g_ref[...]
    probs = masked_probs(query, key, valid_ref[0])
    grad_probs = dot_rows(grad, v_ref[...])
    row_dot = jnp.sum(probs * grad_probs, axis=-1, keepdims=True)
    grad_scores = (probs * (grad_probs - row_dot)).astype(bf16)
    scale = HEAD_DIM ** (-0.5)
    dq_ref[...] = (dot_plain(grad_scores, key) * scale).astype(bf16)
    dk_ref[...] = (dot_cols(grad_scores, query) * scale).astype(bf16)
    dv_ref[...] = dot_cols(probs.astype(bf16), grad).astype(bf16)


def head_call(kernel, valid, operands, out_count, flops):
    rows, width = operands[0].shape
    spec = pl.BlockSpec((rows, HEAD_DIM), lambda h: (0, h))
    shape = jax.ShapeDtypeStruct((rows, width), bf16)
    return pl.pallas_call(
        kernel,
        grid=(width // HEAD_DIM,),
        in_specs=[pl.BlockSpec(memory_space=pltpu.SMEM)] + [spec] * len(operands),
        out_specs=[spec] * out_count,
        out_shape=[shape] * out_count,
        cost_estimate=pl.CostEstimate(
            flops=flops * rows * rows * width,
            bytes_accessed=2 * rows * width * (len(operands) + out_count),
            transcendentals=rows * rows * width // HEAD_DIM,
        ),
        compiler_params=pltpu.CompilerParams(vmem_limit_bytes=48 * 1024 * 1024),
    )(valid, *operands)


def ffn_forward(stream, gain, bias, w_in, w_out):
    stats = norm_stats(stream)
    normed = norm_apply(stream, stats, gain, bias).astype(bf16)
    hidden = dot_rows(normed, w_in)
    sig = jax.nn.sigmoid(hidden)
    active = (hidden * sig).astype(bf16)
    slope = (sig * (1.0 + hidden * (1.0 - sig))).astype(bf16)
    return (stream + 0.5 * dot_plain(active, w_out), (stats, normed, active, slope))


def weight_grad(left, right):
    return dot_cols(left, right).astype(bf16)


def ffn_backward(upstream, stream, gain, kept, w_in, w_out):
    stats, normed, active, slope = kept
    incoming = (0.5 * upstream).astype(bf16)
    grad_out = weight_grad(active, incoming)
    grad_hidden = (dot_rows(incoming, w_out) * slope.astype(f32)).astype(bf16)
    grad_in = weight_grad(grad_hidden, normed)
    back, grad_gain, grad_bias = norm_backward(stream, stats, gain, dot_plain(grad_hidden, w_in))
    return (upstream + back, grad_in, grad_out, grad_gain, grad_bias)


def shift_rows(value, offset):
    rows = value.shape[0]
    if offset == 0:
        return value
    if offset > 0:
        return jnp.pad(value[offset:], ((0, offset), (0, 0)))
    return jnp.pad(value[: rows + offset], ((-offset, 0), (0, 0)))


def merge_stats(one, two):
    count_a, mean_a, dev_a = one
    count_b, mean_b, dev_b = two
    count = count_a + count_b
    mean = (count_a * mean_a + count_b * mean_b) / count
    gap = mean_a - mean_b
    return (count, mean, dev_a + dev_b + gap * gap * (count_a * count_b / count))


def shards(
    inputs,
    cotangent,
    lengths,
    tile_slot,
    master,
    tile_first,
    tile_second,
    norm_params,
    norm_first,
    norm_second,
    conv_params,
    conv_first,
    conv_second,
):
    micro, _, seg_rows, width = inputs.shape
    slots, rows_tile, _ = master.shape
    chan_count, dp_count = lax.axis_size("chan"), lax.axis_size("dp")
    chan_index = lax.axis_index("chan")
    assert micro == chan_count
    rows = seg_rows * chan_count
    tile_count = tile_slot.shape[0]
    quarter = (tile_count - 7) // 4
    base = 4 * quarter

    sizes = (quarter,) * 4 + (1,) * 7
    local = is_slice(dp_count, chan_count, slots)
    both = jnp.stack([inputs[:, 0], cotangent[:, 0]], axis=1)
    mine = both
    if local:
        extra = [
            lax.dynamic_index_in_dim(both, chan_index ^ mask, 0, keepdims=True)
            for mask in range(1, chan_count)
        ]
        sources, moved, convs = gather_sources(master, extra, conv_params)
        place = slot_places(tile_slot, slots)
        mats = [None] * 4 + assemble(place, sources, base, tile_count - base)
        for mask in range(1, chan_count):
            mine = lax.dynamic_update_slice_in_dim(mine, moved[mask - 1], chan_index ^ mask, 0)
        near = jnp.array([0, 2, 1, 3], jnp.int32)
        position = near[jnp.arange(chan_count, dtype=jnp.int32) ^ chan_index]
    else:
        mats = gather_tiles(master.astype(bf16), tile_slot, sizes)
        mine = swap_blocks(both, "chan")
        convs = gather_small(conv_params, "chan")
        position = jnp.arange(chan_count, dtype=jnp.int32)
    source = mine[:, 0].reshape(rows, width).astype(f32)
    upstream = mine[:, 1].reshape(rows, width).astype(f32)
    convs = jnp.moveaxis(convs, 0, 1).reshape(-1, width)
    valid = lax.dynamic_slice_in_dim(lengths[:, 0], chan_index, 1)
    in_first, out_first, in_second, out_second = mats[:4]
    w_query, w_key, w_value, w_output, p_value, p_gate, p_output = mats[4:]
    gains, biases = norm_params[:5], norm_params[5:]
    taps = convs.shape[0] - 2
    margin = (taps - 1) // 2
    bn_gain, bn_bias = convs[taps], convs[taps + 1]
    frame_mask = (jnp.arange(rows, dtype=jnp.int32) < valid[0]).astype(f32)[:, None]

    def forward(stream, norm, first, w_in, w_out):
        if local:
            firsts = (first, first + quarter)
            return ffn_forward_here(
                stream, gains[norm], biases[norm], firsts, quarter, place, sources
            )
        return ffn_forward(stream, gains[norm], biases[norm], w_in, w_out)

    def send_home(value):
        value = value.astype(bf16).reshape(chan_count, seg_rows, width)
        if not local:
            return swap_blocks(value, "chan")
        here, there = swap_in_hops(value)
        return (here, exchange(there, "chan", 2))

    def backward(upstream, stream, norm, kept, first, w_in, w_out, calls):
        if local:
            firsts = (first, first + quarter)
            return ffn_backward_here(
                upstream, stream, gains[norm], kept, firsts, quarter, place, sources, calls
            )
        return ffn_backward(upstream, stream, gains[norm], kept, w_in, w_out)

    stream_one, kept_one = forward(source, 0, 0, in_first, out_first)

    stats_att = norm_stats(stream_one)
    att_in = norm_apply(stream_one, stats_att, gains[1], biases[1]).astype(bf16)
    queries = dot_rows(att_in, w_query).astype(bf16)
    keys = dot_rows(att_in, w_key).astype(bf16)
    values = dot_rows(att_in, w_value).astype(bf16)
    (merged,) = head_call(attend_kernel, valid, (queries, keys, values), 1, 4)
    stream_two = stream_one + dot_plain(merged, w_output)

    stats_conv = norm_stats(stream_two)
    conv_in = norm_apply(stream_two, stats_conv, gains[2], biases[2]).astype(bf16)
    linear = dot_rows(conv_in, p_value)
    gate_sig = jax.nn.sigmoid(dot_rows(conv_in, p_gate))
    glu = linear * gate_sig * frame_mask
    depth = jnp.zeros_like(glu)
    for t in range(taps):
        depth = depth + convs[t] * shift_rows(glu, t - margin)
    count = valid[0].astype(f32)
    local_mean = jnp.sum(depth * frame_mask, axis=0) / count
    local_gap = (depth - local_mean) * frame_mask
    local_dev = jnp.sum(local_gap * local_gap, axis=0)
    stats = (jnp.full((width,), count), local_mean, local_dev)
    mask = 1
    while mask < dp_count:
        other = exchange(jnp.stack(stats), "dp", mask)
        stats = merge_stats(stats, (other[0], other[1], other[2]))
        mask *= 2
    total_count, bn_mean, bn_dev = stats
    inv_std = lax.rsqrt(bn_dev / total_count + norm_eps)
    center = depth - bn_mean
    normal = center * inv_std * bn_gain + bn_bias
    conv_sig = jax.nn.sigmoid(normal)
    conv_act = (normal * conv_sig).astype(bf16)
    stream_three = stream_two + dot_plain(conv_act, p_output)

    stream_four, kept_four = forward(stream_three, 3, 2 * quarter, in_second, out_second)
    stats_last = norm_stats(stream_four)
    result = norm_apply(stream_four, stats_last, gains[4], biases[4]).astype(bf16)

    grad_four, gain_four, bias_four = norm_backward(stream_four, stats_last, gains[4], upstream)
    grad_three, gin_second, gout_second, gain_three, bias_three = backward(
        grad_four, stream_three, 3, kept_four, 2 * quarter, in_second, out_second, ((1, 0),)
    )

    incoming = grad_three.astype(bf16)
    incoming_three = incoming
    grad_po = None if local else weight_grad(conv_act, incoming)
    conv_slope = conv_sig * (1.0 + normal * (1.0 - conv_sig))
    grad_normal = dot_rows(incoming, p_output) * conv_slope
    own_sums = jnp.stack([jnp.sum(grad_normal, axis=0), jnp.sum(grad_normal * center, axis=0)])
    sums = butterfly_sum(own_sums, "dp")
    if local:
        block_out = send_home(result)
        sums, block_out = lax.optimization_barrier((sums, block_out))
        block_out = finish_hops(*block_out)
    else:
        block_out = send_home(result)
    sum_plain, sum_center = sums
    bn_scale = bn_gain * inv_std
    grad_depth = bn_scale * grad_normal - frame_mask * bn_scale * (
        sum_plain + inv_std * inv_std * sum_center * center
    ) / total_count
    grad_glu = jnp.zeros_like(glu)
    tap_grads = []
    for t in range(taps):
        grad_glu = grad_glu + convs[t] * shift_rows(grad_depth, margin - t)
        tap_grads.append(jnp.sum(grad_depth * shift_rows(glu, t - margin), axis=0))
    grad_glu = grad_glu * frame_mask
    grad_linear = (grad_glu * gate_sig).astype(bf16)
    grad_gating = (grad_glu * linear * gate_sig * (1.0 - gate_sig)).astype(bf16)
    if not local:
        grad_pv = weight_grad(grad_linear, conv_in)
        grad_pg = weight_grad(grad_gating, conv_in)
    back, gain_two, bias_two = norm_backward(
        stream_two,
        stats_conv,
        gains[2],
        dot_plain(grad_linear, p_value) + dot_plain(grad_gating, p_gate),
    )
    grad_two = grad_three + back

    incoming = grad_two.astype(bf16)
    grad_wo = None if local else weight_grad(merged, incoming)
    grad_merged = dot_rows(incoming, w_output).astype(bf16)
    if local:
        grad_merged, gin_second, gout_second = lax.optimization_barrier(
            (grad_merged, gin_second, gout_second)
        )
    grad_q, grad_k, grad_v = head_call(
        attend_back_kernel, valid, (queries, keys, values, grad_merged), 3, 10
    )
    if local:
        singles_other, singles_own = single_grads(
            ((0, 0), (1, 0), (2, 0), (3, 1), (4, 2), (5, 2), (6, 3)),
            (grad_q, grad_k, grad_v, merged, grad_linear, grad_gating, conv_act),
            (att_in, incoming, conv_in, incoming_three),
        )
    else:
        grad_wq = weight_grad(grad_q, att_in)
        grad_wk = weight_grad(grad_k, att_in)
        grad_wv = weight_grad(grad_v, att_in)
    back, gain_one, bias_one = norm_backward(
        stream_one,
        stats_att,
        gains[1],
        dot_plain(grad_q, w_query) + dot_plain(grad_k, w_key) + dot_plain(grad_v, w_value),
    )
    grad_one = grad_two + back
    if local:
        grad_one, singles_other = lax.optimization_barrier((grad_one, singles_other))
        singles_other = swap(singles_other, "core")

    grad_zero, gin_first, gout_first, gain_zero, bias_zero = backward(
        grad_one, source, 0, kept_one, 0, in_first, out_first, ((1,), (0,))
    )
    block_grad = send_home(grad_zero)

    conv_small = jnp.stack(tap_grads + [own_sums[1] * inv_std, own_sums[0]])
    conv_small = conv_small.reshape(-1, chan_count, rows_tile)[:, position].reshape(-1, width)
    small = jnp.concatenate(
        [
            jnp.stack(
                [gain_zero, gain_one, gain_two, gain_three, gain_four]
                + [bias_zero, bias_one, bias_two, bias_three, bias_four]
            ),
            conv_small,
        ]
    )
    if local:
        small = small + swap(small, "core")
        groups = [(i * quarter, quarter, False) for i in range(4)]
        groups.append((base, tile_count - base, True))
        pairs = [
            tuple(v.reshape(4, quarter, -1, width) for v in pair)
            for pair in (gin_first, gout_first, gin_second, gout_second)
        ]
        shape = (tile_count - base, 4) + pairs[0][0].shape[2:]
        pairs.append((singles_own.reshape(shape), singles_other.reshape(shape)))
        keep, got, small, block_grad = reduce_tiles_here(
            groups, [p[0] for p in pairs], [p[1] for p in pairs], place, slots, small, block_grad
        )
        block_grad = finish_hops(*block_grad)
        tile_m, tile_v, tile_w, tile_b = update_tiles_here(
            keep,
            got,
            owned_mask(tile_slot, slots).astype(jnp.int32),
            master,
            tile_first,
            tile_second,
        )
    else:
        grads = [gin_first, gout_first, gin_second, gout_second]
        grads += [grad_wq, grad_wk, grad_wv, grad_wo, grad_pv, grad_pg, grad_po]
        owned = reduce_tiles(
            jnp.concatenate(grads).reshape(tile_count, width, width), tile_slot, slots
        )
        small = butterfly_sum(butterfly_sum(small, "dp"), "chan")
        owned = jnp.where(owned_mask(tile_slot, slots)[:, None, None], owned, 0.0)
        tile_m, tile_v, tile_w = adamw_step(
            master, owned, tile_first, tile_second, tile_rate, weight_decay
        )
        tile_b = tile_w.astype(bf16)
    norm_total = small[: norm_params.shape[0]]
    conv_grad = lax.dynamic_slice_in_dim(
        small[norm_params.shape[0] :], chan_index * rows_tile, rows_tile, 1
    )

    norm_m, norm_v, norm_w = adamw_step(
        norm_params, norm_total, norm_first, norm_second, small_rate, 0.0
    )
    conv_m, conv_v, conv_w = adamw_step(
        conv_params, conv_grad, conv_first, conv_second, small_rate, 0.0
    )
    return (
        block_out[:, None],
        block_grad[:, None].astype(f32),
        tile_m,
        tile_v,
        tile_w,
        tile_b,
        norm_m,
        norm_v,
        norm_w,
        conv_m,
        conv_v,
        conv_w,
    )


def solution(mesh):
    in_specs = (
        P(None, "dp", "chan", None),
        P(None, "dp", "chan", None),
        P(None, "dp"),
        P(),
        P("dp", "chan", None),
        P("dp", "chan", None),
        P("dp", "chan", None),
        P(),
        P(),
        P(),
        P(None, "chan"),
        P(None, "chan"),
        P(None, "chan"),
    )
    out_specs = (
        P(None, "dp", "chan", None),
        P(None, "dp", "chan", None),
        P("dp", "chan", None),
        P("dp", "chan", None),
        P("dp", "chan", None),
        P("dp", "chan", None),
        P(),
        P(),
        P(),
        P(None, "chan"),
        P(None, "chan"),
        P(None, "chan"),
    )
    return jax.shard_map(shards, mesh=mesh, in_specs=in_specs, out_specs=out_specs, check_vma=False)
```

```python
import jax
import jax.numpy as jnp
from jax import lax
from jax.experimental import pallas as pl
from jax.experimental.pallas import tpu as pltpu
from jax.sharding import PartitionSpec as P

HEAD_DIM = 128
STEP = 10

norm_eps = 1e-05
masked_score = -1e30
beta_one = 0.9
beta_two = 0.98
adam_eps = 1e-08
tile_rate = 0.06
small_rate = 0.6
weight_decay = 0.01

BOTH = ("dp", "chan")
bf16 = jnp.bfloat16
f32 = jnp.float32


def dot_rows(left, right):
    return lax.dot_general(left, right, (((1,), (1,)), ((), ())), preferred_element_type=f32)


def dot_plain(left, right):
    return jnp.dot(left, right, preferred_element_type=f32)


def dot_cols(left, right):
    return lax.dot_general(left, right, (((0,), (0,)), ((), ())), preferred_element_type=f32)


def adamw_step(weight, gradient, first_old, second_old, rate, decay):
    first_new = beta_one * first_old + (1.0 - beta_one) * gradient
    second_new = beta_two * second_old + (1.0 - beta_two) * gradient * gradient
    first_hat = first_new / (1.0 - beta_one**STEP)
    second_hat = second_new / (1.0 - beta_two**STEP)
    weight_new = weight - rate * (first_hat / (jnp.sqrt(second_hat) + adam_eps) + decay * weight)
    return (first_new, second_new, weight_new)


def exchange(value, axis, mask):
    size = lax.axis_size(axis)
    return lax.ppermute(value, axis, [(i, i ^ mask) for i in range(size)])


def swap_blocks(value, axis):
    size = lax.axis_size(axis)
    me = lax.axis_index(axis)
    result = value
    for mask in range(1, size):
        sent = lax.dynamic_index_in_dim(value, me ^ mask, 0, keepdims=True)
        result = lax.dynamic_update_slice_in_dim(result, exchange(sent, axis, mask), me ^ mask, 0)
    return result


def swap_in_hops(value):
    me = lax.axis_index("chan")
    pairs = value.reshape((2, 2) + value.shape[1:])
    core, y = lax.rem(me, 2), lax.div(me, 2)
    keep = lax.dynamic_index_in_dim(pairs, core, 1, keepdims=False)
    sent = lax.dynamic_index_in_dim(pairs, 1 - core, 1, keepdims=False)
    got = exchange(sent, "chan", 1)
    low = jnp.where(core == 0, keep, got)
    high = jnp.where(core == 0, got, keep)
    mixed = jnp.stack([low, high], axis=1)
    there = lax.dynamic_index_in_dim(mixed, 1 - y, 0, keepdims=False)
    here = lax.dynamic_index_in_dim(mixed, y, 0, keepdims=False)
    return here, there


def finish_hops(here, arrived_there):
    y = lax.div(lax.axis_index("chan"), 2)
    low = jnp.where(y == 0, here, arrived_there)
    high = jnp.where(y == 0, arrived_there, here)
    return jnp.concatenate([low, high])


def gather_small(value, axis):
    size = lax.axis_size(axis)
    me = lax.axis_index(axis)
    result = jnp.zeros((size,) + value.shape, value.dtype)
    result = lax.dynamic_update_slice_in_dim(result, value[None], me, 0)
    for mask in range(1, size):
        result = lax.dynamic_update_slice_in_dim(
            result, exchange(value[None], axis, mask), me ^ mask, 0
        )
    return result


def butterfly_sum(value, axis):
    size = lax.axis_size(axis)
    mask = 1
    while mask < size:
        value = value + exchange(value, axis, mask)
        mask *= 2
    return value


BITS = {"core": 1, "y": 2, "x": 4, "z1": 8, "z2": 16}
ORDERS = (
    ("z2", "y", "z1", "x"),
    ("z1", "z2", "y", "x"),
    ("z2", "y", "x", "z1"),
    ("z1", "x", "y", "z2"),
    ("z2", "z1", "x", "y"),
    ("z1", "x", "z2", "y"),
)
LAST = (("x", (0, 1)), ("z1", (2,)), ("z2", (3,)), ("y", (4, 5)))
HALVES = 2


def is_slice(dp_count, chan_count, slots):
    return (dp_count, chan_count, slots) == (8, 4, 3)


def swap(value, name):
    size = lax.axis_size("dp") * lax.axis_size("chan")
    return lax.ppermute(value, BOTH, [(i, i ^ BITS[name]) for i in range(size)])


def step_groups(step, orders):
    groups = {}
    for part, order in enumerate(orders):
        groups.setdefault(order[step], []).append(part)
    return groups


def gather_parts(master, extra, small):
    half = master.shape[1] // HALVES
    own = [master[:, h * half : (h + 1) * half].astype(bf16) for h in range(HALVES)]
    own = lax.optimization_barrier(own)
    state = [own[p % HALVES][p // HALVES][None] for p in range(6)]
    moved = []
    for step in range(4):
        groups = step_groups(step, ORDERS)
        sent = {
            name: (jnp.concatenate([state[p] for p in parts]) if len(parts) > 1 else state[parts[0]])
            for name, parts in groups.items()
        }
        if step == 0:
            sent = {ORDERS[h][0]: own[h] for h in range(HALVES)}
            sent, extra = lax.optimization_barrier((sent, extra))
            moved = [exchange(value, "chan", mask + 1) for mask, value in enumerate(extra)]
        elif step == 1:
            sent, small = lax.optimization_barrier((sent, small))
            small = jnp.stack([small, exchange(small, "chan", 2)])
        elif step == 2:
            sent, small = lax.optimization_barrier((sent, small))
            small = jnp.concatenate([small, exchange(small, "chan", 1)])
        else:
            sent = lax.optimization_barrier(sent)
        got = {name: swap(value, name) for name, value in sent.items()}
        if step == 3:
            return ([sent[n] for n, _ in LAST], [got[n] for n, _ in LAST], moved, small)
        got, moved, small = lax.optimization_barrier((got, moved, small))
        size = 1 << step
        for name, parts in groups.items():
            for i, p in enumerate(parts):
                state[p] = jnp.concatenate([state[p], got[name][i * size : (i + 1) * size]])


def place_of(part, bits):
    order = ORDERS[part]
    index = bits[order[2]] * 4 + bits[order[1]] * 2 + bits[order[0]]
    for _, parts in LAST:
        if part in parts:
            return (bits[order[3]], index + 8 * parts.index(part))


def array_of(position, h):
    part = position * HALVES + h
    return [i for i, (_, parts) in enumerate(LAST) if part in parts][0]


def slot_places(slot, slots):
    owner, position = slot // slots, slot % slots
    gap = owner ^ lax.axis_index("dp")
    bits = {"x": gap & 1, "z1": (gap >> 1) & 1, "z2": (gap >> 2) & 1}
    rows = []
    for dy in range(2):
        for h in range(HALVES):
            codes = []
            for s in range(slots):
                far, index = place_of(s * HALVES + h, dict(bits, y=jnp.full_like(gap, dy)))
                codes.append((far * 4 + array_of(s, h)) * 16 + index)
            rows.append(jnp.select([position == s for s in range(slots)], codes))
    return jnp.stack(rows).astype(jnp.int32)


def at_place(place, arrays, act):
    which, index = lax.div(place, 16), lax.rem(place, 16)
    for i, array in enumerate(arrays):

        @pl.when(which == i)
        def _():
            act(array, index)


def staged(count, depth, load, drain_in, store, drain_out):
    ahead = depth // 2
    for i in range(count + ahead):
        if i < count:
            if i >= depth:
                drain_out(i - depth)
            load(i)
        if i >= ahead:
            drain_in(i - ahead)
            store(i - ahead)
    for i in range(max(count - depth, 0), count):
        drain_out(i)


DEPTH = 8


SOURCES = 13


def sixteen(refs):
    near, at = [], 0
    for _, parts in LAST:
        near.append(refs[8].at[pl.ds(at, 8 * len(parts))])
        at += 8 * len(parts)
    return list(refs[:8]) + near + list(refs[9:SOURCES])


def assemble_kernel(first, place_ref, *refs):
    sources, outs = sixteen(refs), refs[SOURCES:-3]
    buffer, in_sem, out_sem = refs[-3:]
    items = [(core, g) for core in range(2) for g in range(len(outs))]

    def load(i):
        core, g = items[i]
        for b in range(4):
            at_place(
                place_ref[b, first + g],
                sources[core * 8 : core * 8 + 8],
                lambda array, index: pltpu.make_async_copy(
                    array.at[index], buffer.at[i % DEPTH, b], in_sem.at[i % DEPTH]
                ).start(),
            )

    def drain_in(i):
        slot = buffer.at[i % DEPTH]
        pltpu.make_async_copy(slot, slot, in_sem.at[i % DEPTH]).wait()

    def out_copy(i):
        core, g = items[i]
        return pltpu.make_async_copy(buffer.at[i % DEPTH], outs[g].at[core], out_sem.at[i % DEPTH])

    staged(
        len(items), DEPTH, load, drain_in, lambda i: out_copy(i).start(), lambda i: out_copy(i).wait()
    )


ANYWHERE = pl.BlockSpec(memory_space=pl.ANY)
IN_SMEM = pl.BlockSpec(memory_space=pltpu.SMEM)
IN_VMEM = pl.BlockSpec(memory_space=pltpu.VMEM)


def assemble(place, sources, first, count):
    rows, width = sources[0].shape[1:]
    mats = pl.pallas_call(
        lambda *refs: assemble_kernel(first, *refs),
        in_specs=[IN_SMEM] + [ANYWHERE] * SOURCES,
        out_specs=[ANYWHERE] * count,
        out_shape=[jax.ShapeDtypeStruct((2, 4, rows, width), bf16)] * count,
        scratch_shapes=[
            pltpu.VMEM((DEPTH, 4, rows, width), bf16),
            pltpu.SemaphoreType.DMA((DEPTH,)),
            pltpu.SemaphoreType.DMA((DEPTH,)),
        ],
        compiler_params=pltpu.CompilerParams(vmem_limit_bytes=32 * 1024 * 1024),
        cost_estimate=pl.CostEstimate(
            flops=0, bytes_accessed=count * 32 * rows * width, transcendentals=0
        ),
    )(place, *sources)
    return [m.reshape(-1, width) for m in mats]


def gather_sources(master, extra, small):
    near, far, moved, small = gather_parts(master, extra, small)
    near_other = swap(jnp.concatenate(near), "core")
    far_other = [swap(v, "core") for v in far]
    return near + far + [near_other] + far_other, moved, small


BPS = 2
STEPS = 4 // BPS


def fetch_rows(at, item, firsts, count, place_ref, sources, buffers, sems):
    core, step = item
    rows = sources[0].shape[1]
    for m, first in enumerate(firsts):
        for i in range(BPS):
            for j in range(count):
                at_place(
                    place_ref[step * BPS + i, first + j],
                    sources[core * 8 : core * 8 + 8],
                    lambda array, index: pltpu.make_async_copy(
                        array.at[index],
                        buffers[m].at[at, pl.ds((i * count + j) * rows, rows)],
                        sems.at[m, at],
                    ).start(),
                )


def arrived(m, at, buffers, sems):
    pltpu.make_async_copy(buffers[m].at[at], buffers[m].at[at], sems.at[m, at]).wait()
    return buffers[m][at]


def tail_next(out_ref, ins, outs):
    gain_ref, bias_ref = ins
    next_ref, stats_ref = outs
    lanes = stats_ref.shape[1] // 2
    for r in range(4):
        rows = pl.ds(r * (out_ref.shape[0] // 4), out_ref.shape[0] // 4)
        stream = out_ref[rows, :]
        mean, inv = norm_stats(stream)
        next_ref[rows, :] = norm_apply(
            stream, (mean, inv), gain_ref[...], bias_ref[...]
        ).astype(bf16)
        stats_ref[rows, :lanes] = jnp.broadcast_to(mean, (stream.shape[0], lanes))
        stats_ref[rows, lanes:] = jnp.broadcast_to(inv, (stream.shape[0], lanes))


def tail_last(out_ref, ins, outs):
    gain_ref, bias_ref, up_ref = ins
    result_ref, grad_ref, half_ref, sums_ref = outs
    for r in range(4):
        rows = pl.ds(r * (out_ref.shape[0] // 4), out_ref.shape[0] // 4)
        stream, upstream = out_ref[rows, :], up_ref[rows, :].astype(f32)
        stats = norm_stats(stream)
        result_ref[rows, :] = norm_apply(stream, stats, gain_ref[...], bias_ref[...]).astype(bf16)
        back, grad_gain, grad_bias = norm_backward(stream, stats, gain_ref[...], upstream)
        grad_ref[rows, :] = back
        half_ref[rows, :] = (0.5 * back).astype(bf16)
        sums = jnp.concatenate([grad_gain[None], grad_bias[None]])
        sums_ref[...] = sums if r == 0 else sums_ref[...] + sums


def ffn_kernel(firsts, count, tail, tail_ins, place_ref, normed_ref, base_ref, *refs):
    ins, refs = refs[:tail_ins], refs[tail_ins:]
    sources = sixteen(refs)
    out_ref, act_ref, slope_ref = refs[SOURCES : SOURCES + 3]
    outs, (in_buf, out_buf, sems) = refs[SOURCES + 3 : -3], refs[-3:]
    buffers = (in_buf, out_buf)
    size = in_buf.shape[1]
    items = [(core, q) for core in range(2) for q in range(STEPS)]
    for i in range(2):
        fetch_rows(i, items[i], firsts, count, place_ref, sources, buffers, sems)
    for i, (core, q) in enumerate(items):
        cut = slice(i * size, (i + 1) * size)
        hidden = dot_rows(normed_ref[...], arrived(0, i % 2, buffers, sems))
        sig = jax.nn.sigmoid(hidden)
        active = (hidden * sig).astype(bf16)
        act_ref[:, cut] = active
        slope_ref[:, cut] = (sig * (1.0 + hidden * (1.0 - sig))).astype(bf16)
        before = base_ref[...] if i == 0 else out_ref[...]
        out_ref[...] = before + 0.5 * dot_plain(active, arrived(1, i % 2, buffers, sems))
        if i + 2 < len(items):
            fetch_rows(i % 2, items[i + 2], firsts, count, place_ref, sources, buffers, sems)
    tail(out_ref, ins, outs)


def ffn_back_kernel(cores, based, firsts, count, place_ref, e_ref, act_ref, slope_ref, normed_ref, *refs):
    base_ref, refs = (refs[0], refs[1:]) if based else (None, refs)
    sources, refs = sixteen(refs), refs[SOURCES:]
    dx_ref, grads, refs = refs[0], refs[1 : 1 + 2 * len(cores)], refs[1 + 2 * len(cores) :]
    in_grads, out_grads, put_sems, in_buf, out_buf, sems = refs
    buffers = (in_buf, out_buf)
    size = in_buf.shape[1]
    items = [(core, q) for core in cores for q in range(STEPS)]
    for i in range(2):
        fetch_rows(i, items[i], firsts, count, place_ref, sources, buffers, sems)

    def copy(m, i):
        core, q = items[i]
        target = grads[2 * cores.index(core) + m].at[pl.ds(q * size, size)]
        buffer = (in_grads, out_grads)[m]
        return pltpu.make_async_copy(buffer.at[i % 2], target, put_sems.at[m, i % 2])

    for i, (core, q) in enumerate(items):
        cut = slice((core * STEPS + q) * size, (core * STEPS + q + 1) * size)
        incoming = e_ref[...]
        grad = dot_rows(incoming, arrived(1, i % 2, buffers, sems)) * slope_ref[:, cut].astype(f32)
        grad = grad.astype(bf16)
        change = dot_plain(grad, arrived(0, i % 2, buffers, sems))
        if i + 2 < len(items):
            fetch_rows(i % 2, items[i + 2], firsts, count, place_ref, sources, buffers, sems)
        if i > 0:
            dx_ref[...] += change
        elif based:
            dx_ref[...] = base_ref[...] + change
        else:
            dx_ref[...] = change
        if i >= 2:
            copy(1, i - 2).wait()
        out_grads[i % 2] = dot_cols(act_ref[:, cut], incoming).astype(bf16)
        copy(1, i).start()
        if i >= 2:
            copy(0, i - 2).wait()
        in_grads[i % 2] = dot_cols(grad, normed_ref[...]).astype(bf16)
        copy(0, i).start()
    for i in range(len(items) - 2, len(items)):
        for m in range(2):
            copy(m, i).wait()


def grads_kernel(pairs, lefts, rights, *refs):
    left_refs, right_refs = refs[:lefts], refs[lefts : lefts + rights]
    other, own, buffer, sems = refs[lefts + rights :]
    half = own.shape[1]
    for k, (i, j) in enumerate(pairs):
        slot = k % 2
        if k >= 2:
            pltpu.make_async_copy(buffer.at[slot], buffer.at[slot], sems.at[slot]).wait()
        buffer[slot] = dot_cols(left_refs[i][...], right_refs[j][...]).astype(bf16)
        pltpu.make_async_copy(buffer.at[slot, pl.ds(0, half)], own.at[k], sems.at[slot]).start()
        pltpu.make_async_copy(buffer.at[slot, pl.ds(half, half)], other.at[k], sems.at[slot]).start()
    for slot in range(2):
        pltpu.make_async_copy(buffer.at[slot], buffer.at[slot], sems.at[slot]).wait()


def single_grads(pairs, lefts, rights):
    rows, width = lefts[0].shape
    shape = jax.ShapeDtypeStruct((len(pairs), width // 2, width), bf16)
    return pl.pallas_call(
        lambda *refs: grads_kernel(pairs, len(lefts), len(rights), *refs),
        in_specs=[IN_VMEM] * (len(lefts) + len(rights)),
        out_specs=[ANYWHERE] * 2,
        out_shape=[shape] * 2,
        scratch_shapes=[pltpu.VMEM((2, width, width), bf16), pltpu.SemaphoreType.DMA((2,))],
        compiler_params=pltpu.CompilerParams(vmem_limit_bytes=32 * 1024 * 1024),
        cost_estimate=pl.CostEstimate(
            flops=2 * len(pairs) * rows * width * width,
            bytes_accessed=2 * len(pairs) * width * (width + 2 * rows),
            transcendentals=0,
        ),
    )(*lefts, *rights)


def ffn_scratch(count, rows, width):
    return [
        pltpu.VMEM((2, BPS * count * rows, width), bf16),
        pltpu.VMEM((2, BPS * count * rows, width), bf16),
        pltpu.SemaphoreType.DMA((2, 2)),
    ]


LANES = 128


def ffn_forward_here(stream, gain, bias, firsts, count, place, sources, tail, tail_ins):
    rows, width = stream.shape
    block = sources[0].shape[1]
    hidden = 8 * count * block
    shape = jax.ShapeDtypeStruct
    stats = norm_stats(stream)
    normed = norm_apply(stream, stats, gain, bias).astype(bf16)
    if tail is tail_next:
        more = [shape((rows, width), bf16), shape((rows, 2 * LANES), f32)]
    else:
        more = [
            shape((rows, width), bf16),
            shape((rows, width), f32),
            shape((rows, width), bf16),
            shape((2, width), f32),
        ]
    result, active, slope, *more = pl.pallas_call(
        lambda *refs: ffn_kernel(firsts, count, tail, len(tail_ins), *refs),
        in_specs=[IN_SMEM] + [IN_VMEM] * (2 + len(tail_ins)) + [ANYWHERE] * SOURCES,
        out_specs=[IN_VMEM] * (3 + len(more)),
        out_shape=[
            shape((rows, width), f32),
            shape((rows, hidden), bf16),
            shape((rows, hidden), bf16),
        ]
        + more,
        scratch_shapes=ffn_scratch(count, block, width),
        compiler_params=pltpu.CompilerParams(vmem_limit_bytes=FORWARD_MB * 1024 * 1024),
        cost_estimate=pl.CostEstimate(
            flops=4 * rows * width * hidden,
            bytes_accessed=4 * hidden * (width + rows),
            transcendentals=rows * hidden,
        ),
    )(place, normed, stream, *tail_ins, *sources)
    return (result, (stats, normed, active, slope), more)


FORWARD_MB = 36
BACKWARD_MB = 40


def ffn_backward_here(
    upstream, incoming, stream, gain, kept, firsts, count, place, sources, calls
):
    stats, normed, active, slope = kept
    rows, width = stream.shape
    block = sources[0].shape[1]
    half = 4 * count * block
    size = BPS * count * block
    shape = jax.ShapeDtypeStruct
    base, grads = [], []
    for cores in calls:
        dx, *some = pl.pallas_call(
            lambda *refs, cores=cores: ffn_back_kernel(cores, bool(base), firsts, count, *refs),
            in_specs=[IN_SMEM] + [IN_VMEM] * (4 + len(base)) + [ANYWHERE] * SOURCES,
            out_specs=[IN_VMEM] + [ANYWHERE] * (2 * len(cores)),
            out_shape=[shape((rows, width), f32)]
            + [shape((half, width), bf16)] * (2 * len(cores)),
            scratch_shapes=[
                pltpu.VMEM((2, size, width), bf16),
                pltpu.VMEM((2, size, width), bf16),
                pltpu.SemaphoreType.DMA((2, 2)),
            ]
            + ffn_scratch(count, block, width),
            compiler_params=pltpu.CompilerParams(vmem_limit_bytes=BACKWARD_MB * 1024 * 1024),
            cost_estimate=pl.CostEstimate(
                flops=8 * rows * width * half * len(cores),
                bytes_accessed=8 * half * (width + rows) * len(cores),
                transcendentals=0,
            ),
        )(place, incoming, active, slope, normed, *base, *sources)
        base = [dx]
        if not grads:
            some = [swap(v, "core") for v in some[:2]] + some[2:]
        grads += some
    other_in, other_out, own_in, own_out = grads
    back, grad_gain, grad_bias = norm_backward(stream, stats, gain, dx)
    return (upstream + back, (own_in, other_in), (own_out, other_out), grad_gain, grad_bias)


SCATTER = 6


def scatter_kernel(groups, place_ref, *refs):
    owns, others = refs[: len(groups)], refs[len(groups) : 2 * len(groups)]
    outs = refs[2 * len(groups) : 2 * len(groups) + 8]
    own_buf, other_buf, in_sem, out_sem = refs[2 * len(groups) + 8 :]
    items = []
    for g, (first, count, whole) in enumerate(groups):
        if whole:
            items += [(g, k, [(b, first + k) for b in range(4)]) for k in range(count)]
        else:
            items += [(g, b, [(b, first + j) for j in range(count)]) for b in range(4)]

    def in_copies(i):
        g, k, _ = items[i]
        slot = i % SCATTER
        return (
            pltpu.make_async_copy(owns[g].at[k], own_buf.at[slot], in_sem.at[0, slot]),
            pltpu.make_async_copy(others[g].at[k], other_buf.at[slot], in_sem.at[1, slot]),
        )

    def load(i):
        for copy in in_copies(i):
            copy.start()

    def drain_in(i):
        for copy in in_copies(i):
            copy.wait()

    def store(i):
        slot = i % SCATTER
        own_buf[slot] = (own_buf[slot].astype(f32) + other_buf[slot].astype(f32)).astype(bf16)
        for at, (b, tile) in enumerate(items[i][2]):
            at_place(
                place_ref[b, tile],
                outs,
                lambda array, index: pltpu.make_async_copy(
                    own_buf.at[slot, at], array.at[index], out_sem.at[slot]
                ).start(),
            )

    def drain_out(i):
        slot = own_buf.at[i % SCATTER]
        pltpu.make_async_copy(slot, slot, out_sem.at[i % SCATTER]).wait()

    staged(len(items), SCATTER, load, drain_in, store, drain_out)


def combine_kernel(plan, count, *refs):
    keeps, gots, outs = refs[:count], refs[count : 2 * count], refs[2 * count :]
    rows = 16

    def body(r, carry):
        cut = pl.ds(pl.multiple_of(r * rows, rows), rows)
        for out, at, array, index in plan:
            total = keeps[array][index, cut, :].astype(f32) + gots[array][index, cut, :].astype(f32)
            outs[out][at, cut, :] = total.astype(bf16)
        return carry

    lax.fori_loop(0, keeps[0].shape[1] // rows, body, 0)


def combine(step, keep, got):
    before, now = step_groups(step + 1, ORDERS), step_groups(step, ORDERS)
    size = 1 << step
    lies = {
        p: (a, 2 * i * size)
        for a, parts in enumerate(before.values())
        for i, p in enumerate(parts)
    }
    plan, shapes = [], []
    for half in (1, 0):
        for parts in now.values():
            for i, p in enumerate(parts):
                array, first = lies[p]
                plan += [
                    (len(shapes), i * size + k, array, first + half * size + k)
                    for k in range(size)
                ]
            some = next(iter(keep.values()))
            shapes.append(jax.ShapeDtypeStruct((size * len(parts),) + some.shape[1:], bf16))
    blocks = sum(s.shape[0] for s in shapes)
    outs = pl.pallas_call(
        lambda *refs: combine_kernel(plan, len(before), *refs),
        in_specs=[IN_VMEM] * (2 * len(before)),
        out_specs=[IN_VMEM] * len(shapes),
        out_shape=shapes,
        compiler_params=pltpu.CompilerParams(
            vmem_limit_bytes=(3 * blocks * 2 * some.shape[1] * some.shape[2]) + (4 << 20)
        ),
        cost_estimate=pl.CostEstimate(
            flops=blocks * some.shape[1] * some.shape[2],
            bytes_accessed=6 * blocks * some.shape[1] * some.shape[2],
            transcendentals=0,
        ),
    )(*[keep[n] for n in before], *[got[n] for n in before])
    return dict(zip(now, outs[: len(now)])), dict(zip(now, outs[len(now) :]))


def reduce_tiles_here(groups, owns, others, place, slots, small, ahead):
    rows, width = owns[0].shape[2:]
    shapes = [jax.ShapeDtypeStruct((8 * len(parts), rows, width), bf16) for _, parts in LAST]
    arrays = pl.pallas_call(
        lambda *refs: scatter_kernel(groups, *refs),
        in_specs=[IN_SMEM] + [ANYWHERE] * (2 * len(groups)),
        out_specs=[ANYWHERE] * 8,
        out_shape=shapes + shapes,
        scratch_shapes=[
            pltpu.VMEM((SCATTER, 4, rows, width), bf16),
            pltpu.VMEM((SCATTER, 4, rows, width), bf16),
            pltpu.SemaphoreType.DMA((2, SCATTER)),
            pltpu.SemaphoreType.DMA((SCATTER,)),
        ],
        compiler_params=pltpu.CompilerParams(vmem_limit_bytes=32 * 1024 * 1024),
        cost_estimate=pl.CostEstimate(
            flops=0, bytes_accessed=6 * 92 * rows * width, transcendentals=0
        ),
    )(place, *owns, *others)
    arrays, ahead = lax.optimization_barrier((arrays, ahead))
    keep = {n: a for (n, _), a in zip(LAST, arrays[:4])}
    send = {n: a for (n, _), a in zip(LAST, arrays[4:])}
    for step in range(3, -1, -1):
        if step == 2:
            size = 1 << step
            state = {}
            for name, parts in step_groups(step + 1, ORDERS).items():
                for i, p in enumerate(parts):
                    cut = slice(2 * i * size, 2 * (i + 1) * size)
                    state[p] = keep[name][cut].astype(f32) + got[name][cut].astype(f32)
            halves = []
            for cut in (slice(size, None), slice(0, size)):
                halves.append(
                    {
                        name: jnp.concatenate([state[p][cut] for p in parts]).astype(bf16)
                        for name, parts in step_groups(step, ORDERS).items()
                    }
                )
            send, keep = halves
        elif step < 2:
            send, keep = combine(step, keep, got)
        send, small = lax.optimization_barrier((send, small))
        got = {name: swap(value, name) for name, value in send.items()}
        small = small + swap(small, ("z2", "z1", "x", "y")[step])
        got, small = lax.optimization_barrier((got, small))
    order = step_groups(0, ORDERS)
    return [keep[n] for n in order], [got[n] for n in order], small, ahead


def update_kernel(filled_ref, k0, g0, k1, g1, w_ref, m_ref, v_ref, m_new, v_new, w_new, b_new):
    half = pl.program_id(1)
    first = k0[...].astype(f32) + g0[...].astype(f32)
    second = k1[...].astype(f32) + g1[...].astype(f32)
    gradient = jnp.where(half == 0, first, second)
    gradient = jnp.where(filled_ref[pl.program_id(0)] > 0, gradient, 0.0)
    moment, square, weight = adamw_step(
        w_ref[...], gradient, m_ref[...], v_ref[...], tile_rate, weight_decay
    )
    m_new[...], v_new[...], w_new[...] = moment, square, weight
    b_new[...] = weight.astype(bf16)


def update_tiles_here(keep, got, filled, master, tile_first, tile_second):
    slots, full, width = master.shape
    rows = full // HALVES
    part = pl.BlockSpec((1, rows, width), lambda s, h: (s, 0, 0))
    here = pl.BlockSpec((1, rows, width), lambda s, h: (s, h, 0))
    shape = jax.ShapeDtypeStruct(master.shape, f32)
    return pl.pallas_call(
        update_kernel,
        grid=(slots, HALVES),
        in_specs=[IN_SMEM] + [part] * 4 + [here] * 3,
        out_specs=[here] * 4,
        out_shape=[shape] * 3 + [jax.ShapeDtypeStruct(master.shape, bf16)],
        compiler_params=pltpu.CompilerParams(vmem_limit_bytes=32 * 1024 * 1024),
        cost_estimate=pl.CostEstimate(
            flops=20 * slots * full * width,
            bytes_accessed=30 * slots * full * width,
            transcendentals=slots * full * width,
        ),
    )(filled, keep[0], got[0], keep[1], got[1], master, tile_first, tile_second)


def owned_mask(tile_slot, slots):
    slot = lax.axis_index("dp") * slots + jnp.arange(slots, dtype=jnp.int32)
    return jnp.any(slot[:, None] == tile_slot[None, :], axis=1)


def gather_tiles(own, tile_slot, sizes):
    width = own.shape[2]
    strips = lax.all_gather(own, "dp", axis=0, tiled=True)
    strips = strips.at[tile_slot].get(mode="promise_in_bounds")
    whole = lax.all_gather(strips, "chan", axis=1, tiled=True)
    mats, first = [], 0
    for n in sizes:
        mats.append(whole[first : first + n].reshape(-1, width))
        first += n
    return mats


def reduce_tiles(grads, tile_slot, slots):
    slot = jnp.arange(lax.axis_size("dp") * slots, dtype=jnp.int32)
    tile_of = jnp.argmax(slot[:, None] == tile_slot[None, :], axis=1).astype(jnp.int32)
    strips = lax.psum_scatter(grads, "chan", scatter_dimension=1, tiled=True)
    placed = strips.at[tile_of].get(mode="promise_in_bounds")
    return lax.psum_scatter(placed, "dp", scatter_dimension=0, tiled=True).astype(f32)


def norm_stats(stream):
    mean = jnp.mean(stream, axis=-1, keepdims=True)
    center = stream - mean
    spread = jnp.mean(center * center, axis=-1, keepdims=True)
    return (mean, lax.rsqrt(spread + norm_eps))


def norm_apply(stream, stats, gain, bias):
    mean, inv = stats
    return (stream - mean) * inv * gain + bias


def norm_backward(stream, stats, gain, upstream):
    mean, inv = stats
    hat = (stream - mean) * inv
    scaled = upstream * gain
    back = (
        scaled
        - jnp.mean(scaled, axis=-1, keepdims=True)
        - hat * jnp.mean(scaled * hat, axis=-1, keepdims=True)
    ) * inv
    return (back, jnp.sum(upstream * hat, axis=0), jnp.sum(upstream, axis=0))


def masked_probs(query, key, valid):
    scores = dot_rows(query, key) * HEAD_DIM ** (-0.5)
    column = lax.broadcasted_iota(jnp.int32, (1, scores.shape[1]), 1)
    scores = jnp.where(column < valid, scores, masked_score)
    exponent = jnp.exp(scores - jnp.max(scores, axis=-1, keepdims=True))
    return exponent, 1.0 / jnp.sum(exponent, axis=-1, keepdims=True)


TOGETHER = 4


def attend_kernel(valid_ref, q_ref, k_ref, v_ref, out_ref):
    for i in range(TOGETHER):
        cut = slice(i * HEAD_DIM, (i + 1) * HEAD_DIM)
        exponent, inverse = masked_probs(q_ref[:, cut], k_ref[:, cut], valid_ref[0])
        probs = (exponent * inverse).astype(bf16)
        out_ref[:, cut] = dot_plain(probs, v_ref[:, cut]).astype(bf16)


def attend_back_kernel(valid_ref, q_ref, k_ref, v_ref, g_ref, dq_ref, dk_ref, dv_ref):
    scale = HEAD_DIM ** (-0.5)
    for i in range(TOGETHER):
        cut = slice(i * HEAD_DIM, (i + 1) * HEAD_DIM)
        query, key, grad = q_ref[:, cut], k_ref[:, cut], g_ref[:, cut]
        exponent, inverse = masked_probs(query, key, valid_ref[0])
        probs = exponent * inverse
        grad_probs = dot_rows(grad, v_ref[:, cut])
        row_dot = jnp.sum(probs * grad_probs, axis=-1, keepdims=True)
        grad_scores = (probs * (grad_probs - row_dot)).astype(bf16)
        dq_ref[:, cut] = (dot_plain(grad_scores, key) * scale).astype(bf16)
        dk_ref[:, cut] = (dot_cols(grad_scores, query) * scale).astype(bf16)
        dv_ref[:, cut] = dot_cols(probs.astype(bf16), grad).astype(bf16)


def head_call(kernel, valid, operands, out_count, flops):
    rows, width = operands[0].shape
    spec = pl.BlockSpec((rows, TOGETHER * HEAD_DIM), lambda h: (0, h))
    shape = jax.ShapeDtypeStruct((rows, width), bf16)
    return pl.pallas_call(
        kernel,
        grid=(width // HEAD_DIM // TOGETHER,),
        in_specs=[IN_SMEM] + [spec] * len(operands),
        out_specs=[spec] * out_count,
        out_shape=[shape] * out_count,
        cost_estimate=pl.CostEstimate(
            flops=flops * rows * rows * width,
            bytes_accessed=2 * rows * width * (len(operands) + out_count),
            transcendentals=rows * rows * width // HEAD_DIM,
        ),
        compiler_params=pltpu.CompilerParams(vmem_limit_bytes=32 * 1024 * 1024),
    )(valid, *operands)


def ffn_forward(stream, gain, bias, w_in, w_out):
    stats = norm_stats(stream)
    normed = norm_apply(stream, stats, gain, bias).astype(bf16)
    hidden = dot_rows(normed, w_in)
    sig = jax.nn.sigmoid(hidden)
    active = (hidden * sig).astype(bf16)
    slope = (sig * (1.0 + hidden * (1.0 - sig))).astype(bf16)
    return (stream + 0.5 * dot_plain(active, w_out), (stats, normed, active, slope))


def weight_grad(left, right):
    return dot_cols(left, right).astype(bf16)


def ffn_backward(upstream, stream, gain, kept, w_in, w_out):
    stats, normed, active, slope = kept
    incoming = (0.5 * upstream).astype(bf16)
    grad_out = weight_grad(active, incoming)
    grad_hidden = (dot_rows(incoming, w_out) * slope.astype(f32)).astype(bf16)
    grad_in = weight_grad(grad_hidden, normed)
    back, grad_gain, grad_bias = norm_backward(stream, stats, gain, dot_plain(grad_hidden, w_in))
    return (upstream + back, grad_in, grad_out, grad_gain, grad_bias)


def shift_rows(value, offset):
    rows = value.shape[0]
    if offset == 0:
        return value
    if offset > 0:
        return jnp.pad(value[offset:], ((0, offset), (0, 0)))
    return jnp.pad(value[: rows + offset], ((-offset, 0), (0, 0)))


def merge_stats(one, two):
    count_a, mean_a, dev_a = one
    count_b, mean_b, dev_b = two
    count = count_a + count_b
    mean = (count_a * mean_a + count_b * mean_b) / count
    gap = mean_a - mean_b
    return (count, mean, dev_a + dev_b + gap * gap * (count_a * count_b / count))


def shards(
    inputs,
    cotangent,
    lengths,
    tile_slot,
    master,
    tile_first,
    tile_second,
    norm_params,
    norm_first,
    norm_second,
    conv_params,
    conv_first,
    conv_second,
):
    micro, _, seg_rows, width = inputs.shape
    slots, rows_tile, _ = master.shape
    chan_count, dp_count = lax.axis_size("chan"), lax.axis_size("dp")
    chan_index = lax.axis_index("chan")
    assert micro == chan_count
    rows = seg_rows * chan_count
    tile_count = tile_slot.shape[0]
    quarter = (tile_count - 7) // 4
    base = 4 * quarter

    sizes = (quarter,) * 4 + (1,) * 7
    local = is_slice(dp_count, chan_count, slots)
    both = jnp.stack([inputs[:, 0], cotangent[:, 0]], axis=1)
    mine = both
    if local:
        extra = [
            lax.dynamic_index_in_dim(both, chan_index ^ mask, 0, keepdims=True)
            for mask in range(1, chan_count)
        ]
        sources, moved, convs = gather_sources(master, extra, conv_params)
        place = slot_places(tile_slot, slots)
        mats = [None] * tile_count
        for mask in range(1, chan_count):
            mine = lax.dynamic_update_slice_in_dim(mine, moved[mask - 1], chan_index ^ mask, 0)
        near = jnp.array([0, 2, 1, 3], jnp.int32)
        position = near[jnp.arange(chan_count, dtype=jnp.int32) ^ chan_index]
    else:
        mats = gather_tiles(master.astype(bf16), tile_slot, sizes)
        mine = swap_blocks(both, "chan")
        convs = gather_small(conv_params, "chan")
        position = jnp.arange(chan_count, dtype=jnp.int32)
    source = mine[:, 0].reshape(rows, width).astype(f32)
    cotangent_rows = mine[:, 1].reshape(rows, width)
    convs = jnp.moveaxis(convs, 0, 1).reshape(-1, width)
    valid = lax.dynamic_slice_in_dim(lengths[:, 0], chan_index, 1)
    in_first, out_first, in_second, out_second = mats[:4]
    gains, biases = norm_params[:5], norm_params[5:]
    taps = convs.shape[0] - 2
    margin = (taps - 1) // 2
    bn_gain, bn_bias = convs[taps], convs[taps + 1]
    frame_mask = (jnp.arange(rows, dtype=jnp.int32) < valid[0]).astype(f32)[:, None]

    def send_home(value):
        value = value.astype(bf16).reshape(chan_count, seg_rows, width)
        if not local:
            return swap_blocks(value, "chan")
        here, there = swap_in_hops(value)
        return (here, exchange(there, "chan", 2))

    if local:
        stream_one, kept_one, (att_in, stats_att) = ffn_forward_here(
            source,
            gains[0],
            biases[0],
            (0, quarter),
            quarter,
            place,
            sources,
            tail_next,
            (gains[1:2], biases[1:2]),
        )
        stats_att = (stats_att[:, :1], stats_att[:, LANES : LANES + 1])
        stream_one, place_after = lax.optimization_barrier((stream_one, place))
        mats[4:] = assemble(place_after, sources, base, tile_count - base)
    else:
        stream_one, kept_one = ffn_forward(source, gains[0], biases[0], in_first, out_first)
        stats_att = norm_stats(stream_one)
        att_in = norm_apply(stream_one, stats_att, gains[1], biases[1]).astype(bf16)
    w_query, w_key, w_value, w_output, p_value, p_gate, p_output = mats[4:]
    queries = dot_rows(att_in, w_query).astype(bf16)
    keys = dot_rows(att_in, w_key).astype(bf16)
    values = dot_rows(att_in, w_value).astype(bf16)
    (merged,) = head_call(attend_kernel, valid, (queries, keys, values), 1, 4)
    stream_two = stream_one + dot_plain(merged, w_output)

    stats_conv = norm_stats(stream_two)
    conv_in = norm_apply(stream_two, stats_conv, gains[2], biases[2]).astype(bf16)
    linear = dot_rows(conv_in, p_value)
    gate_sig = jax.nn.sigmoid(dot_rows(conv_in, p_gate))
    glu = linear * gate_sig * frame_mask
    depth = jnp.zeros_like(glu)
    for t in range(taps):
        depth = depth + convs[t] * shift_rows(glu, t - margin)
    count = valid[0].astype(f32)
    local_mean = jnp.sum(depth * frame_mask, axis=0) / count
    local_gap = (depth - local_mean) * frame_mask
    local_dev = jnp.sum(local_gap * local_gap, axis=0)
    stats = (jnp.full((width,), count), local_mean, local_dev)
    mask = 1
    while mask < dp_count:
        other = exchange(jnp.stack(stats), "dp", mask)
        stats = merge_stats(stats, (other[0], other[1], other[2]))
        mask *= 2
    total_count, bn_mean, bn_dev = stats
    inv_std = lax.rsqrt(bn_dev / total_count + norm_eps)
    center = depth - bn_mean
    normal = center * inv_std * bn_gain + bn_bias
    conv_sig = jax.nn.sigmoid(normal)
    conv_act = (normal * conv_sig).astype(bf16)
    stream_three = stream_two + dot_plain(conv_act, p_output)

    if local:
        _, kept_four, (result, grad_four, half_four, sums_four) = ffn_forward_here(
            stream_three,
            gains[3],
            biases[3],
            (2 * quarter, 3 * quarter),
            quarter,
            place,
            sources,
            tail_last,
            (gains[4:5], biases[4:5], cotangent_rows),
        )
        gain_four, bias_four = sums_four[0], sums_four[1]
        grad_three, gin_second, gout_second, gain_three, bias_three = ffn_backward_here(
            grad_four,
            half_four,
            stream_three,
            gains[3],
            kept_four,
            (2 * quarter, 3 * quarter),
            quarter,
            place,
            sources,
            ((1, 0),),
        )
    else:
        stream_four, kept_four = ffn_forward(
            stream_three, gains[3], biases[3], in_second, out_second
        )
        stats_last = norm_stats(stream_four)
        result = norm_apply(stream_four, stats_last, gains[4], biases[4]).astype(bf16)
        grad_four, gain_four, bias_four = norm_backward(
            stream_four, stats_last, gains[4], cotangent_rows.astype(f32)
        )
        grad_three, gin_second, gout_second, gain_three, bias_three = ffn_backward(
            grad_four, stream_three, gains[3], kept_four, in_second, out_second
        )

    incoming = grad_three.astype(bf16)
    incoming_three = incoming
    grad_po = None if local else weight_grad(conv_act, incoming)
    conv_slope = conv_sig * (1.0 + normal * (1.0 - conv_sig))
    grad_normal = dot_rows(incoming, p_output) * conv_slope
    own_sums = jnp.stack([jnp.sum(grad_normal, axis=0), jnp.sum(grad_normal * center, axis=0)])
    sums = butterfly_sum(own_sums, "dp")
    if local:
        block_out = send_home(result)
        sums, block_out = lax.optimization_barrier((sums, block_out))
        block_out = finish_hops(*block_out)
    else:
        block_out = send_home(result)
    sum_plain, sum_center = sums
    bn_scale = bn_gain * inv_std
    grad_depth = bn_scale * grad_normal - frame_mask * bn_scale * (
        sum_plain + inv_std * inv_std * sum_center * center
    ) / total_count
    grad_glu = jnp.zeros_like(glu)
    tap_grads = []
    for t in range(taps):
        grad_glu = grad_glu + convs[t] * shift_rows(grad_depth, margin - t)
        tap_grads.append(jnp.sum(grad_depth * shift_rows(glu, t - margin), axis=0))
    grad_glu = grad_glu * frame_mask
    grad_linear = (grad_glu * gate_sig).astype(bf16)
    grad_gating = (grad_glu * linear * gate_sig * (1.0 - gate_sig)).astype(bf16)
    if not local:
        grad_pv = weight_grad(grad_linear, conv_in)
        grad_pg = weight_grad(grad_gating, conv_in)
    back, gain_two, bias_two = norm_backward(
        stream_two,
        stats_conv,
        gains[2],
        dot_plain(grad_linear, p_value) + dot_plain(grad_gating, p_gate),
    )
    grad_two = grad_three + back

    incoming = grad_two.astype(bf16)
    grad_wo = None if local else weight_grad(merged, incoming)
    grad_merged = dot_rows(incoming, w_output).astype(bf16)
    if local:
        grad_merged, gin_second, gout_second = lax.optimization_barrier(
            (grad_merged, gin_second, gout_second)
        )
    grad_q, grad_k, grad_v = head_call(
        attend_back_kernel, valid, (queries, keys, values, grad_merged), 3, 10
    )
    if local:
        singles_other, singles_own = single_grads(
            ((0, 0), (1, 0), (2, 0), (3, 1), (4, 2), (5, 2), (6, 3)),
            (grad_q, grad_k, grad_v, merged, grad_linear, grad_gating, conv_act),
            (att_in, incoming, conv_in, incoming_three),
        )
    else:
        grad_wq = weight_grad(grad_q, att_in)
        grad_wk = weight_grad(grad_k, att_in)
        grad_wv = weight_grad(grad_v, att_in)
    back, gain_one, bias_one = norm_backward(
        stream_one,
        stats_att,
        gains[1],
        dot_plain(grad_q, w_query) + dot_plain(grad_k, w_key) + dot_plain(grad_v, w_value),
    )
    grad_one = grad_two + back
    if local:
        grad_one, singles_other = lax.optimization_barrier((grad_one, singles_other))
        singles_other = swap(singles_other, "core")

    if local:
        grad_zero, gin_first, gout_first, gain_zero, bias_zero = ffn_backward_here(
            grad_one,
            (0.5 * grad_one).astype(bf16),
            source,
            gains[0],
            kept_one,
            (0, quarter),
            quarter,
            place,
            sources,
            ((1,), (0,)),
        )
    else:
        grad_zero, gin_first, gout_first, gain_zero, bias_zero = ffn_backward(
            grad_one, source, gains[0], kept_one, in_first, out_first
        )
    block_grad = send_home(grad_zero)

    conv_small = jnp.stack(tap_grads + [own_sums[1] * inv_std, own_sums[0]])
    conv_small = conv_small.reshape(-1, chan_count, rows_tile)[:, position].reshape(-1, width)
    small = jnp.concatenate(
        [
            jnp.stack(
                [gain_zero, gain_one, gain_two, gain_three, gain_four]
                + [bias_zero, bias_one, bias_two, bias_three, bias_four]
            ),
            conv_small,
        ]
    )
    if local:
        small = small + swap(small, "core")
        groups = [(i * quarter, quarter, False) for i in range(4)]
        groups.append((base, tile_count - base, True))
        pairs = [
            tuple(v.reshape(4, quarter, -1, width) for v in pair)
            for pair in (gin_first, gout_first, gin_second, gout_second)
        ]
        shape = (tile_count - base, 4) + pairs[0][0].shape[2:]
        pairs.append((singles_own.reshape(shape), singles_other.reshape(shape)))
        keep, got, small, block_grad = reduce_tiles_here(
            groups, [p[0] for p in pairs], [p[1] for p in pairs], place, slots, small, block_grad
        )
        block_grad = finish_hops(*block_grad)
        tile_m, tile_v, tile_w, tile_b = update_tiles_here(
            keep,
            got,
            owned_mask(tile_slot, slots).astype(jnp.int32),
            master,
            tile_first,
            tile_second,
        )
    else:
        grads = [gin_first, gout_first, gin_second, gout_second]
        grads += [grad_wq, grad_wk, grad_wv, grad_wo, grad_pv, grad_pg, grad_po]
        owned = reduce_tiles(
            jnp.concatenate(grads).reshape(tile_count, width, width), tile_slot, slots
        )
        small = butterfly_sum(butterfly_sum(small, "dp"), "chan")
        owned = jnp.where(owned_mask(tile_slot, slots)[:, None, None], owned, 0.0)
        tile_m, tile_v, tile_w = adamw_step(
            master, owned, tile_first, tile_second, tile_rate, weight_decay
        )
        tile_b = tile_w.astype(bf16)
    norm_total = small[: norm_params.shape[0]]
    conv_grad = lax.dynamic_slice_in_dim(
        small[norm_params.shape[0] :], chan_index * rows_tile, rows_tile, 1
    )

    norm_m, norm_v, norm_w = adamw_step(
        norm_params, norm_total, norm_first, norm_second, small_rate, 0.0
    )
    conv_m, conv_v, conv_w = adamw_step(
        conv_params, conv_grad, conv_first, conv_second, small_rate, 0.0
    )
    return (
        block_out[:, None],
        block_grad[:, None].astype(f32),
        tile_m,
        tile_v,
        tile_w,
        tile_b,
        norm_m,
        norm_v,
        norm_w,
        conv_m,
        conv_v,
        conv_w,
    )


def solution(mesh):
    in_specs = (
        P(None, "dp", "chan", None),
        P(None, "dp", "chan", None),
        P(None, "dp"),
        P(),
        P("dp", "chan", None),
        P("dp", "chan", None),
        P("dp", "chan", None),
        P(),
        P(),
        P(),
        P(None, "chan"),
        P(None, "chan"),
        P(None, "chan"),
    )
    out_specs = (
        P(None, "dp", "chan", None),
        P(None, "dp", "chan", None),
        P("dp", "chan", None),
        P("dp", "chan", None),
        P("dp", "chan", None),
        P("dp", "chan", None),
        P(),
        P(),
        P(),
        P(None, "chan"),
        P(None, "chan"),
        P(None, "chan"),
    )
    return jax.shard_map(shards, mesh=mesh, in_specs=in_specs, out_specs=out_specs, check_vma=False)
```

```python
import jax
import jax.numpy as jnp
from jax import lax
from jax.experimental import pallas as pl
from jax.experimental.pallas import tpu as pltpu
from jax.sharding import PartitionSpec as P

HEAD_DIM = 128
STEP = 10

norm_eps = 1e-05
masked_score = -1e30
beta_one = 0.9
beta_two = 0.98
adam_eps = 1e-08
tile_rate = 0.06
small_rate = 0.6
weight_decay = 0.01

BOTH = ("dp", "chan")
bf16 = jnp.bfloat16
f32 = jnp.float32


def dot_rows(left, right):
    return lax.dot_general(left, right, (((1,), (1,)), ((), ())), preferred_element_type=f32)


def dot_plain(left, right):
    return jnp.dot(left, right, preferred_element_type=f32)


def dot_cols(left, right):
    return lax.dot_general(left, right, (((0,), (0,)), ((), ())), preferred_element_type=f32)


def adamw_step(weight, gradient, first_old, second_old, rate, decay):
    first_new = beta_one * first_old + (1.0 - beta_one) * gradient
    second_new = beta_two * second_old + (1.0 - beta_two) * gradient * gradient
    first_hat = first_new / (1.0 - beta_one**STEP)
    second_hat = second_new / (1.0 - beta_two**STEP)
    weight_new = weight - rate * (first_hat / (jnp.sqrt(second_hat) + adam_eps) + decay * weight)
    return (first_new, second_new, weight_new)


def exchange(value, axis, mask):
    size = lax.axis_size(axis)
    return lax.ppermute(value, axis, [(i, i ^ mask) for i in range(size)])


def swap_blocks(value, axis):
    size = lax.axis_size(axis)
    me = lax.axis_index(axis)
    result = value
    for mask in range(1, size):
        sent = lax.dynamic_index_in_dim(value, me ^ mask, 0, keepdims=True)
        result = lax.dynamic_update_slice_in_dim(result, exchange(sent, axis, mask), me ^ mask, 0)
    return result


def swap_in_hops(value):
    me = lax.axis_index("chan")
    pairs = value.reshape((2, 2) + value.shape[1:])
    core, y = lax.rem(me, 2), lax.div(me, 2)
    keep = lax.dynamic_index_in_dim(pairs, core, 1, keepdims=False)
    sent = lax.dynamic_index_in_dim(pairs, 1 - core, 1, keepdims=False)
    got = exchange(sent, "chan", 1)
    low = jnp.where(core == 0, keep, got)
    high = jnp.where(core == 0, got, keep)
    mixed = jnp.stack([low, high], axis=1)
    there = lax.dynamic_index_in_dim(mixed, 1 - y, 0, keepdims=False)
    here = lax.dynamic_index_in_dim(mixed, y, 0, keepdims=False)
    return here, there


def finish_hops(here, arrived_there):
    y = lax.div(lax.axis_index("chan"), 2)
    low = jnp.where(y == 0, here, arrived_there)
    high = jnp.where(y == 0, arrived_there, here)
    return jnp.concatenate([low, high])


def gather_small(value, axis):
    size = lax.axis_size(axis)
    me = lax.axis_index(axis)
    result = jnp.zeros((size,) + value.shape, value.dtype)
    result = lax.dynamic_update_slice_in_dim(result, value[None], me, 0)
    for mask in range(1, size):
        result = lax.dynamic_update_slice_in_dim(
            result, exchange(value[None], axis, mask), me ^ mask, 0
        )
    return result


def butterfly_sum(value, axis):
    size = lax.axis_size(axis)
    mask = 1
    while mask < size:
        value = value + exchange(value, axis, mask)
        mask *= 2
    return value


BITS = {"core": 1, "y": 2, "x": 4, "z1": 8, "z2": 16}
ORDERS = (
    ("z2", "y", "z1", "x"),
    ("z1", "z2", "y", "x"),
    ("z2", "y", "x", "z1"),
    ("z1", "x", "y", "z2"),
    ("z2", "z1", "x", "y"),
    ("z1", "x", "z2", "y"),
)
LAST = (("x", (0, 1)), ("z1", (2,)), ("z2", (3,)), ("y", (4, 5)))
HALVES = 2


def is_slice(dp_count, chan_count, slots):
    return (dp_count, chan_count, slots) == (8, 4, 3)


def swap(value, name):
    size = lax.axis_size("dp") * lax.axis_size("chan")
    return lax.ppermute(value, BOTH, [(i, i ^ BITS[name]) for i in range(size)])


def step_groups(step, orders):
    groups = {}
    for part, order in enumerate(orders):
        groups.setdefault(order[step], []).append(part)
    return groups


def gather_parts(master, extra, small):
    half = master.shape[1] // HALVES
    own = [master[:, h * half : (h + 1) * half].astype(bf16) for h in range(HALVES)]
    own = lax.optimization_barrier(own)
    state = [own[p % HALVES][p // HALVES][None] for p in range(6)]
    moved = []
    for step in range(4):
        groups = step_groups(step, ORDERS)
        sent = {
            name: (jnp.concatenate([state[p] for p in parts]) if len(parts) > 1 else state[parts[0]])
            for name, parts in groups.items()
        }
        if step == 0:
            sent = {ORDERS[h][0]: own[h] for h in range(HALVES)}
            sent, extra = lax.optimization_barrier((sent, extra))
            moved = [exchange(value, "chan", mask + 1) for mask, value in enumerate(extra)]
        elif step == 1:
            sent, small = lax.optimization_barrier((sent, small))
            small = jnp.stack([small, exchange(small, "chan", 2)])
        elif step == 2:
            sent, small = lax.optimization_barrier((sent, small))
            small = jnp.concatenate([small, exchange(small, "chan", 1)])
        else:
            sent = lax.optimization_barrier(sent)
        got = {name: swap(value, name) for name, value in sent.items()}
        if step == 3:
            return ([sent[n] for n, _ in LAST], [got[n] for n, _ in LAST], moved, small)
        got, moved, small = lax.optimization_barrier((got, moved, small))
        size = 1 << step
        for name, parts in groups.items():
            for i, p in enumerate(parts):
                state[p] = jnp.concatenate([state[p], got[name][i * size : (i + 1) * size]])


def place_of(part, bits):
    order = ORDERS[part]
    index = bits[order[2]] * 4 + bits[order[1]] * 2 + bits[order[0]]
    for _, parts in LAST:
        if part in parts:
            return (bits[order[3]], index + 8 * parts.index(part))


def array_of(position, h):
    part = position * HALVES + h
    return [i for i, (_, parts) in enumerate(LAST) if part in parts][0]


def slot_places(slot, slots):
    owner, position = slot // slots, slot % slots
    gap = owner ^ lax.axis_index("dp")
    bits = {"x": gap & 1, "z1": (gap >> 1) & 1, "z2": (gap >> 2) & 1}
    rows = []
    for dy in range(2):
        for h in range(HALVES):
            codes = []
            for s in range(slots):
                far, index = place_of(s * HALVES + h, dict(bits, y=jnp.full_like(gap, dy)))
                codes.append((far * 4 + array_of(s, h)) * 16 + index)
            rows.append(jnp.select([position == s for s in range(slots)], codes))
    return jnp.stack(rows).astype(jnp.int32)


def at_place(place, arrays, act):
    which, index = lax.div(place, 16), lax.rem(place, 16)
    for i, array in enumerate(arrays):

        @pl.when(which == i)
        def _():
            act(array, index)


def staged(count, depth, load, drain_in, store, drain_out):
    ahead = depth // 2
    for i in range(count + ahead):
        if i < count:
            if i >= depth:
                drain_out(i - depth)
            load(i)
        if i >= ahead:
            drain_in(i - ahead)
            store(i - ahead)
    for i in range(max(count - depth, 0), count):
        drain_out(i)


DEPTH = 8


SOURCES = 13


def sixteen(refs):
    near, at = [], 0
    for _, parts in LAST:
        near.append(refs[8].at[pl.ds(at, 8 * len(parts))])
        at += 8 * len(parts)
    return list(refs[:8]) + near + list(refs[9:SOURCES])


def assemble_kernel(first, place_ref, *refs):
    sources, outs = sixteen(refs), refs[SOURCES:-3]
    buffer, in_sem, out_sem = refs[-3:]
    items = [(core, g) for core in range(2) for g in range(len(outs))]

    def load(i):
        core, g = items[i]
        for b in range(4):
            at_place(
                place_ref[b, first + g],
                sources[core * 8 : core * 8 + 8],
                lambda array, index: pltpu.make_async_copy(
                    array.at[index], buffer.at[i % DEPTH, b], in_sem.at[i % DEPTH]
                ).start(),
            )

    def drain_in(i):
        slot = buffer.at[i % DEPTH]
        pltpu.make_async_copy(slot, slot, in_sem.at[i % DEPTH]).wait()

    def out_copy(i):
        core, g = items[i]
        return pltpu.make_async_copy(buffer.at[i % DEPTH], outs[g].at[core], out_sem.at[i % DEPTH])

    staged(
        len(items), DEPTH, load, drain_in, lambda i: out_copy(i).start(), lambda i: out_copy(i).wait()
    )


ANYWHERE = pl.BlockSpec(memory_space=pl.ANY)
IN_SMEM = pl.BlockSpec(memory_space=pltpu.SMEM)
IN_VMEM = pl.BlockSpec(memory_space=pltpu.VMEM)


def assemble(place, sources, first, count):
    rows, width = sources[0].shape[1:]
    mats = pl.pallas_call(
        lambda *refs: assemble_kernel(first, *refs),
        in_specs=[IN_SMEM] + [ANYWHERE] * SOURCES,
        out_specs=[ANYWHERE] * count,
        out_shape=[jax.ShapeDtypeStruct((2, 4, rows, width), bf16)] * count,
        scratch_shapes=[
            pltpu.VMEM((DEPTH, 4, rows, width), bf16),
            pltpu.SemaphoreType.DMA((DEPTH,)),
            pltpu.SemaphoreType.DMA((DEPTH,)),
        ],
        compiler_params=pltpu.CompilerParams(vmem_limit_bytes=12 * 1024 * 1024),
        cost_estimate=pl.CostEstimate(
            flops=0, bytes_accessed=count * 32 * rows * width, transcendentals=0
        ),
    )(place, *sources)
    return [m.reshape(-1, width) for m in mats]


def gather_sources(master, extra, small):
    near, far, moved, small = gather_parts(master, extra, small)
    near_other = swap(jnp.concatenate(near), "core")
    far_other = [swap(v, "core") for v in far]
    return near + far + [near_other] + far_other, moved, small


BPS = 2
STEPS = 4 // BPS


def fetch_rows(at, item, firsts, count, place_ref, sources, buffers, sems):
    core, step = item
    rows = sources[0].shape[1]
    for m, first in enumerate(firsts):
        for i in range(BPS):
            for j in range(count):
                at_place(
                    place_ref[step * BPS + i, first + j],
                    sources[core * 8 : core * 8 + 8],
                    lambda array, index: pltpu.make_async_copy(
                        array.at[index],
                        buffers[m].at[at, pl.ds((i * count + j) * rows, rows)],
                        sems.at[m, at],
                    ).start(),
                )


def arrived(m, at, buffers, sems):
    pltpu.make_async_copy(buffers[m].at[at], buffers[m].at[at], sems.at[m, at]).wait()
    return buffers[m][at]


def tail_next(out_ref, ins, outs):
    gain_ref, bias_ref = ins
    next_ref, stats_ref = outs
    lanes = stats_ref.shape[1] // 2
    for r in range(4):
        rows = pl.ds(r * (out_ref.shape[0] // 4), out_ref.shape[0] // 4)
        stream = out_ref[rows, :]
        mean, inv = norm_stats(stream)
        next_ref[rows, :] = norm_apply(
            stream, (mean, inv), gain_ref[...], bias_ref[...]
        ).astype(bf16)
        stats_ref[rows, :lanes] = jnp.broadcast_to(mean, (stream.shape[0], lanes))
        stats_ref[rows, lanes:] = jnp.broadcast_to(inv, (stream.shape[0], lanes))


def tail_last(out_ref, ins, outs):
    gain_ref, bias_ref, up_ref = ins
    result_ref, grad_ref, half_ref, sums_ref = outs
    for r in range(4):
        rows = pl.ds(r * (out_ref.shape[0] // 4), out_ref.shape[0] // 4)
        stream, upstream = out_ref[rows, :], up_ref[rows, :].astype(f32)
        stats = norm_stats(stream)
        result_ref[rows, :] = norm_apply(stream, stats, gain_ref[...], bias_ref[...]).astype(bf16)
        back, grad_gain, grad_bias = norm_backward(stream, stats, gain_ref[...], upstream)
        grad_ref[rows, :] = back
        half_ref[rows, :] = (0.5 * back).astype(bf16)
        sums = jnp.concatenate([grad_gain[None], grad_bias[None]])
        sums_ref[...] = sums if r == 0 else sums_ref[...] + sums


def ffn_kernel(firsts, count, tail, tail_ins, place_ref, normed_ref, base_ref, *refs):
    ins, refs = refs[:tail_ins], refs[tail_ins:]
    sources = sixteen(refs)
    out_ref, act_ref, slope_ref = refs[SOURCES : SOURCES + 3]
    outs, (in_buf, out_buf, sems) = refs[SOURCES + 3 : -3], refs[-3:]
    buffers = (in_buf, out_buf)
    size = in_buf.shape[1]
    items = [(core, q) for core in range(2) for q in range(STEPS)]
    for i in range(2):
        fetch_rows(i, items[i], firsts, count, place_ref, sources, buffers, sems)
    for i, (core, q) in enumerate(items):
        cut = slice(i * size, (i + 1) * size)
        hidden = dot_rows(normed_ref[...], arrived(0, i % 2, buffers, sems))
        sig = jax.nn.sigmoid(hidden)
        active = (hidden * sig).astype(bf16)
        act_ref[:, cut] = active
        slope_ref[:, cut] = (sig * (1.0 + hidden * (1.0 - sig))).astype(bf16)
        before = base_ref[...] if i == 0 else out_ref[...]
        out_ref[...] = before + 0.5 * dot_plain(active, arrived(1, i % 2, buffers, sems))
        if i + 2 < len(items):
            fetch_rows(i % 2, items[i + 2], firsts, count, place_ref, sources, buffers, sems)
    tail(out_ref, ins, outs)


def ffn_back_kernel(cores, based, firsts, count, place_ref, e_ref, act_ref, slope_ref, normed_ref, *refs):
    base_ref, refs = (refs[0], refs[1:]) if based else (None, refs)
    sources, refs = sixteen(refs), refs[SOURCES:]
    dx_ref, grads, refs = refs[0], refs[1 : 1 + 2 * len(cores)], refs[1 + 2 * len(cores) :]
    in_grads, out_grads, put_sems, in_buf, out_buf, sems = refs
    buffers = (in_buf, out_buf)
    size = in_buf.shape[1]
    items = [(core, q) for core in cores for q in range(STEPS)]
    for i in range(2):
        fetch_rows(i, items[i], firsts, count, place_ref, sources, buffers, sems)

    def copy(m, i):
        core, q = items[i]
        target = grads[2 * cores.index(core) + m].at[pl.ds(q * size, size)]
        buffer = (in_grads, out_grads)[m]
        return pltpu.make_async_copy(buffer.at[i % 2], target, put_sems.at[m, i % 2])

    for i, (core, q) in enumerate(items):
        cut = slice((core * STEPS + q) * size, (core * STEPS + q + 1) * size)
        incoming = e_ref[...]
        grad = dot_rows(incoming, arrived(1, i % 2, buffers, sems)) * slope_ref[:, cut].astype(f32)
        grad = grad.astype(bf16)
        change = dot_plain(grad, arrived(0, i % 2, buffers, sems))
        if i + 2 < len(items):
            fetch_rows(i % 2, items[i + 2], firsts, count, place_ref, sources, buffers, sems)
        if i > 0:
            dx_ref[...] += change
        elif based:
            dx_ref[...] = base_ref[...] + change
        else:
            dx_ref[...] = change
        if i >= 2:
            copy(1, i - 2).wait()
        out_grads[i % 2] = dot_cols(act_ref[:, cut], incoming).astype(bf16)
        copy(1, i).start()
        if i >= 2:
            copy(0, i - 2).wait()
        in_grads[i % 2] = dot_cols(grad, normed_ref[...]).astype(bf16)
        copy(0, i).start()
    for i in range(len(items) - 2, len(items)):
        for m in range(2):
            copy(m, i).wait()


def grads_kernel(pairs, lefts, rights, *refs):
    left_refs, right_refs = refs[:lefts], refs[lefts : lefts + rights]
    other, own, buffer, sems = refs[lefts + rights :]
    half = own.shape[1]
    for k, (i, j) in enumerate(pairs):
        slot = k % 2
        if k >= 2:
            pltpu.make_async_copy(buffer.at[slot], buffer.at[slot], sems.at[slot]).wait()
        buffer[slot] = dot_cols(left_refs[i][...], right_refs[j][...]).astype(bf16)
        pltpu.make_async_copy(buffer.at[slot, pl.ds(0, half)], own.at[k], sems.at[slot]).start()
        pltpu.make_async_copy(buffer.at[slot, pl.ds(half, half)], other.at[k], sems.at[slot]).start()
    for slot in range(2):
        pltpu.make_async_copy(buffer.at[slot], buffer.at[slot], sems.at[slot]).wait()


def single_grads(pairs, lefts, rights):
    rows, width = lefts[0].shape
    shape = jax.ShapeDtypeStruct((len(pairs), width // 2, width), bf16)
    return pl.pallas_call(
        lambda *refs: grads_kernel(pairs, len(lefts), len(rights), *refs),
        in_specs=[IN_VMEM] * (len(lefts) + len(rights)),
        out_specs=[ANYWHERE] * 2,
        out_shape=[shape] * 2,
        scratch_shapes=[pltpu.VMEM((2, width, width), bf16), pltpu.SemaphoreType.DMA((2,))],
        compiler_params=pltpu.CompilerParams(vmem_limit_bytes=24 * 1024 * 1024),
        cost_estimate=pl.CostEstimate(
            flops=2 * len(pairs) * rows * width * width,
            bytes_accessed=2 * len(pairs) * width * (width + 2 * rows),
            transcendentals=0,
        ),
    )(*lefts, *rights)


def ffn_scratch(count, rows, width):
    return [
        pltpu.VMEM((2, BPS * count * rows, width), bf16),
        pltpu.VMEM((2, BPS * count * rows, width), bf16),
        pltpu.SemaphoreType.DMA((2, 2)),
    ]


LANES = 128


def ffn_forward_here(stream, gain, bias, firsts, count, place, sources, tail, tail_ins):
    rows, width = stream.shape
    block = sources[0].shape[1]
    hidden = 8 * count * block
    shape = jax.ShapeDtypeStruct
    stats = norm_stats(stream)
    normed = norm_apply(stream, stats, gain, bias).astype(bf16)
    if tail is tail_next:
        more = [shape((rows, width), bf16), shape((rows, 2 * LANES), f32)]
    else:
        more = [
            shape((rows, width), bf16),
            shape((rows, width), f32),
            shape((rows, width), bf16),
            shape((2, width), f32),
        ]
    result, active, slope, *more = pl.pallas_call(
        lambda *refs: ffn_kernel(firsts, count, tail, len(tail_ins), *refs),
        in_specs=[IN_SMEM] + [IN_VMEM] * (2 + len(tail_ins)) + [ANYWHERE] * SOURCES,
        out_specs=[IN_VMEM] * (3 + len(more)),
        out_shape=[
            shape((rows, width), f32),
            shape((rows, hidden), bf16),
            shape((rows, hidden), bf16),
        ]
        + more,
        scratch_shapes=ffn_scratch(count, block, width),
        compiler_params=pltpu.CompilerParams(vmem_limit_bytes=FORWARD_MB * 1024 * 1024),
        cost_estimate=pl.CostEstimate(
            flops=4 * rows * width * hidden,
            bytes_accessed=4 * hidden * (width + rows),
            transcendentals=rows * hidden,
        ),
    )(place, normed, stream, *tail_ins, *sources)
    return (result, (stats, normed, active, slope), more)


FORWARD_MB = 32
BACKWARD_MB = 38


def ffn_backward_here(
    upstream, incoming, stream, gain, kept, firsts, count, place, sources, calls
):
    stats, normed, active, slope = kept
    rows, width = stream.shape
    block = sources[0].shape[1]
    half = 4 * count * block
    size = BPS * count * block
    shape = jax.ShapeDtypeStruct
    base, grads = [], []
    for cores in calls:
        dx, *some = pl.pallas_call(
            lambda *refs, cores=cores: ffn_back_kernel(cores, bool(base), firsts, count, *refs),
            in_specs=[IN_SMEM] + [IN_VMEM] * (4 + len(base)) + [ANYWHERE] * SOURCES,
            out_specs=[IN_VMEM] + [ANYWHERE] * (2 * len(cores)),
            out_shape=[shape((rows, width), f32)]
            + [shape((half, width), bf16)] * (2 * len(cores)),
            scratch_shapes=[
                pltpu.VMEM((2, size, width), bf16),
                pltpu.VMEM((2, size, width), bf16),
                pltpu.SemaphoreType.DMA((2, 2)),
            ]
            + ffn_scratch(count, block, width),
            compiler_params=pltpu.CompilerParams(vmem_limit_bytes=BACKWARD_MB * 1024 * 1024),
            cost_estimate=pl.CostEstimate(
                flops=8 * rows * width * half * len(cores),
                bytes_accessed=8 * half * (width + rows) * len(cores),
                transcendentals=0,
            ),
        )(place, incoming, active, slope, normed, *base, *sources)
        base = [dx]
        if not grads:
            some = [swap(v, "core") for v in some[:2]] + some[2:]
        grads += some
    other_in, other_out, own_in, own_out = grads
    back, grad_gain, grad_bias = norm_backward(stream, stats, gain, dx)
    return (upstream + back, (own_in, other_in), (own_out, other_out), grad_gain, grad_bias)


SCATTER = 6


def scatter_kernel(groups, place_ref, *refs):
    owns, others = refs[: len(groups)], refs[len(groups) : 2 * len(groups)]
    outs = refs[2 * len(groups) : 2 * len(groups) + 8]
    own_buf, other_buf, in_sem, out_sem = refs[2 * len(groups) + 8 :]
    items = []
    for g, (first, count, whole) in enumerate(groups):
        if whole:
            items += [(g, k, [(b, first + k) for b in range(4)]) for k in range(count)]
        else:
            items += [(g, b, [(b, first + j) for j in range(count)]) for b in range(4)]

    def in_copies(i):
        g, k, _ = items[i]
        slot = i % SCATTER
        return (
            pltpu.make_async_copy(owns[g].at[k], own_buf.at[slot], in_sem.at[0, slot]),
            pltpu.make_async_copy(others[g].at[k], other_buf.at[slot], in_sem.at[1, slot]),
        )

    def load(i):
        for copy in in_copies(i):
            copy.start()

    def drain_in(i):
        for copy in in_copies(i):
            copy.wait()

    def store(i):
        slot = i % SCATTER
        own_buf[slot] = (own_buf[slot].astype(f32) + other_buf[slot].astype(f32)).astype(bf16)
        for at, (b, tile) in enumerate(items[i][2]):
            at_place(
                place_ref[b, tile],
                outs,
                lambda array, index: pltpu.make_async_copy(
                    own_buf.at[slot, at], array.at[index], out_sem.at[slot]
                ).start(),
            )

    def drain_out(i):
        slot = own_buf.at[i % SCATTER]
        pltpu.make_async_copy(slot, slot, out_sem.at[i % SCATTER]).wait()

    staged(len(items), SCATTER, load, drain_in, store, drain_out)


def combine_kernel(plan, count, *refs):
    keeps, gots, outs = refs[:count], refs[count : 2 * count], refs[2 * count :]
    rows = 16

    def body(r, carry):
        cut = pl.ds(pl.multiple_of(r * rows, rows), rows)
        for out, at, array, index in plan:
            total = keeps[array][index, cut, :].astype(f32) + gots[array][index, cut, :].astype(f32)
            outs[out][at, cut, :] = total.astype(bf16)
        return carry

    lax.fori_loop(0, keeps[0].shape[1] // rows, body, 0)


def combine(step, keep, got):
    before, now = step_groups(step + 1, ORDERS), step_groups(step, ORDERS)
    size = 1 << step
    lies = {
        p: (a, 2 * i * size)
        for a, parts in enumerate(before.values())
        for i, p in enumerate(parts)
    }
    plan, shapes = [], []
    for half in (1, 0):
        for parts in now.values():
            for i, p in enumerate(parts):
                array, first = lies[p]
                plan += [
                    (len(shapes), i * size + k, array, first + half * size + k)
                    for k in range(size)
                ]
            some = next(iter(keep.values()))
            shapes.append(jax.ShapeDtypeStruct((size * len(parts),) + some.shape[1:], bf16))
    blocks = sum(s.shape[0] for s in shapes)
    outs = pl.pallas_call(
        lambda *refs: combine_kernel(plan, len(before), *refs),
        in_specs=[IN_VMEM] * (2 * len(before)),
        out_specs=[IN_VMEM] * len(shapes),
        out_shape=shapes,
        compiler_params=pltpu.CompilerParams(
            vmem_limit_bytes=(3 * blocks * 2 * some.shape[1] * some.shape[2]) + (4 << 20)
        ),
        cost_estimate=pl.CostEstimate(
            flops=blocks * some.shape[1] * some.shape[2],
            bytes_accessed=6 * blocks * some.shape[1] * some.shape[2],
            transcendentals=0,
        ),
    )(*[keep[n] for n in before], *[got[n] for n in before])
    return dict(zip(now, outs[: len(now)])), dict(zip(now, outs[len(now) :]))


def reduce_tiles_here(groups, owns, others, place, slots, small, ahead):
    rows, width = owns[0].shape[2:]
    shapes = [jax.ShapeDtypeStruct((8 * len(parts), rows, width), bf16) for _, parts in LAST]
    arrays = pl.pallas_call(
        lambda *refs: scatter_kernel(groups, *refs),
        in_specs=[IN_SMEM] + [ANYWHERE] * (2 * len(groups)),
        out_specs=[ANYWHERE] * 8,
        out_shape=shapes + shapes,
        scratch_shapes=[
            pltpu.VMEM((SCATTER, 4, rows, width), bf16),
            pltpu.VMEM((SCATTER, 4, rows, width), bf16),
            pltpu.SemaphoreType.DMA((2, SCATTER)),
            pltpu.SemaphoreType.DMA((SCATTER,)),
        ],
        compiler_params=pltpu.CompilerParams(vmem_limit_bytes=32 * 1024 * 1024),
        cost_estimate=pl.CostEstimate(
            flops=0, bytes_accessed=6 * 92 * rows * width, transcendentals=0
        ),
    )(place, *owns, *others)
    arrays, ahead = lax.optimization_barrier((arrays, ahead))
    keep = {n: a for (n, _), a in zip(LAST, arrays[:4])}
    send = {n: a for (n, _), a in zip(LAST, arrays[4:])}
    for step in range(3, -1, -1):
        if step == 2:
            size = 1 << step
            state = {}
            for name, parts in step_groups(step + 1, ORDERS).items():
                for i, p in enumerate(parts):
                    cut = slice(2 * i * size, 2 * (i + 1) * size)
                    state[p] = keep[name][cut].astype(f32) + got[name][cut].astype(f32)
            halves = []
            for cut in (slice(size, None), slice(0, size)):
                halves.append(
                    {
                        name: jnp.concatenate([state[p][cut] for p in parts]).astype(bf16)
                        for name, parts in step_groups(step, ORDERS).items()
                    }
                )
            send, keep = halves
        elif step < 2:
            send, keep = combine(step, keep, got)
        send, small = lax.optimization_barrier((send, small))
        got = {name: swap(value, name) for name, value in send.items()}
        small = small + swap(small, ("z2", "z1", "x", "y")[step])
        got, small = lax.optimization_barrier((got, small))
    order = step_groups(0, ORDERS)
    return [keep[n] for n in order], [got[n] for n in order], small, ahead


def update_kernel(filled_ref, k0, g0, k1, g1, w_ref, m_ref, v_ref, m_new, v_new, w_new, b_new):
    half = pl.program_id(1)
    first = k0[...].astype(f32) + g0[...].astype(f32)
    second = k1[...].astype(f32) + g1[...].astype(f32)
    gradient = jnp.where(half == 0, first, second)
    gradient = jnp.where(filled_ref[pl.program_id(0)] > 0, gradient, 0.0)
    moment, square, weight = adamw_step(
        w_ref[...], gradient, m_ref[...], v_ref[...], tile_rate, weight_decay
    )
    m_new[...], v_new[...], w_new[...] = moment, square, weight
    b_new[...] = weight.astype(bf16)


def update_tiles_here(keep, got, filled, master, tile_first, tile_second):
    slots, full, width = master.shape
    rows = full // HALVES
    part = pl.BlockSpec((1, rows, width), lambda s, h: (s, 0, 0))
    here = pl.BlockSpec((1, rows, width), lambda s, h: (s, h, 0))
    shape = jax.ShapeDtypeStruct(master.shape, f32)
    return pl.pallas_call(
        update_kernel,
        grid=(slots, HALVES),
        in_specs=[IN_SMEM] + [part] * 4 + [here] * 3,
        out_specs=[here] * 4,
        out_shape=[shape] * 3 + [jax.ShapeDtypeStruct(master.shape, bf16)],
        compiler_params=pltpu.CompilerParams(vmem_limit_bytes=16 * 1024 * 1024),
        cost_estimate=pl.CostEstimate(
            flops=20 * slots * full * width,
            bytes_accessed=30 * slots * full * width,
            transcendentals=slots * full * width,
        ),
    )(filled, keep[0], got[0], keep[1], got[1], master, tile_first, tile_second)


def owned_mask(tile_slot, slots):
    slot = lax.axis_index("dp") * slots + jnp.arange(slots, dtype=jnp.int32)
    return jnp.any(slot[:, None] == tile_slot[None, :], axis=1)


def gather_tiles(own, tile_slot, sizes):
    width = own.shape[2]
    strips = lax.all_gather(own, "dp", axis=0, tiled=True)
    strips = strips.at[tile_slot].get(mode="promise_in_bounds")
    whole = lax.all_gather(strips, "chan", axis=1, tiled=True)
    mats, first = [], 0
    for n in sizes:
        mats.append(whole[first : first + n].reshape(-1, width))
        first += n
    return mats


def reduce_tiles(grads, tile_slot, slots):
    slot = jnp.arange(lax.axis_size("dp") * slots, dtype=jnp.int32)
    tile_of = jnp.argmax(slot[:, None] == tile_slot[None, :], axis=1).astype(jnp.int32)
    strips = lax.psum_scatter(grads, "chan", scatter_dimension=1, tiled=True)
    placed = strips.at[tile_of].get(mode="promise_in_bounds")
    return lax.psum_scatter(placed, "dp", scatter_dimension=0, tiled=True).astype(f32)


def norm_stats(stream):
    mean = jnp.mean(stream, axis=-1, keepdims=True)
    center = stream - mean
    spread = jnp.mean(center * center, axis=-1, keepdims=True)
    return (mean, lax.rsqrt(spread + norm_eps))


def norm_apply(stream, stats, gain, bias):
    mean, inv = stats
    return (stream - mean) * inv * gain + bias


def norm_backward(stream, stats, gain, upstream):
    mean, inv = stats
    hat = (stream - mean) * inv
    scaled = upstream * gain
    back = (
        scaled
        - jnp.mean(scaled, axis=-1, keepdims=True)
        - hat * jnp.mean(scaled * hat, axis=-1, keepdims=True)
    ) * inv
    return (back, jnp.sum(upstream * hat, axis=0), jnp.sum(upstream, axis=0))


def masked_probs(query, key, valid):
    scores = dot_rows(query, key) * HEAD_DIM ** (-0.5)
    column = lax.broadcasted_iota(jnp.int32, (1, scores.shape[1]), 1)
    scores = jnp.where(column < valid, scores, masked_score)
    exponent = jnp.exp(scores - jnp.max(scores, axis=-1, keepdims=True))
    return exponent, 1.0 / jnp.sum(exponent, axis=-1, keepdims=True)


TOGETHER = 4


def attend_kernel(valid_ref, q_ref, k_ref, v_ref, out_ref):
    for i in range(TOGETHER):
        cut = slice(i * HEAD_DIM, (i + 1) * HEAD_DIM)
        exponent, inverse = masked_probs(q_ref[:, cut], k_ref[:, cut], valid_ref[0])
        probs = (exponent * inverse).astype(bf16)
        out_ref[:, cut] = dot_plain(probs, v_ref[:, cut]).astype(bf16)


def attend_back_kernel(valid_ref, q_ref, k_ref, v_ref, g_ref, dq_ref, dk_ref, dv_ref):
    scale = HEAD_DIM ** (-0.5)
    for i in range(TOGETHER):
        cut = slice(i * HEAD_DIM, (i + 1) * HEAD_DIM)
        query, key, grad = q_ref[:, cut], k_ref[:, cut], g_ref[:, cut]
        exponent, inverse = masked_probs(query, key, valid_ref[0])
        probs = exponent * inverse
        grad_probs = dot_rows(grad, v_ref[:, cut])
        row_dot = jnp.sum(probs * grad_probs, axis=-1, keepdims=True)
        grad_scores = (probs * (grad_probs - row_dot)).astype(bf16)
        dq_ref[:, cut] = (dot_plain(grad_scores, key) * scale).astype(bf16)
        dk_ref[:, cut] = (dot_cols(grad_scores, query) * scale).astype(bf16)
        dv_ref[:, cut] = dot_cols(probs.astype(bf16), grad).astype(bf16)


def head_call(kernel, valid, operands, out_count, flops):
    rows, width = operands[0].shape
    spec = pl.BlockSpec((rows, TOGETHER * HEAD_DIM), lambda h: (0, h))
    shape = jax.ShapeDtypeStruct((rows, width), bf16)
    return pl.pallas_call(
        kernel,
        grid=(width // HEAD_DIM // TOGETHER,),
        in_specs=[IN_SMEM] + [spec] * len(operands),
        out_specs=[spec] * out_count,
        out_shape=[shape] * out_count,
        cost_estimate=pl.CostEstimate(
            flops=flops * rows * rows * width,
            bytes_accessed=2 * rows * width * (len(operands) + out_count),
            transcendentals=rows * rows * width // HEAD_DIM,
        ),
        compiler_params=pltpu.CompilerParams(vmem_limit_bytes=24 * 1024 * 1024),
    )(valid, *operands)


def ffn_forward(stream, gain, bias, w_in, w_out):
    stats = norm_stats(stream)
    normed = norm_apply(stream, stats, gain, bias).astype(bf16)
    hidden = dot_rows(normed, w_in)
    sig = jax.nn.sigmoid(hidden)
    active = (hidden * sig).astype(bf16)
    slope = (sig * (1.0 + hidden * (1.0 - sig))).astype(bf16)
    return (stream + 0.5 * dot_plain(active, w_out), (stats, normed, active, slope))


def weight_grad(left, right):
    return dot_cols(left, right).astype(bf16)


def ffn_backward(upstream, stream, gain, kept, w_in, w_out):
    stats, normed, active, slope = kept
    incoming = (0.5 * upstream).astype(bf16)
    grad_out = weight_grad(active, incoming)
    grad_hidden = (dot_rows(incoming, w_out) * slope.astype(f32)).astype(bf16)
    grad_in = weight_grad(grad_hidden, normed)
    back, grad_gain, grad_bias = norm_backward(stream, stats, gain, dot_plain(grad_hidden, w_in))
    return (upstream + back, grad_in, grad_out, grad_gain, grad_bias)


def shift_rows(value, offset):
    rows = value.shape[0]
    if offset == 0:
        return value
    if offset > 0:
        return jnp.pad(value[offset:], ((0, offset), (0, 0)))
    return jnp.pad(value[: rows + offset], ((-offset, 0), (0, 0)))


def merge_stats(one, two):
    count_a, mean_a, dev_a = one
    count_b, mean_b, dev_b = two
    count = count_a + count_b
    mean = (count_a * mean_a + count_b * mean_b) / count
    gap = mean_a - mean_b
    return (count, mean, dev_a + dev_b + gap * gap * (count_a * count_b / count))


def shards(
    inputs,
    cotangent,
    lengths,
    tile_slot,
    master,
    tile_first,
    tile_second,
    norm_params,
    norm_first,
    norm_second,
    conv_params,
    conv_first,
    conv_second,
):
    micro, _, seg_rows, width = inputs.shape
    slots, rows_tile, _ = master.shape
    chan_count, dp_count = lax.axis_size("chan"), lax.axis_size("dp")
    chan_index = lax.axis_index("chan")
    assert micro == chan_count
    rows = seg_rows * chan_count
    tile_count = tile_slot.shape[0]
    quarter = (tile_count - 7) // 4
    base = 4 * quarter

    sizes = (quarter,) * 4 + (1,) * 7
    local = is_slice(dp_count, chan_count, slots)
    both = jnp.stack([inputs[:, 0], cotangent[:, 0]], axis=1)
    mine = both
    if local:
        extra = [
            lax.dynamic_index_in_dim(both, chan_index ^ mask, 0, keepdims=True)
            for mask in range(1, chan_count)
        ]
        sources, moved, convs = gather_sources(master, extra, conv_params)
        place = slot_places(tile_slot, slots)
        mats = [None] * tile_count
        for mask in range(1, chan_count):
            mine = lax.dynamic_update_slice_in_dim(mine, moved[mask - 1], chan_index ^ mask, 0)
        near = jnp.array([0, 2, 1, 3], jnp.int32)
        position = near[jnp.arange(chan_count, dtype=jnp.int32) ^ chan_index]
    else:
        mats = gather_tiles(master.astype(bf16), tile_slot, sizes)
        mine = swap_blocks(both, "chan")
        convs = gather_small(conv_params, "chan")
        position = jnp.arange(chan_count, dtype=jnp.int32)
    source = mine[:, 0].reshape(rows, width).astype(f32)
    cotangent_rows = mine[:, 1].reshape(rows, width)
    convs = jnp.moveaxis(convs, 0, 1).reshape(-1, width)
    valid = lax.dynamic_slice_in_dim(lengths[:, 0], chan_index, 1)
    in_first, out_first, in_second, out_second = mats[:4]
    gains, biases = norm_params[:5], norm_params[5:]
    taps = convs.shape[0] - 2
    margin = (taps - 1) // 2
    bn_gain, bn_bias = convs[taps], convs[taps + 1]
    frame_mask = (jnp.arange(rows, dtype=jnp.int32) < valid[0]).astype(f32)[:, None]

    def send_home(value):
        value = value.astype(bf16).reshape(chan_count, seg_rows, width)
        if not local:
            return swap_blocks(value, "chan")
        here, there = swap_in_hops(value)
        return (here, exchange(there, "chan", 2))

    if local:
        stream_one, kept_one, (att_in, stats_att) = ffn_forward_here(
            source,
            gains[0],
            biases[0],
            (0, quarter),
            quarter,
            place,
            sources,
            tail_next,
            (gains[1:2], biases[1:2]),
        )
        stats_att = (stats_att[:, :1], stats_att[:, LANES : LANES + 1])
        stream_one, place_after = lax.optimization_barrier((stream_one, place))
        mats[4:] = assemble(place_after, sources, base, tile_count - base)
    else:
        stream_one, kept_one = ffn_forward(source, gains[0], biases[0], in_first, out_first)
        stats_att = norm_stats(stream_one)
        att_in = norm_apply(stream_one, stats_att, gains[1], biases[1]).astype(bf16)
    w_query, w_key, w_value, w_output, p_value, p_gate, p_output = mats[4:]
    queries = dot_rows(att_in, w_query).astype(bf16)
    keys = dot_rows(att_in, w_key).astype(bf16)
    values = dot_rows(att_in, w_value).astype(bf16)
    (merged,) = head_call(attend_kernel, valid, (queries, keys, values), 1, 4)
    stream_two = stream_one + dot_plain(merged, w_output)

    stats_conv = norm_stats(stream_two)
    conv_in = norm_apply(stream_two, stats_conv, gains[2], biases[2]).astype(bf16)
    linear = dot_rows(conv_in, p_value)
    gate_sig = jax.nn.sigmoid(dot_rows(conv_in, p_gate))
    glu = linear * gate_sig * frame_mask
    depth = jnp.zeros_like(glu)
    for t in range(taps):
        depth = depth + convs[t] * shift_rows(glu, t - margin)
    count = valid[0].astype(f32)
    local_mean = jnp.sum(depth * frame_mask, axis=0) / count
    local_gap = (depth - local_mean) * frame_mask
    local_dev = jnp.sum(local_gap * local_gap, axis=0)
    stats = (jnp.full((width,), count), local_mean, local_dev)
    mask = 1
    while mask < dp_count:
        other = exchange(jnp.stack(stats), "dp", mask)
        stats = merge_stats(stats, (other[0], other[1], other[2]))
        mask *= 2
    total_count, bn_mean, bn_dev = stats
    inv_std = lax.rsqrt(bn_dev / total_count + norm_eps)
    center = depth - bn_mean
    normal = center * inv_std * bn_gain + bn_bias
    conv_sig = jax.nn.sigmoid(normal)
    conv_act = (normal * conv_sig).astype(bf16)
    stream_three = stream_two + dot_plain(conv_act, p_output)

    if local:
        _, kept_four, (result, grad_four, half_four, sums_four) = ffn_forward_here(
            stream_three,
            gains[3],
            biases[3],
            (2 * quarter, 3 * quarter),
            quarter,
            place,
            sources,
            tail_last,
            (gains[4:5], biases[4:5], cotangent_rows),
        )
        gain_four, bias_four = sums_four[0], sums_four[1]
        grad_three, gin_second, gout_second, gain_three, bias_three = ffn_backward_here(
            grad_four,
            half_four,
            stream_three,
            gains[3],
            kept_four,
            (2 * quarter, 3 * quarter),
            quarter,
            place,
            sources,
            ((1, 0),),
        )
    else:
        stream_four, kept_four = ffn_forward(
            stream_three, gains[3], biases[3], in_second, out_second
        )
        stats_last = norm_stats(stream_four)
        result = norm_apply(stream_four, stats_last, gains[4], biases[4]).astype(bf16)
        grad_four, gain_four, bias_four = norm_backward(
            stream_four, stats_last, gains[4], cotangent_rows.astype(f32)
        )
        grad_three, gin_second, gout_second, gain_three, bias_three = ffn_backward(
            grad_four, stream_three, gains[3], kept_four, in_second, out_second
        )

    incoming = grad_three.astype(bf16)
    incoming_three = incoming
    grad_po = None if local else weight_grad(conv_act, incoming)
    conv_slope = conv_sig * (1.0 + normal * (1.0 - conv_sig))
    grad_normal = dot_rows(incoming, p_output) * conv_slope
    own_sums = jnp.stack([jnp.sum(grad_normal, axis=0), jnp.sum(grad_normal * center, axis=0)])
    sums = butterfly_sum(own_sums, "dp")
    block_out = send_home(result)
    if local:
        sums, block_out = lax.optimization_barrier((sums, block_out))
        block_out = finish_hops(*block_out)
    sum_plain, sum_center = sums
    bn_scale = bn_gain * inv_std
    grad_depth = bn_scale * grad_normal - frame_mask * bn_scale * (
        sum_plain + inv_std * inv_std * sum_center * center
    ) / total_count
    grad_glu = jnp.zeros_like(glu)
    tap_grads = []
    for t in range(taps):
        grad_glu = grad_glu + convs[t] * shift_rows(grad_depth, margin - t)
        tap_grads.append(jnp.sum(grad_depth * shift_rows(glu, t - margin), axis=0))
    grad_glu = grad_glu * frame_mask
    grad_linear = (grad_glu * gate_sig).astype(bf16)
    grad_gating = (grad_glu * linear * gate_sig * (1.0 - gate_sig)).astype(bf16)
    if not local:
        grad_pv = weight_grad(grad_linear, conv_in)
        grad_pg = weight_grad(grad_gating, conv_in)
    back, gain_two, bias_two = norm_backward(
        stream_two,
        stats_conv,
        gains[2],
        dot_plain(grad_linear, p_value) + dot_plain(grad_gating, p_gate),
    )
    grad_two = grad_three + back

    incoming = grad_two.astype(bf16)
    grad_wo = None if local else weight_grad(merged, incoming)
    grad_merged = dot_rows(incoming, w_output).astype(bf16)
    if local:
        grad_merged, gin_second, gout_second = lax.optimization_barrier(
            (grad_merged, gin_second, gout_second)
        )
    grad_q, grad_k, grad_v = head_call(
        attend_back_kernel, valid, (queries, keys, values, grad_merged), 3, 10
    )
    if local:
        singles_other, singles_own = single_grads(
            ((0, 0), (1, 0), (2, 0), (3, 1), (4, 2), (5, 2), (6, 3)),
            (grad_q, grad_k, grad_v, merged, grad_linear, grad_gating, conv_act),
            (att_in, incoming, conv_in, incoming_three),
        )
    else:
        grad_wq = weight_grad(grad_q, att_in)
        grad_wk = weight_grad(grad_k, att_in)
        grad_wv = weight_grad(grad_v, att_in)
    back, gain_one, bias_one = norm_backward(
        stream_one,
        stats_att,
        gains[1],
        dot_plain(grad_q, w_query) + dot_plain(grad_k, w_key) + dot_plain(grad_v, w_value),
    )
    grad_one = grad_two + back
    if local:
        grad_one, singles_other = lax.optimization_barrier((grad_one, singles_other))
        singles_other = swap(singles_other, "core")

    if local:
        grad_zero, gin_first, gout_first, gain_zero, bias_zero = ffn_backward_here(
            grad_one,
            (0.5 * grad_one).astype(bf16),
            source,
            gains[0],
            kept_one,
            (0, quarter),
            quarter,
            place,
            sources,
            ((1,), (0,)),
        )
    else:
        grad_zero, gin_first, gout_first, gain_zero, bias_zero = ffn_backward(
            grad_one, source, gains[0], kept_one, in_first, out_first
        )
    block_grad = send_home(grad_zero)

    conv_small = jnp.stack(tap_grads + [own_sums[1] * inv_std, own_sums[0]])
    conv_small = conv_small.reshape(-1, chan_count, rows_tile)[:, position].reshape(-1, width)
    small = jnp.concatenate(
        [
            jnp.stack(
                [gain_zero, gain_one, gain_two, gain_three, gain_four]
                + [bias_zero, bias_one, bias_two, bias_three, bias_four]
            ),
            conv_small,
        ]
    )
    if local:
        small = small + swap(small, "core")
        groups = [(i * quarter, quarter, False) for i in range(4)]
        groups.append((base, tile_count - base, True))
        pairs = [
            tuple(v.reshape(4, quarter, -1, width) for v in pair)
            for pair in (gin_first, gout_first, gin_second, gout_second)
        ]
        shape = (tile_count - base, 4) + pairs[0][0].shape[2:]
        pairs.append((singles_own.reshape(shape), singles_other.reshape(shape)))
        keep, got, small, block_grad = reduce_tiles_here(
            groups, [p[0] for p in pairs], [p[1] for p in pairs], place, slots, small, block_grad
        )
        block_grad = finish_hops(*block_grad)
        tile_m, tile_v, tile_w, tile_b = update_tiles_here(
            keep,
            got,
            owned_mask(tile_slot, slots).astype(jnp.int32),
            master,
            tile_first,
            tile_second,
        )
    else:
        grads = [gin_first, gout_first, gin_second, gout_second]
        grads += [grad_wq, grad_wk, grad_wv, grad_wo, grad_pv, grad_pg, grad_po]
        owned = reduce_tiles(
            jnp.concatenate(grads).reshape(tile_count, width, width), tile_slot, slots
        )
        small = butterfly_sum(butterfly_sum(small, "dp"), "chan")
        owned = jnp.where(owned_mask(tile_slot, slots)[:, None, None], owned, 0.0)
        tile_m, tile_v, tile_w = adamw_step(
            master, owned, tile_first, tile_second, tile_rate, weight_decay
        )
        tile_b = tile_w.astype(bf16)
    norm_total = small[: norm_params.shape[0]]
    conv_grad = lax.dynamic_slice_in_dim(
        small[norm_params.shape[0] :], chan_index * rows_tile, rows_tile, 1
    )

    norm_m, norm_v, norm_w = adamw_step(
        norm_params, norm_total, norm_first, norm_second, small_rate, 0.0
    )
    conv_m, conv_v, conv_w = adamw_step(
        conv_params, conv_grad, conv_first, conv_second, small_rate, 0.0
    )
    return (
        block_out[:, None],
        block_grad[:, None].astype(f32),
        tile_m,
        tile_v,
        tile_w,
        tile_b,
        norm_m,
        norm_v,
        norm_w,
        conv_m,
        conv_v,
        conv_w,
    )


def solution(mesh):
    in_specs = (
        P(None, "dp", "chan", None),
        P(None, "dp", "chan", None),
        P(None, "dp"),
        P(),
        P("dp", "chan", None),
        P("dp", "chan", None),
        P("dp", "chan", None),
        P(),
        P(),
        P(),
        P(None, "chan"),
        P(None, "chan"),
        P(None, "chan"),
    )
    out_specs = (
        P(None, "dp", "chan", None),
        P(None, "dp", "chan", None),
        P("dp", "chan", None),
        P("dp", "chan", None),
        P("dp", "chan", None),
        P("dp", "chan", None),
        P(),
        P(),
        P(),
        P(None, "chan"),
        P(None, "chan"),
        P(None, "chan"),
    )
    return jax.shard_map(shards, mesh=mesh, in_specs=in_specs, out_specs=out_specs, check_vma=False)
```

```python
import jax
import jax.numpy as jnp
from jax import lax
from jax.experimental import pallas as pl
from jax.experimental.pallas import tpu as pltpu
from jax.sharding import PartitionSpec as P

HEAD_DIM = 128
STEP = 10

norm_eps = 1e-05
masked_score = -1e30
beta_one = 0.9
beta_two = 0.98
adam_eps = 1e-08
tile_rate = 0.06
small_rate = 0.6
weight_decay = 0.01

BOTH = ("dp", "chan")
bf16 = jnp.bfloat16
f32 = jnp.float32


def dot_rows(left, right):
    return lax.dot_general(left, right, (((1,), (1,)), ((), ())), preferred_element_type=f32)


def dot_plain(left, right):
    return jnp.dot(left, right, preferred_element_type=f32)


def dot_cols(left, right):
    return lax.dot_general(left, right, (((0,), (0,)), ((), ())), preferred_element_type=f32)


def adamw_step(weight, gradient, first_old, second_old, rate, decay):
    first_new = beta_one * first_old + (1.0 - beta_one) * gradient
    second_new = beta_two * second_old + (1.0 - beta_two) * gradient * gradient
    first_hat = first_new / (1.0 - beta_one**STEP)
    second_hat = second_new / (1.0 - beta_two**STEP)
    weight_new = weight - rate * (first_hat / (jnp.sqrt(second_hat) + adam_eps) + decay * weight)
    return (first_new, second_new, weight_new)


def exchange(value, axis, mask):
    size = lax.axis_size(axis)
    return lax.ppermute(value, axis, [(i, i ^ mask) for i in range(size)])


def swap_blocks(value, axis):
    size = lax.axis_size(axis)
    me = lax.axis_index(axis)
    result = value
    for mask in range(1, size):
        sent = lax.dynamic_index_in_dim(value, me ^ mask, 0, keepdims=True)
        result = lax.dynamic_update_slice_in_dim(result, exchange(sent, axis, mask), me ^ mask, 0)
    return result


def swap_in_hops(value):
    me = lax.axis_index("chan")
    pairs = value.reshape((2, 2) + value.shape[1:])
    core, y = lax.rem(me, 2), lax.div(me, 2)
    keep = lax.dynamic_index_in_dim(pairs, core, 1, keepdims=False)
    sent = lax.dynamic_index_in_dim(pairs, 1 - core, 1, keepdims=False)
    got = exchange(sent, "chan", 1)
    low = jnp.where(core == 0, keep, got)
    high = jnp.where(core == 0, got, keep)
    mixed = jnp.stack([low, high], axis=1)
    there = lax.dynamic_index_in_dim(mixed, 1 - y, 0, keepdims=False)
    here = lax.dynamic_index_in_dim(mixed, y, 0, keepdims=False)
    return here, there


def finish_hops(here, arrived_there):
    y = lax.div(lax.axis_index("chan"), 2)
    low = jnp.where(y == 0, here, arrived_there)
    high = jnp.where(y == 0, arrived_there, here)
    return jnp.concatenate([low, high])


def gather_small(value, axis):
    size = lax.axis_size(axis)
    me = lax.axis_index(axis)
    result = jnp.zeros((size,) + value.shape, value.dtype)
    result = lax.dynamic_update_slice_in_dim(result, value[None], me, 0)
    for mask in range(1, size):
        result = lax.dynamic_update_slice_in_dim(
            result, exchange(value[None], axis, mask), me ^ mask, 0
        )
    return result


def butterfly_sum(value, axis):
    size = lax.axis_size(axis)
    mask = 1
    while mask < size:
        value = value + exchange(value, axis, mask)
        mask *= 2
    return value


BITS = {"core": 1, "y": 2, "x": 4, "z1": 8, "z2": 16}
ORDERS = (
    ("z2", "y", "z1", "x"),
    ("z1", "z2", "y", "x"),
    ("z2", "y", "x", "z1"),
    ("z1", "x", "y", "z2"),
    ("z2", "z1", "x", "y"),
    ("z1", "x", "z2", "y"),
)
LAST = (("x", (0, 1)), ("z1", (2,)), ("z2", (3,)), ("y", (4, 5)))
HALVES = 2


def is_slice(dp_count, chan_count, slots):
    return (dp_count, chan_count, slots) == (8, 4, 3)


def swap(value, name):
    size = lax.axis_size("dp") * lax.axis_size("chan")
    return lax.ppermute(value, BOTH, [(i, i ^ BITS[name]) for i in range(size)])


def step_groups(step, orders):
    groups = {}
    for part, order in enumerate(orders):
        groups.setdefault(order[step], []).append(part)
    return groups


def gather_parts(master, extra, small):
    half = master.shape[1] // HALVES
    own = [master[:, h * half : (h + 1) * half].astype(bf16) for h in range(HALVES)]
    own = lax.optimization_barrier(own)
    state = [own[p % HALVES][p // HALVES][None] for p in range(6)]
    moved = []
    for step in range(4):
        groups = step_groups(step, ORDERS)
        sent = {
            name: (jnp.concatenate([state[p] for p in parts]) if len(parts) > 1 else state[parts[0]])
            for name, parts in groups.items()
        }
        if step == 0:
            sent = {ORDERS[h][0]: own[h] for h in range(HALVES)}
            sent, extra = lax.optimization_barrier((sent, extra))
            moved = [exchange(value, "chan", mask + 1) for mask, value in enumerate(extra)]
        elif step == 1:
            sent, small = lax.optimization_barrier((sent, small))
            small = jnp.stack([small, exchange(small, "chan", 2)])
        elif step == 2:
            sent, small = lax.optimization_barrier((sent, small))
            small = jnp.concatenate([small, exchange(small, "chan", 1)])
        else:
            sent = lax.optimization_barrier(sent)
        got = {name: swap(value, name) for name, value in sent.items()}
        if step == 3:
            return ([sent[n] for n, _ in LAST], [got[n] for n, _ in LAST], moved, small)
        got, moved, small = lax.optimization_barrier((got, moved, small))
        size = 1 << step
        for name, parts in groups.items():
            for i, p in enumerate(parts):
                state[p] = jnp.concatenate([state[p], got[name][i * size : (i + 1) * size]])


def place_of(part, bits):
    order = ORDERS[part]
    index = bits[order[2]] * 4 + bits[order[1]] * 2 + bits[order[0]]
    for _, parts in LAST:
        if part in parts:
            return (bits[order[3]], index + 8 * parts.index(part))


def array_of(position, h):
    part = position * HALVES + h
    return [i for i, (_, parts) in enumerate(LAST) if part in parts][0]


def slot_places(slot, slots):
    owner, position = slot // slots, slot % slots
    gap = owner ^ lax.axis_index("dp")
    bits = {"x": gap & 1, "z1": (gap >> 1) & 1, "z2": (gap >> 2) & 1}
    rows = []
    for dy in range(2):
        for h in range(HALVES):
            codes = []
            for s in range(slots):
                far, index = place_of(s * HALVES + h, dict(bits, y=jnp.full_like(gap, dy)))
                codes.append((far * 4 + array_of(s, h)) * 16 + index)
            rows.append(jnp.select([position == s for s in range(slots)], codes))
    return jnp.stack(rows).astype(jnp.int32)


def at_place(place, arrays, act):
    which, index = lax.div(place, 16), lax.rem(place, 16)
    for i, array in enumerate(arrays):

        @pl.when(which == i)
        def _():
            act(array, index)


def staged(count, depth, load, drain_in, store, drain_out):
    ahead = depth // 2
    for i in range(count + ahead):
        if i < count:
            if i >= depth:
                drain_out(i - depth)
            load(i)
        if i >= ahead:
            drain_in(i - ahead)
            store(i - ahead)
    for i in range(max(count - depth, 0), count):
        drain_out(i)


DEPTH = 8


SOURCES = 13


def sixteen(refs):
    near, at = [], 0
    for _, parts in LAST:
        near.append(refs[8].at[pl.ds(at, 8 * len(parts))])
        at += 8 * len(parts)
    return list(refs[:8]) + near + list(refs[9:SOURCES])


def assemble_kernel(first, place_ref, *refs):
    sources, outs = sixteen(refs), refs[SOURCES:-3]
    buffer, in_sem, out_sem = refs[-3:]
    items = [(core, g) for core in range(2) for g in range(len(outs))]

    def load(i):
        core, g = items[i]
        for b in range(4):
            at_place(
                place_ref[b, first + g],
                sources[core * 8 : core * 8 + 8],
                lambda array, index: pltpu.make_async_copy(
                    array.at[index], buffer.at[i % DEPTH, b], in_sem.at[i % DEPTH]
                ).start(),
            )

    def drain_in(i):
        slot = buffer.at[i % DEPTH]
        pltpu.make_async_copy(slot, slot, in_sem.at[i % DEPTH]).wait()

    def out_copy(i):
        core, g = items[i]
        return pltpu.make_async_copy(buffer.at[i % DEPTH], outs[g].at[core], out_sem.at[i % DEPTH])

    staged(
        len(items), DEPTH, load, drain_in, lambda i: out_copy(i).start(), lambda i: out_copy(i).wait()
    )


ANYWHERE = pl.BlockSpec(memory_space=pl.ANY)
IN_SMEM = pl.BlockSpec(memory_space=pltpu.SMEM)
IN_VMEM = pl.BlockSpec(memory_space=pltpu.VMEM)


def assemble(place, sources, first, count):
    rows, width = sources[0].shape[1:]
    mats = pl.pallas_call(
        lambda *refs: assemble_kernel(first, *refs),
        in_specs=[IN_SMEM] + [ANYWHERE] * SOURCES,
        out_specs=[ANYWHERE] * count,
        out_shape=[jax.ShapeDtypeStruct((2, 4, rows, width), bf16)] * count,
        scratch_shapes=[
            pltpu.VMEM((DEPTH, 4, rows, width), bf16),
            pltpu.SemaphoreType.DMA((DEPTH,)),
            pltpu.SemaphoreType.DMA((DEPTH,)),
        ],
        compiler_params=pltpu.CompilerParams(vmem_limit_bytes=12 * 1024 * 1024),
        cost_estimate=pl.CostEstimate(
            flops=0, bytes_accessed=count * 32 * rows * width, transcendentals=0
        ),
    )(place, *sources)
    return [m.reshape(-1, width) for m in mats]


def gather_sources(master, extra, small):
    near, far, moved, small = gather_parts(master, extra, small)
    near_other = swap(jnp.concatenate(near), "core")
    far_other = [swap(v, "core") for v in far]
    return near + far + [near_other] + far_other, moved, small


BPS = 2
STEPS = 4 // BPS


def fetch_rows(at, item, firsts, count, place_ref, sources, buffers, sems):
    core, step = item
    rows = sources[0].shape[1]
    for m, first in enumerate(firsts):
        for i in range(BPS):
            for j in range(count):
                at_place(
                    place_ref[step * BPS + i, first + j],
                    sources[core * 8 : core * 8 + 8],
                    lambda array, index: pltpu.make_async_copy(
                        array.at[index],
                        buffers[m].at[at, pl.ds((i * count + j) * rows, rows)],
                        sems.at[m, at],
                    ).start(),
                )


def arrived(m, at, buffers, sems):
    pltpu.make_async_copy(buffers[m].at[at], buffers[m].at[at], sems.at[m, at]).wait()
    return buffers[m][at]


def tail_next(out_ref, ins, outs):
    gain_ref, bias_ref = ins
    next_ref, stats_ref = outs
    lanes = stats_ref.shape[1] // 2
    for r in range(4):
        rows = pl.ds(r * (out_ref.shape[0] // 4), out_ref.shape[0] // 4)
        stream = out_ref[rows, :]
        mean, inv = norm_stats(stream)
        next_ref[rows, :] = norm_apply(
            stream, (mean, inv), gain_ref[...], bias_ref[...]
        ).astype(bf16)
        stats_ref[rows, :lanes] = jnp.broadcast_to(mean, (stream.shape[0], lanes))
        stats_ref[rows, lanes:] = jnp.broadcast_to(inv, (stream.shape[0], lanes))


def tail_last(out_ref, ins, outs):
    gain_ref, bias_ref, up_ref = ins
    result_ref, grad_ref, half_ref, sums_ref = outs
    for r in range(4):
        rows = pl.ds(r * (out_ref.shape[0] // 4), out_ref.shape[0] // 4)
        stream, upstream = out_ref[rows, :], up_ref[rows, :].astype(f32)
        stats = norm_stats(stream)
        result_ref[rows, :] = norm_apply(stream, stats, gain_ref[...], bias_ref[...]).astype(bf16)
        back, grad_gain, grad_bias = norm_backward(stream, stats, gain_ref[...], upstream)
        grad_ref[rows, :] = back
        half_ref[rows, :] = (0.5 * back).astype(bf16)
        sums = jnp.concatenate([grad_gain[None], grad_bias[None]])
        sums_ref[...] = sums if r == 0 else sums_ref[...] + sums


def ffn_kernel(firsts, count, tail, tail_ins, place_ref, normed_ref, base_ref, *refs):
    ins, refs = refs[:tail_ins], refs[tail_ins:]
    sources = sixteen(refs)
    out_ref, act_ref, slope_ref = refs[SOURCES : SOURCES + 3]
    outs, (in_buf, out_buf, sems) = refs[SOURCES + 3 : -3], refs[-3:]
    buffers = (in_buf, out_buf)
    size = in_buf.shape[1]
    items = [(core, q) for core in range(2) for q in range(STEPS)]
    for i in range(2):
        fetch_rows(i, items[i], firsts, count, place_ref, sources, buffers, sems)
    for i, (core, q) in enumerate(items):
        cut = slice(i * size, (i + 1) * size)
        hidden = dot_rows(normed_ref[...], arrived(0, i % 2, buffers, sems))
        sig = jax.nn.sigmoid(hidden)
        active = (hidden * sig).astype(bf16)
        act_ref[:, cut] = active
        slope_ref[:, cut] = (sig * (1.0 + hidden * (1.0 - sig))).astype(bf16)
        before = base_ref[...] if i == 0 else out_ref[...]
        out_ref[...] = before + 0.5 * dot_plain(active, arrived(1, i % 2, buffers, sems))
        if i + 2 < len(items):
            fetch_rows(i % 2, items[i + 2], firsts, count, place_ref, sources, buffers, sems)
    tail(out_ref, ins, outs)


def ffn_back_kernel(cores, based, firsts, count, place_ref, e_ref, act_ref, slope_ref, normed_ref, *refs):
    base_ref, refs = (refs[0], refs[1:]) if based else (None, refs)
    sources, refs = sixteen(refs), refs[SOURCES:]
    dx_ref, grads, refs = refs[0], refs[1 : 1 + 2 * len(cores)], refs[1 + 2 * len(cores) :]
    in_grads, out_grads, put_sems, in_buf, out_buf, sems = refs
    buffers = (in_buf, out_buf)
    size = in_buf.shape[1]
    items = [(core, q) for core in cores for q in range(STEPS)]
    for i in range(2):
        fetch_rows(i, items[i], firsts, count, place_ref, sources, buffers, sems)

    def copy(m, i):
        core, q = items[i]
        target = grads[2 * cores.index(core) + m].at[pl.ds(q * size, size)]
        buffer = (in_grads, out_grads)[m]
        return pltpu.make_async_copy(buffer.at[i % 2], target, put_sems.at[m, i % 2])

    for i, (core, q) in enumerate(items):
        cut = slice((core * STEPS + q) * size, (core * STEPS + q + 1) * size)
        incoming = e_ref[...]
        grad = dot_rows(incoming, arrived(1, i % 2, buffers, sems)) * slope_ref[:, cut].astype(f32)
        grad = grad.astype(bf16)
        change = dot_plain(grad, arrived(0, i % 2, buffers, sems))
        if i + 2 < len(items):
            fetch_rows(i % 2, items[i + 2], firsts, count, place_ref, sources, buffers, sems)
        if i > 0:
            dx_ref[...] += change
        elif based:
            dx_ref[...] = base_ref[...] + change
        else:
            dx_ref[...] = change
        if i >= 2:
            copy(1, i - 2).wait()
        out_grads[i % 2] = dot_cols(act_ref[:, cut], incoming).astype(bf16)
        copy(1, i).start()
        if i >= 2:
            copy(0, i - 2).wait()
        in_grads[i % 2] = dot_cols(grad, normed_ref[...]).astype(bf16)
        copy(0, i).start()
    for i in range(len(items) - 2, len(items)):
        for m in range(2):
            copy(m, i).wait()


def grads_kernel(pairs, lefts, rights, *refs):
    left_refs, right_refs = refs[:lefts], refs[lefts : lefts + rights]
    other, own, buffer, sems = refs[lefts + rights :]
    half = own.shape[1]
    for k, (i, j) in enumerate(pairs):
        slot = k % 2
        if k >= 2:
            pltpu.make_async_copy(buffer.at[slot], buffer.at[slot], sems.at[slot]).wait()
        buffer[slot] = dot_cols(left_refs[i][...], right_refs[j][...]).astype(bf16)
        pltpu.make_async_copy(buffer.at[slot, pl.ds(0, half)], own.at[k], sems.at[slot]).start()
        pltpu.make_async_copy(buffer.at[slot, pl.ds(half, half)], other.at[k], sems.at[slot]).start()
    for slot in range(2):
        pltpu.make_async_copy(buffer.at[slot], buffer.at[slot], sems.at[slot]).wait()


def single_grads(pairs, lefts, rights):
    rows, width = lefts[0].shape
    shape = jax.ShapeDtypeStruct((len(pairs), width // 2, width), bf16)
    return pl.pallas_call(
        lambda *refs: grads_kernel(pairs, len(lefts), len(rights), *refs),
        in_specs=[IN_VMEM] * (len(lefts) + len(rights)),
        out_specs=[ANYWHERE] * 2,
        out_shape=[shape] * 2,
        scratch_shapes=[pltpu.VMEM((2, width, width), bf16), pltpu.SemaphoreType.DMA((2,))],
        compiler_params=pltpu.CompilerParams(vmem_limit_bytes=24 * 1024 * 1024),
        cost_estimate=pl.CostEstimate(
            flops=2 * len(pairs) * rows * width * width,
            bytes_accessed=2 * len(pairs) * width * (width + 2 * rows),
            transcendentals=0,
        ),
    )(*lefts, *rights)


def ffn_scratch(count, rows, width):
    return [
        pltpu.VMEM((2, BPS * count * rows, width), bf16),
        pltpu.VMEM((2, BPS * count * rows, width), bf16),
        pltpu.SemaphoreType.DMA((2, 2)),
    ]


LANES = 128


def ffn_forward_here(stream, gain, bias, firsts, count, place, sources, tail, tail_ins):
    rows, width = stream.shape
    block = sources[0].shape[1]
    hidden = 8 * count * block
    shape = jax.ShapeDtypeStruct
    stats = norm_stats(stream)
    normed = norm_apply(stream, stats, gain, bias).astype(bf16)
    if tail is tail_next:
        more = [shape((rows, width), bf16), shape((rows, 2 * LANES), f32)]
    else:
        more = [
            shape((rows, width), bf16),
            shape((rows, width), f32),
            shape((rows, width), bf16),
            shape((2, width), f32),
        ]
    result, active, slope, *more = pl.pallas_call(
        lambda *refs: ffn_kernel(firsts, count, tail, len(tail_ins), *refs),
        in_specs=[IN_SMEM] + [IN_VMEM] * (2 + len(tail_ins)) + [ANYWHERE] * SOURCES,
        out_specs=[IN_VMEM] * (3 + len(more)),
        out_shape=[
            shape((rows, width), f32),
            shape((rows, hidden), bf16),
            shape((rows, hidden), bf16),
        ]
        + more,
        scratch_shapes=ffn_scratch(count, block, width),
        compiler_params=pltpu.CompilerParams(vmem_limit_bytes=FORWARD_MB * 1024 * 1024),
        cost_estimate=pl.CostEstimate(
            flops=4 * rows * width * hidden,
            bytes_accessed=4 * hidden * (width + rows),
            transcendentals=rows * hidden,
        ),
    )(place, normed, stream, *tail_ins, *sources)
    return (result, (stats, normed, active, slope), more)


FORWARD_MB = 28
BACKWARD_MB = 36


def ffn_backward_here(
    upstream, incoming, stream, gain, kept, firsts, count, place, sources, calls
):
    stats, normed, active, slope = kept
    rows, width = stream.shape
    block = sources[0].shape[1]
    half = 4 * count * block
    size = BPS * count * block
    shape = jax.ShapeDtypeStruct
    base, grads = [], []
    for cores in calls:
        dx, *some = pl.pallas_call(
            lambda *refs, cores=cores: ffn_back_kernel(cores, bool(base), firsts, count, *refs),
            in_specs=[IN_SMEM] + [IN_VMEM] * (4 + len(base)) + [ANYWHERE] * SOURCES,
            out_specs=[IN_VMEM] + [ANYWHERE] * (2 * len(cores)),
            out_shape=[shape((rows, width), f32)]
            + [shape((half, width), bf16)] * (2 * len(cores)),
            scratch_shapes=[
                pltpu.VMEM((2, size, width), bf16),
                pltpu.VMEM((2, size, width), bf16),
                pltpu.SemaphoreType.DMA((2, 2)),
            ]
            + ffn_scratch(count, block, width),
            compiler_params=pltpu.CompilerParams(vmem_limit_bytes=BACKWARD_MB * 1024 * 1024),
            cost_estimate=pl.CostEstimate(
                flops=8 * rows * width * half * len(cores),
                bytes_accessed=8 * half * (width + rows) * len(cores),
                transcendentals=0,
            ),
        )(place, incoming, active, slope, normed, *base, *sources)
        base = [dx]
        if not grads:
            some = [swap(v, "core") for v in some[:2]] + some[2:]
        grads += some
    other_in, other_out, own_in, own_out = grads
    back, grad_gain, grad_bias = norm_backward(stream, stats, gain, dx)
    return (upstream + back, (own_in, other_in), (own_out, other_out), grad_gain, grad_bias)


SCATTER = 6


def scatter_kernel(groups, place_ref, *refs):
    owns, others = refs[: len(groups)], refs[len(groups) : 2 * len(groups)]
    outs = refs[2 * len(groups) : 2 * len(groups) + 8]
    own_buf, other_buf, in_sem, out_sem = refs[2 * len(groups) + 8 :]
    items = []
    for g, (first, count, whole) in enumerate(groups):
        if whole:
            items += [(g, k, [(b, first + k) for b in range(4)]) for k in range(count)]
        else:
            items += [(g, b, [(b, first + j) for j in range(count)]) for b in range(4)]

    def in_copies(i):
        g, k, _ = items[i]
        slot = i % SCATTER
        return (
            pltpu.make_async_copy(owns[g].at[k], own_buf.at[slot], in_sem.at[0, slot]),
            pltpu.make_async_copy(others[g].at[k], other_buf.at[slot], in_sem.at[1, slot]),
        )

    def load(i):
        for copy in in_copies(i):
            copy.start()

    def drain_in(i):
        for copy in in_copies(i):
            copy.wait()

    def store(i):
        slot = i % SCATTER
        own_buf[slot] = (own_buf[slot].astype(f32) + other_buf[slot].astype(f32)).astype(bf16)
        for at, (b, tile) in enumerate(items[i][2]):
            at_place(
                place_ref[b, tile],
                outs,
                lambda array, index: pltpu.make_async_copy(
                    own_buf.at[slot, at], array.at[index], out_sem.at[slot]
                ).start(),
            )

    def drain_out(i):
        slot = own_buf.at[i % SCATTER]
        pltpu.make_async_copy(slot, slot, out_sem.at[i % SCATTER]).wait()

    staged(len(items), SCATTER, load, drain_in, store, drain_out)


def combine_kernel(plan, count, *refs):
    keeps, gots, outs = refs[:count], refs[count : 2 * count], refs[2 * count :]
    rows = 16

    def body(r, carry):
        cut = pl.ds(pl.multiple_of(r * rows, rows), rows)
        for out, at, array, index in plan:
            total = keeps[array][index, cut, :].astype(f32) + gots[array][index, cut, :].astype(f32)
            outs[out][at, cut, :] = total.astype(bf16)
        return carry

    lax.fori_loop(0, keeps[0].shape[1] // rows, body, 0)


def combine(step, keep, got):
    before, now = step_groups(step + 1, ORDERS), step_groups(step, ORDERS)
    size = 1 << step
    lies = {
        p: (a, 2 * i * size)
        for a, parts in enumerate(before.values())
        for i, p in enumerate(parts)
    }
    plan, shapes = [], []
    for half in (1, 0):
        for parts in now.values():
            for i, p in enumerate(parts):
                array, first = lies[p]
                plan += [
                    (len(shapes), i * size + k, array, first + half * size + k)
                    for k in range(size)
                ]
            some = next(iter(keep.values()))
            shapes.append(jax.ShapeDtypeStruct((size * len(parts),) + some.shape[1:], bf16))
    blocks = sum(s.shape[0] for s in shapes)
    outs = pl.pallas_call(
        lambda *refs: combine_kernel(plan, len(before), *refs),
        in_specs=[IN_VMEM] * (2 * len(before)),
        out_specs=[IN_VMEM] * len(shapes),
        out_shape=shapes,
        compiler_params=pltpu.CompilerParams(
            vmem_limit_bytes=(3 * blocks * 2 * some.shape[1] * some.shape[2]) + (4 << 20)
        ),
        cost_estimate=pl.CostEstimate(
            flops=blocks * some.shape[1] * some.shape[2],
            bytes_accessed=6 * blocks * some.shape[1] * some.shape[2],
            transcendentals=0,
        ),
    )(*[keep[n] for n in before], *[got[n] for n in before])
    return dict(zip(now, outs[: len(now)])), dict(zip(now, outs[len(now) :]))


def reduce_tiles_here(groups, owns, others, place, slots, small, ahead):
    rows, width = owns[0].shape[2:]
    shapes = [jax.ShapeDtypeStruct((8 * len(parts), rows, width), bf16) for _, parts in LAST]
    arrays = pl.pallas_call(
        lambda *refs: scatter_kernel(groups, *refs),
        in_specs=[IN_SMEM] + [ANYWHERE] * (2 * len(groups)),
        out_specs=[ANYWHERE] * 8,
        out_shape=shapes + shapes,
        scratch_shapes=[
            pltpu.VMEM((SCATTER, 4, rows, width), bf16),
            pltpu.VMEM((SCATTER, 4, rows, width), bf16),
            pltpu.SemaphoreType.DMA((2, SCATTER)),
            pltpu.SemaphoreType.DMA((SCATTER,)),
        ],
        compiler_params=pltpu.CompilerParams(vmem_limit_bytes=32 * 1024 * 1024),
        cost_estimate=pl.CostEstimate(
            flops=0, bytes_accessed=6 * 92 * rows * width, transcendentals=0
        ),
    )(place, *owns, *others)
    arrays, ahead = lax.optimization_barrier((arrays, ahead))
    keep = {n: a for (n, _), a in zip(LAST, arrays[:4])}
    send = {n: a for (n, _), a in zip(LAST, arrays[4:])}
    for step in range(3, -1, -1):
        if step == 2:
            size = 1 << step
            state = {}
            for name, parts in step_groups(step + 1, ORDERS).items():
                for i, p in enumerate(parts):
                    cut = slice(2 * i * size, 2 * (i + 1) * size)
                    state[p] = keep[name][cut].astype(f32) + got[name][cut].astype(f32)
            halves = []
            for cut in (slice(size, None), slice(0, size)):
                halves.append(
                    {
                        name: jnp.concatenate([state[p][cut] for p in parts]).astype(bf16)
                        for name, parts in step_groups(step, ORDERS).items()
                    }
                )
            send, keep = halves
        elif step < 2:
            send, keep = combine(step, keep, got)
        send, small = lax.optimization_barrier((send, small))
        got = {name: swap(value, name) for name, value in send.items()}
        small = small + swap(small, ("z2", "z1", "x", "y")[step])
        got, small = lax.optimization_barrier((got, small))
    order = step_groups(0, ORDERS)
    return [keep[n] for n in order], [got[n] for n in order], small, ahead


def update_kernel(filled_ref, k0, g0, k1, g1, w_ref, m_ref, v_ref, m_new, v_new, w_new, b_new):
    half = pl.program_id(1)
    first = k0[...].astype(f32) + g0[...].astype(f32)
    second = k1[...].astype(f32) + g1[...].astype(f32)
    gradient = jnp.where(half == 0, first, second)
    gradient = jnp.where(filled_ref[pl.program_id(0)] > 0, gradient, 0.0)
    moment, square, weight = adamw_step(
        w_ref[...], gradient, m_ref[...], v_ref[...], tile_rate, weight_decay
    )
    m_new[...], v_new[...], w_new[...] = moment, square, weight
    b_new[...] = weight.astype(bf16)


def update_tiles_here(keep, got, filled, master, tile_first, tile_second):
    slots, full, width = master.shape
    rows = full // HALVES
    part = pl.BlockSpec((1, rows, width), lambda s, h: (s, 0, 0))
    here = pl.BlockSpec((1, rows, width), lambda s, h: (s, h, 0))
    shape = jax.ShapeDtypeStruct(master.shape, f32)
    return pl.pallas_call(
        update_kernel,
        grid=(slots, HALVES),
        in_specs=[IN_SMEM] + [part] * 4 + [here] * 3,
        out_specs=[here] * 4,
        out_shape=[shape] * 3 + [jax.ShapeDtypeStruct(master.shape, bf16)],
        compiler_params=pltpu.CompilerParams(vmem_limit_bytes=16 * 1024 * 1024),
        cost_estimate=pl.CostEstimate(
            flops=20 * slots * full * width,
            bytes_accessed=30 * slots * full * width,
            transcendentals=slots * full * width,
        ),
    )(filled, keep[0], got[0], keep[1], got[1], master, tile_first, tile_second)


def owned_mask(tile_slot, slots):
    slot = lax.axis_index("dp") * slots + jnp.arange(slots, dtype=jnp.int32)
    return jnp.any(slot[:, None] == tile_slot[None, :], axis=1)


def gather_tiles(own, tile_slot, sizes):
    width = own.shape[2]
    strips = lax.all_gather(own, "dp", axis=0, tiled=True)
    strips = strips.at[tile_slot].get(mode="promise_in_bounds")
    whole = lax.all_gather(strips, "chan", axis=1, tiled=True)
    mats, first = [], 0
    for n in sizes:
        mats.append(whole[first : first + n].reshape(-1, width))
        first += n
    return mats


def reduce_tiles(grads, tile_slot, slots):
    slot = jnp.arange(lax.axis_size("dp") * slots, dtype=jnp.int32)
    tile_of = jnp.argmax(slot[:, None] == tile_slot[None, :], axis=1).astype(jnp.int32)
    strips = lax.psum_scatter(grads, "chan", scatter_dimension=1, tiled=True)
    placed = strips.at[tile_of].get(mode="promise_in_bounds")
    return lax.psum_scatter(placed, "dp", scatter_dimension=0, tiled=True).astype(f32)


def norm_stats(stream):
    mean = jnp.mean(stream, axis=-1, keepdims=True)
    center = stream - mean
    spread = jnp.mean(center * center, axis=-1, keepdims=True)
    return (mean, lax.rsqrt(spread + norm_eps))


def norm_apply(stream, stats, gain, bias):
    mean, inv = stats
    return (stream - mean) * inv * gain + bias


def norm_backward(stream, stats, gain, upstream):
    mean, inv = stats
    hat = (stream - mean) * inv
    scaled = upstream * gain
    back = (
        scaled
        - jnp.mean(scaled, axis=-1, keepdims=True)
        - hat * jnp.mean(scaled * hat, axis=-1, keepdims=True)
    ) * inv
    return (back, jnp.sum(upstream * hat, axis=0), jnp.sum(upstream, axis=0))


def masked_probs(query, key, valid):
    scores = dot_rows(query, key) * HEAD_DIM ** (-0.5)
    column = lax.broadcasted_iota(jnp.int32, (1, scores.shape[1]), 1)
    scores = jnp.where(column < valid, scores, masked_score)
    exponent = jnp.exp(scores - jnp.max(scores, axis=-1, keepdims=True))
    return exponent, 1.0 / jnp.sum(exponent, axis=-1, keepdims=True)


TOGETHER = 4


def attend_kernel(valid_ref, q_ref, k_ref, v_ref, out_ref):
    for i in range(TOGETHER):
        cut = slice(i * HEAD_DIM, (i + 1) * HEAD_DIM)
        exponent, inverse = masked_probs(q_ref[:, cut], k_ref[:, cut], valid_ref[0])
        probs = (exponent * inverse).astype(bf16)
        out_ref[:, cut] = dot_plain(probs, v_ref[:, cut]).astype(bf16)


def attend_back_kernel(valid_ref, q_ref, k_ref, v_ref, g_ref, dq_ref, dk_ref, dv_ref):
    scale = HEAD_DIM ** (-0.5)
    for i in range(TOGETHER):
        cut = slice(i * HEAD_DIM, (i + 1) * HEAD_DIM)
        query, key, grad = q_ref[:, cut], k_ref[:, cut], g_ref[:, cut]
        exponent, inverse = masked_probs(query, key, valid_ref[0])
        probs = exponent * inverse
        grad_probs = dot_rows(grad, v_ref[:, cut])
        row_dot = jnp.sum(probs * grad_probs, axis=-1, keepdims=True)
        grad_scores = (probs * (grad_probs - row_dot)).astype(bf16)
        dq_ref[:, cut] = (dot_plain(grad_scores, key) * scale).astype(bf16)
        dk_ref[:, cut] = (dot_cols(grad_scores, query) * scale).astype(bf16)
        dv_ref[:, cut] = dot_cols(probs.astype(bf16), grad).astype(bf16)


def head_call(kernel, valid, operands, out_count, flops):
    rows, width = operands[0].shape
    spec = pl.BlockSpec((rows, TOGETHER * HEAD_DIM), lambda h: (0, h))
    shape = jax.ShapeDtypeStruct((rows, width), bf16)
    return pl.pallas_call(
        kernel,
        grid=(width // HEAD_DIM // TOGETHER,),
        in_specs=[IN_SMEM] + [spec] * len(operands),
        out_specs=[spec] * out_count,
        out_shape=[shape] * out_count,
        cost_estimate=pl.CostEstimate(
            flops=flops * rows * rows * width,
            bytes_accessed=2 * rows * width * (len(operands) + out_count),
            transcendentals=rows * rows * width // HEAD_DIM,
        ),
        compiler_params=pltpu.CompilerParams(vmem_limit_bytes=24 * 1024 * 1024),
    )(valid, *operands)


def ffn_forward(stream, gain, bias, w_in, w_out):
    stats = norm_stats(stream)
    normed = norm_apply(stream, stats, gain, bias).astype(bf16)
    hidden = dot_rows(normed, w_in)
    sig = jax.nn.sigmoid(hidden)
    active = (hidden * sig).astype(bf16)
    slope = (sig * (1.0 + hidden * (1.0 - sig))).astype(bf16)
    return (stream + 0.5 * dot_plain(active, w_out), (stats, normed, active, slope))


def weight_grad(left, right):
    return dot_cols(left, right).astype(bf16)


def ffn_backward(upstream, stream, gain, kept, w_in, w_out):
    stats, normed, active, slope = kept
    incoming = (0.5 * upstream).astype(bf16)
    grad_out = weight_grad(active, incoming)
    grad_hidden = (dot_rows(incoming, w_out) * slope.astype(f32)).astype(bf16)
    grad_in = weight_grad(grad_hidden, normed)
    back, grad_gain, grad_bias = norm_backward(stream, stats, gain, dot_plain(grad_hidden, w_in))
    return (upstream + back, grad_in, grad_out, grad_gain, grad_bias)


def shift_rows(value, offset):
    rows = value.shape[0]
    if offset == 0:
        return value
    if offset > 0:
        return jnp.pad(value[offset:], ((0, offset), (0, 0)))
    return jnp.pad(value[: rows + offset], ((-offset, 0), (0, 0)))


def merge_stats(one, two):
    count_a, mean_a, dev_a = one
    count_b, mean_b, dev_b = two
    count = count_a + count_b
    mean = (count_a * mean_a + count_b * mean_b) / count
    gap = mean_a - mean_b
    return (count, mean, dev_a + dev_b + gap * gap * (count_a * count_b / count))


def shards(
    inputs,
    cotangent,
    lengths,
    tile_slot,
    master,
    tile_first,
    tile_second,
    norm_params,
    norm_first,
    norm_second,
    conv_params,
    conv_first,
    conv_second,
):
    micro, _, seg_rows, width = inputs.shape
    slots, rows_tile, _ = master.shape
    chan_count, dp_count = lax.axis_size("chan"), lax.axis_size("dp")
    chan_index = lax.axis_index("chan")
    assert micro == chan_count
    rows = seg_rows * chan_count
    tile_count = tile_slot.shape[0]
    quarter = (tile_count - 7) // 4
    base = 4 * quarter

    sizes = (quarter,) * 4 + (1,) * 7
    local = is_slice(dp_count, chan_count, slots)
    both = jnp.stack([inputs[:, 0], cotangent[:, 0]], axis=1)
    mine = both
    if local:
        extra = [
            lax.dynamic_index_in_dim(both, chan_index ^ mask, 0, keepdims=True)
            for mask in range(1, chan_count)
        ]
        sources, moved, convs = gather_sources(master, extra, conv_params)
        place = slot_places(tile_slot, slots)
        mats = [None] * tile_count
        for mask in range(1, chan_count):
            mine = lax.dynamic_update_slice_in_dim(mine, moved[mask - 1], chan_index ^ mask, 0)
        near = jnp.array([0, 2, 1, 3], jnp.int32)
        position = near[jnp.arange(chan_count, dtype=jnp.int32) ^ chan_index]
    else:
        mats = gather_tiles(master.astype(bf16), tile_slot, sizes)
        mine = swap_blocks(both, "chan")
        convs = gather_small(conv_params, "chan")
        position = jnp.arange(chan_count, dtype=jnp.int32)
    source = mine[:, 0].reshape(rows, width).astype(f32)
    cotangent_rows = mine[:, 1].reshape(rows, width)
    convs = jnp.moveaxis(convs, 0, 1).reshape(-1, width)
    valid = lax.dynamic_slice_in_dim(lengths[:, 0], chan_index, 1)
    in_first, out_first, in_second, out_second = mats[:4]
    gains, biases = norm_params[:5], norm_params[5:]
    taps = convs.shape[0] - 2
    margin = (taps - 1) // 2
    bn_gain, bn_bias = convs[taps], convs[taps + 1]
    frame_mask = (jnp.arange(rows, dtype=jnp.int32) < valid[0]).astype(f32)[:, None]

    def send_home(value):
        value = value.astype(bf16).reshape(chan_count, seg_rows, width)
        if not local:
            return swap_blocks(value, "chan")
        here, there = swap_in_hops(value)
        return (here, exchange(there, "chan", 2))

    if local:
        stream_one, kept_one, (att_in, stats_att) = ffn_forward_here(
            source,
            gains[0],
            biases[0],
            (0, quarter),
            quarter,
            place,
            sources,
            tail_next,
            (gains[1:2], biases[1:2]),
        )
        stats_att = (stats_att[:, :1], stats_att[:, LANES : LANES + 1])
        stream_one, place_after = lax.optimization_barrier((stream_one, place))
        mats[4:] = assemble(place_after, sources, base, tile_count - base)
    else:
        stream_one, kept_one = ffn_forward(source, gains[0], biases[0], in_first, out_first)
        stats_att = norm_stats(stream_one)
        att_in = norm_apply(stream_one, stats_att, gains[1], biases[1]).astype(bf16)
    w_query, w_key, w_value, w_output, p_value, p_gate, p_output = mats[4:]
    queries = dot_rows(att_in, w_query).astype(bf16)
    keys = dot_rows(att_in, w_key).astype(bf16)
    values = dot_rows(att_in, w_value).astype(bf16)
    (merged,) = head_call(attend_kernel, valid, (queries, keys, values), 1, 4)
    stream_two = stream_one + dot_plain(merged, w_output)

    stats_conv = norm_stats(stream_two)
    conv_in = norm_apply(stream_two, stats_conv, gains[2], biases[2]).astype(bf16)
    linear = dot_rows(conv_in, p_value)
    gate_sig = jax.nn.sigmoid(dot_rows(conv_in, p_gate))
    glu = linear * gate_sig * frame_mask
    depth = jnp.zeros_like(glu)
    for t in range(taps):
        depth = depth + convs[t] * shift_rows(glu, t - margin)
    count = valid[0].astype(f32)
    local_mean = jnp.sum(depth * frame_mask, axis=0) / count
    local_gap = (depth - local_mean) * frame_mask
    local_dev = jnp.sum(local_gap * local_gap, axis=0)
    stats = (jnp.full((width,), count), local_mean, local_dev)
    mask = 1
    while mask < dp_count:
        other = exchange(jnp.stack(stats), "dp", mask)
        stats = merge_stats(stats, (other[0], other[1], other[2]))
        mask *= 2
    total_count, bn_mean, bn_dev = stats
    inv_std = lax.rsqrt(bn_dev / total_count + norm_eps)
    center = depth - bn_mean
    normal = center * inv_std * bn_gain + bn_bias
    conv_sig = jax.nn.sigmoid(normal)
    conv_act = (normal * conv_sig).astype(bf16)
    stream_three = stream_two + dot_plain(conv_act, p_output)

    if local:
        _, kept_four, (result, grad_four, half_four, sums_four) = ffn_forward_here(
            stream_three,
            gains[3],
            biases[3],
            (2 * quarter, 3 * quarter),
            quarter,
            place,
            sources,
            tail_last,
            (gains[4:5], biases[4:5], cotangent_rows),
        )
        gain_four, bias_four = sums_four[0], sums_four[1]
        grad_three, gin_second, gout_second, gain_three, bias_three = ffn_backward_here(
            grad_four,
            half_four,
            stream_three,
            gains[3],
            kept_four,
            (2 * quarter, 3 * quarter),
            quarter,
            place,
            sources,
            ((1, 0),),
        )
    else:
        stream_four, kept_four = ffn_forward(
            stream_three, gains[3], biases[3], in_second, out_second
        )
        stats_last = norm_stats(stream_four)
        result = norm_apply(stream_four, stats_last, gains[4], biases[4]).astype(bf16)
        grad_four, gain_four, bias_four = norm_backward(
            stream_four, stats_last, gains[4], cotangent_rows.astype(f32)
        )
        grad_three, gin_second, gout_second, gain_three, bias_three = ffn_backward(
            grad_four, stream_three, gains[3], kept_four, in_second, out_second
        )

    incoming = grad_three.astype(bf16)
    incoming_three = incoming
    grad_po = None if local else weight_grad(conv_act, incoming)
    conv_slope = conv_sig * (1.0 + normal * (1.0 - conv_sig))
    grad_normal = dot_rows(incoming, p_output) * conv_slope
    own_sums = jnp.stack([jnp.sum(grad_normal, axis=0), jnp.sum(grad_normal * center, axis=0)])
    sums = butterfly_sum(own_sums, "dp")
    block_out = send_home(result)
    if local:
        sums, block_out = lax.optimization_barrier((sums, block_out))
        block_out = finish_hops(*block_out)
    sum_plain, sum_center = sums
    bn_scale = bn_gain * inv_std
    grad_depth = bn_scale * grad_normal - frame_mask * bn_scale * (
        sum_plain + inv_std * inv_std * sum_center * center
    ) / total_count
    grad_glu = jnp.zeros_like(glu)
    tap_grads = []
    for t in range(taps):
        grad_glu = grad_glu + convs[t] * shift_rows(grad_depth, margin - t)
        tap_grads.append(jnp.sum(grad_depth * shift_rows(glu, t - margin), axis=0))
    grad_glu = grad_glu * frame_mask
    grad_linear = (grad_glu * gate_sig).astype(bf16)
    grad_gating = (grad_glu * linear * gate_sig * (1.0 - gate_sig)).astype(bf16)
    if not local:
        grad_pv = weight_grad(grad_linear, conv_in)
        grad_pg = weight_grad(grad_gating, conv_in)
    back, gain_two, bias_two = norm_backward(
        stream_two,
        stats_conv,
        gains[2],
        dot_plain(grad_linear, p_value) + dot_plain(grad_gating, p_gate),
    )
    grad_two = grad_three + back

    incoming = grad_two.astype(bf16)
    grad_wo = None if local else weight_grad(merged, incoming)
    grad_merged = dot_rows(incoming, w_output).astype(bf16)
    if local:
        grad_merged, gin_second, gout_second = lax.optimization_barrier(
            (grad_merged, gin_second, gout_second)
        )
    grad_q, grad_k, grad_v = head_call(
        attend_back_kernel, valid, (queries, keys, values, grad_merged), 3, 10
    )
    if local:
        singles_other, singles_own = single_grads(
            ((0, 0), (1, 0), (2, 0), (3, 1), (4, 2), (5, 2), (6, 3)),
            (grad_q, grad_k, grad_v, merged, grad_linear, grad_gating, conv_act),
            (att_in, incoming, conv_in, incoming_three),
        )
    else:
        grad_wq = weight_grad(grad_q, att_in)
        grad_wk = weight_grad(grad_k, att_in)
        grad_wv = weight_grad(grad_v, att_in)
    back, gain_one, bias_one = norm_backward(
        stream_one,
        stats_att,
        gains[1],
        dot_plain(grad_q, w_query) + dot_plain(grad_k, w_key) + dot_plain(grad_v, w_value),
    )
    grad_one = grad_two + back
    if local:
        grad_one, singles_other = lax.optimization_barrier((grad_one, singles_other))
        singles_other = swap(singles_other, "core")

    if local:
        grad_zero, gin_first, gout_first, gain_zero, bias_zero = ffn_backward_here(
            grad_one,
            (0.5 * grad_one).astype(bf16),
            source,
            gains[0],
            kept_one,
            (0, quarter),
            quarter,
            place,
            sources,
            ((1,), (0,)),
        )
    else:
        grad_zero, gin_first, gout_first, gain_zero, bias_zero = ffn_backward(
            grad_one, source, gains[0], kept_one, in_first, out_first
        )
    block_grad = send_home(grad_zero)

    conv_small = jnp.stack(tap_grads + [own_sums[1] * inv_std, own_sums[0]])
    conv_small = conv_small.reshape(-1, chan_count, rows_tile)[:, position].reshape(-1, width)
    small = jnp.concatenate(
        [
            jnp.stack(
                [gain_zero, gain_one, gain_two, gain_three, gain_four]
                + [bias_zero, bias_one, bias_two, bias_three, bias_four]
            ),
            conv_small,
        ]
    )
    if local:
        small = small + swap(small, "core")
        groups = [(i * quarter, quarter, False) for i in range(4)]
        groups.append((base, tile_count - base, True))
        pairs = [
            tuple(v.reshape(4, quarter, -1, width) for v in pair)
            for pair in (gin_first, gout_first, gin_second, gout_second)
        ]
        shape = (tile_count - base, 4) + pairs[0][0].shape[2:]
        pairs.append((singles_own.reshape(shape), singles_other.reshape(shape)))
        keep, got, small, block_grad = reduce_tiles_here(
            groups, [p[0] for p in pairs], [p[1] for p in pairs], place, slots, small, block_grad
        )
        block_grad = finish_hops(*block_grad)
        tile_m, tile_v, tile_w, tile_b = update_tiles_here(
            keep,
            got,
            owned_mask(tile_slot, slots).astype(jnp.int32),
            master,
            tile_first,
            tile_second,
        )
    else:
        grads = [gin_first, gout_first, gin_second, gout_second]
        grads += [grad_wq, grad_wk, grad_wv, grad_wo, grad_pv, grad_pg, grad_po]
        owned = reduce_tiles(
            jnp.concatenate(grads).reshape(tile_count, width, width), tile_slot, slots
        )
        small = butterfly_sum(butterfly_sum(small, "dp"), "chan")
        owned = jnp.where(owned_mask(tile_slot, slots)[:, None, None], owned, 0.0)
        tile_m, tile_v, tile_w = adamw_step(
            master, owned, tile_first, tile_second, tile_rate, weight_decay
        )
        tile_b = tile_w.astype(bf16)
    norm_total = small[: norm_params.shape[0]]
    conv_grad = lax.dynamic_slice_in_dim(
        small[norm_params.shape[0] :], chan_index * rows_tile, rows_tile, 1
    )

    norm_m, norm_v, norm_w = adamw_step(
        norm_params, norm_total, norm_first, norm_second, small_rate, 0.0
    )
    conv_m, conv_v, conv_w = adamw_step(
        conv_params, conv_grad, conv_first, conv_second, small_rate, 0.0
    )
    return (
        block_out[:, None],
        block_grad[:, None].astype(f32),
        tile_m,
        tile_v,
        tile_w,
        tile_b,
        norm_m,
        norm_v,
        norm_w,
        conv_m,
        conv_v,
        conv_w,
    )


def solution(mesh):
    in_specs = (
        P(None, "dp", "chan", None),
        P(None, "dp", "chan", None),
        P(None, "dp"),
        P(),
        P("dp", "chan", None),
        P("dp", "chan", None),
        P("dp", "chan", None),
        P(),
        P(),
        P(),
        P(None, "chan"),
        P(None, "chan"),
        P(None, "chan"),
    )
    out_specs = (
        P(None, "dp", "chan", None),
        P(None, "dp", "chan", None),
        P("dp", "chan", None),
        P("dp", "chan", None),
        P("dp", "chan", None),
        P("dp", "chan", None),
        P(),
        P(),
        P(),
        P(None, "chan"),
        P(None, "chan"),
        P(None, "chan"),
    )
    return jax.shard_map(shards, mesh=mesh, in_specs=in_specs, out_specs=out_specs, check_vma=False)
```
